32 devices in a mesh: dp: 8 (over y, x, core), mp: 4 (over z).
Axes of the slice: x: 2, y: 2, z: 4, core: 2. Of those that a mesh axis runs over, the one named last changes fastest.
Arguments:
- sequence: bfloat16 [128, 532, 512], P(('dp', 'mp')), may hold values from -6 to 6
- cotangent: bfloat16 [128, 532, 512], P(('dp', 'mp')), may hold values from -6 to 6
- w_query: bfloat16 [512, 512], replicated, may hold values from -0.25 to 0.25
- b_query: bfloat16 [512], replicated, may hold values from -2.5 to 2.5
- w_key: bfloat16 [512, 512], replicated, may hold values from -0.25 to 0.25
- w_value: bfloat16 [512, 512], replicated, may hold values from -0.25 to 0.25
- b_value: bfloat16 [512], replicated, may hold values from -2.5 to 2.5
- w_out: bfloat16 [512, 512], replicated, may hold values from -1.5 to 1.5
- b_out: bfloat16 [512], replicated, may hold values from -2.5 to 2.5
- gain_attn: bfloat16 [512], replicated, may hold values from 0.5 to 1.5
- shift_attn: bfloat16 [512], replicated, may hold values from -2.5 to 2.5
- w_in: bfloat16 [512, 2048], P(None, 'mp'), may hold values from -0.25 to 0.25
- b_in: bfloat16 [2048], P('mp'), may hold values from -2.5 to 2.5
- w_back: bfloat16 [2048, 512], P('mp'), may hold values from -0.125 to 0.125
- b_back: bfloat16 [512], replicated, may hold values from -2.5 to 2.5
- gain_ffn: bfloat16 [512], replicated, may hold values from 0.5 to 1.5
- shift_ffn: bfloat16 [512], replicated, may hold values from -2.5 to 2.5
Outputs:
- layer_out: bfloat16 [128, 532, 512], P(('dp', 'mp'))
- input_grad: float32 [128, 532, 512], P(('dp', 'mp'))
- grad_w_query: float32 [512, 512], P('mp')
- grad_b_query: float32 [512], P('mp')
- grad_w_key: float32 [512, 512], P('mp')
- grad_w_value: float32 [512, 512], P('mp')
- grad_b_value: float32 [512], P('mp')
- grad_w_out: float32 [512, 512], P('mp')
- grad_b_out: float32 [512], P('mp')
- grad_gain_attn: float32 [512], P('mp')
- grad_shift_attn: float32 [512], P('mp')
- grad_w_in: float32 [512, 2048], P(None, 'mp')
- grad_b_in: float32 [2048], P('mp')
- grad_w_back: float32 [2048, 512], P('mp')
- grad_b_back: float32 [512], P('mp')
- grad_gain_ffn: float32 [512], P('mp')
- grad_shift_ffn: float32 [512], P('mp')
The draws below stay inside these ranges and needn't reach their ends.
All inputs are finite; a program needn't handle non-finite values.
Results may differ from the reference program's by a relative error of at most 0.019.
Values may be sent and summed in bfloat16 or wider, within the bound.
No kernel may reach another device: no remote copies, remote signals or barrier semaphores. Data moves between devices by JAX's collectives and lax.ppermute only.
A program may use at most 192 MiB of HBM per device.

```python
import math
import jax
import jax.numpy as jnp
from jax import lax

D = 512
HEADS = 8
FF = 2048
ROWS = 532
SPANS = 128


def spiked(entries, own_key, source, target, shards_of, factor):
    def block_of(axis_at):
        return (jnp.arange(entries.shape[axis_at]) // (entries.shape[axis_at] // shards_of)).reshape((-1,) + (1,) * (entries.ndim - 1 - axis_at))

    near = jax.random.permutation(own_key, shards_of)[block_of(target)]
    other_side = (block_of(target) + shards_of // 2) % shards_of
    return jnp.where((block_of(source) == near) | (block_of(source) == other_side), factor * entries, entries)


def shard_levels(key, extent, shards, smallest, largest):
    factor_of, own = 1.0, jax.random.fold_in(key, 6)
    for position, shards_of in shards:
        heights = jnp.exp(jax.random.uniform(jax.random.fold_in(own, position), (shards_of,), jnp.float32, smallest / len(shards), largest / len(shards)))
        factor_of = factor_of * jnp.repeat(heights, extent[position] // shards_of).reshape([-1 if axis == position else 1 for axis in range(len(extent))])
    return factor_of


def centred(key, extent, deviation, bound, pieces=(), dtype=jnp.bfloat16):
    level = shard_levels(key, extent, pieces, -0.22, 0.18) if pieces else 1.0
    entries = jax.random.normal(key, extent, jnp.float32) * deviation * level
    return jnp.minimum(jnp.maximum(entries, -bound), bound).astype(dtype)


def heavy_noise(key, dims, deviation, limit, pieces, heavy, dtype=jnp.bfloat16):
    drawn = deviation * jax.random.normal(key, dims, jnp.float32)
    if pieces:
        drawn = drawn * shard_levels(key, dims, pieces, -0.22, 0.18)
    return jnp.clip(spiked(drawn, jax.random.fold_in(key, 3), *heavy), -limit, limit).astype(dtype)


def setup_inputs(seed: int = 0) -> dict:
    arg_keys = jax.random.split(jax.random.key(seed), 18)
    sequence = centred(arg_keys[0], (SPANS, ROWS, D), 1.0, 6.0, ((0, 32),))
    cotangent = heavy_noise(arg_keys[1], (SPANS, ROWS, D), 1.0, 6.0, ((0, 32),), (0, 2, 32, 2.75))
    w_query = centred(arg_keys[2], (D, D), D ** -0.5, 0.25)
    b_query = centred(arg_keys[3], (D,), 0.3, 2.5)
    w_key = centred(arg_keys[4], (D, D), D ** -0.5, 0.25)
    w_value = centred(arg_keys[5], (D, D), D ** -0.5, 0.25)
    b_value = centred(arg_keys[6], (D,), 0.3, 2.5)
    w_out = centred(arg_keys[7], (D, D), (D // 32) ** -0.5, 1.5)
    b_out = centred(arg_keys[8], (D,), 0.3, 2.5)
    gain_attn = jnp.clip(1.0 + 0.1 * jax.random.normal(arg_keys[9], (D,), jnp.float32), 0.5, 1.5).astype(jnp.bfloat16)
    shift_attn = centred(arg_keys[10], (D,), 0.3, 2.5)
    w_in = centred(arg_keys[11], (D, FF), D ** -0.5, 0.25, ((1, 4),))
    b_in = centred(arg_keys[12], (FF,), 0.3, 2.5, ((0, 4),))
    w_back = centred(arg_keys[13], (FF, D), FF ** -0.5, 0.125, ((0, 4),))
    b_back = centred(arg_keys[14], (D,), 0.3, 2.5)
    gain_ffn = jnp.clip(1.0 + 0.1 * jax.random.normal(arg_keys[15], (D,), jnp.float32), 0.5, 1.5).astype(jnp.bfloat16)
    shift_ffn = centred(arg_keys[16], (D,), 0.3, 2.5)
    return dict(sequence=sequence, cotangent=cotangent, w_query=w_query, b_query=b_query, w_key=w_key, w_value=w_value, b_value=b_value, w_out=w_out, b_out=b_out, gain_attn=gain_attn, shift_attn=shift_attn, w_in=w_in, b_in=b_in, w_back=w_back, b_back=b_back, gain_ffn=gain_ffn, shift_ffn=shift_ffn)


@jax.custom_vjp
def low(v):
    return lax.optimization_barrier(v.astype(jnp.bfloat16)).astype(jnp.float32)

@jax.custom_vjp
def low_back(v):
    return v

def low_keep(v):
    return (low(v), None)

def low_pass(kept, grad):
    return (grad,)

def back_keep(v):
    return (v, None)

def back_low(kept, grad):
    return (low(grad),)
low.defvjp(low_keep, low_pass)
low_back.defvjp(back_keep, back_low)
HIGHEST = lax.Precision.HIGHEST

def project(inputs, matrix):
    return jnp.einsum('grd,de->gre', inputs, matrix, precision=HIGHEST)

def normalize(summed_rows, gain, shift):
    centre = summed_rows - lax.optimization_barrier(jnp.mean(summed_rows, -1, keepdims=True))
    inverse = lax.rsqrt(lax.optimization_barrier(jnp.mean(centre * centre, -1, keepdims=True)) + 1e-05)
    return centre * inverse * gain + shift

def layer(inputs, w_query, b_query, w_key, w_value, b_value, w_out, b_out, gain_attn, shift_attn, w_in, b_in, w_back, b_back, gain_ffn, shift_ffn):
    group_size, row_count, model_width = inputs.shape
    head_size = model_width // HEADS
    shape = (group_size, row_count, HEADS, head_size)
    queries = low_back(low(project(inputs, w_query) + b_query)).reshape(shape)
    key_rows = low_back(low(project(inputs, w_key))).reshape(shape)
    value_rows = low_back(low(project(inputs, w_value) + b_value)).reshape(shape)
    scores = low_back(jnp.einsum('grhd,gshd->ghrs', queries, key_rows, precision=HIGHEST) * head_size ** (-0.5))
    weights = low(jax.nn.softmax(scores, axis=-1))
    mixed = jnp.einsum('ghrs,gshd->grhd', weights, value_rows, precision=HIGHEST)
    mixed = low_back(low(mixed.reshape(group_size, row_count, model_width)))
    attn = low_back(project(mixed, w_out) + b_out)
    normed = normalize(inputs + attn, gain_attn, shift_attn)
    hidden_pre = low_back(project(low(normed), w_in) + b_in)
    hidden_act = low(jax.nn.gelu(hidden_pre, approximate=True))
    ffn = low_back(project(hidden_act, w_back) + b_back)
    return normalize(normed + ffn, gain_ffn, shift_ffn)

def reference(sequence, cotangent, w_query, b_query, w_key, w_value, b_value, w_out, b_out, gain_attn, shift_attn, w_in, b_in, w_back, b_back, gain_ffn, shift_ffn):
    params = tuple((p.astype(jnp.float32) for p in (w_query, b_query, w_key, w_value, b_value, w_out, b_out, gain_attn, shift_attn, w_in, b_in, w_back, b_back, gain_ffn, shift_ffn)))
    span_count, row_count, model_width = sequence.shape
    group_size = math.gcd(span_count, 8)
    shape = (span_count // group_size, group_size, row_count, model_width)
    inputs_all = sequence.astype(jnp.float32).reshape(shape)
    grads_all = cotangent.astype(jnp.float32).reshape(shape)

    def scan_step(totals, inputs_pair):
        inputs_group, grads_group = inputs_pair
        outputs, pullback = jax.vjp(layer, inputs_group, *params)
        pulled = pullback(grads_group)
        totals = tuple((total + grad for total, grad in zip(totals, pulled[1:])))
        return (totals, (outputs.astype(jnp.bfloat16), pulled[0]))
    zeros = tuple((jnp.zeros_like(p) for p in params))
    totals, (outputs, input_grads) = lax.scan(scan_step, zeros, (inputs_all, grads_all))
    full = (span_count, row_count, model_width)
    return (outputs.reshape(full), input_grads.reshape(full), totals[0], totals[1], totals[2], totals[3], totals[4], totals[5], totals[6], totals[7], totals[8], totals[9], totals[10], totals[11], totals[12], totals[13], totals[14])
```

```python
import functools

import jax
import jax.numpy as jnp
from jax import lax
from jax.experimental import pallas as pl
from jax.experimental.pallas import tpu as pltpu
from jax.sharding import PartitionSpec as P

HEADS = 8
GROUPS = 2
INNER = 8
NEG = -1e30
C0 = (2.0 / 3.141592653589793) ** 0.5
C1 = C0 * 0.044715
f32 = jnp.float32
bf16 = jnp.bfloat16


def dot(left, right, a, b):
    return lax.dot_general(left, right, (((a,), (b,)), ((), ())), preferred_element_type=f32)


def nn(left, right):
    return dot(left, right, 1, 0)


def nt(left, right):
    return dot(left, right, 1, 1)


def tn(left, right):
    return dot(left, right, 0, 0)


def fold(v):
    return jnp.sum(v.reshape(v.shape[0] // 8, 8, v.shape[1]), 0)


def row_mean(v):
    return jnp.mean(v, -1, keepdims=True)


def params(mib=60):
    return pltpu.CompilerParams(vmem_limit_bytes=mib * 2**20)


def whole(a):
    return pl.BlockSpec(a.shape, lambda *_: (0,) * len(a.shape), pipeline_mode=pl.Buffered(1))


def shape(dims, dtype):
    return jax.ShapeDtypeStruct(tuple(dims), dtype)


def attend_body(rows, pad, x_ref, wq_ref, wk_ref, wv_ref, wo_ref, vec_ref,
                qt_ref, k_ref, vt_ref, mt_ref, lt_ref, so_ref, xp, wqt, wvt, cols):
    width = x_ref.shape[-1]
    hs = width // HEADS
    main = rows // 128 * 128
    left = pad - main
    group = 128 // left
    top = rows // 16 * 16

    @pl.when(pl.program_id(0) == 0)
    def _():
        wqt[...] = wq_ref[...].T
        wvt[...] = wv_ref[...].T
        xp[top:, :] = jnp.zeros((pad - top, width), bf16)
        cols[...] = vec_ref[0:8, :].T

    xp[:rows, :] = x_ref[0]
    x = xp[...]
    scale = hs**-0.5
    qt_ref[0] = (nt(wqt[...], x) + cols[:, 0:1]).astype(bf16) * bf16(scale)
    k_ref[0] = nn(x, wk_ref[...]).astype(bf16)
    vt_ref[0] = (nt(wvt[...], x) + cols[:, 1:2]).astype(bf16)
    valid = lax.broadcasted_iota(jnp.int32, (pad - top, 1), 0) < rows - top
    ones = jnp.ones((16, pad), bf16)

    def soft(st):
        s_top = st[:top]
        s_bot = jnp.where(valid, st[top:], NEG)
        m = jnp.maximum(jnp.max(s_top, 0, keepdims=True), jnp.max(s_bot, 0, keepdims=True))
        p = jnp.concatenate([jnp.exp(s_top - m).astype(bf16), jnp.exp(s_bot - m).astype(bf16)], 0)
        return m, p

    for h in range(HEADS):
        c = slice(hs * h, hs * h + hs)
        m, p = soft(nn(k_ref[0, :, c], qt_ref[0, c, :main]))
        ot = nn(jnp.concatenate([vt_ref[0, c, :], ones], 0), p)
        total = ot[hs : hs + 1]
        mt_ref[0, c, :main] = (ot[:hs] * (1.0 / total)).astype(bf16)
        lt_ref[0, h // (HEADS // GROUPS), h % (HEADS // GROUPS) : h % (HEADS // GROUPS) + 1, :main] = m + jnp.log(total)
    for g in range(HEADS // group):
        w = hs * group
        c = slice(w * g, w * g + w)
        same = (lax.broadcasted_iota(jnp.int32, (w, 128), 0) // hs
                == lax.broadcasted_iota(jnp.int32, (w, 128), 1) // left)
        ql = jnp.where(same, jnp.concatenate([qt_ref[0, c, main:pad]] * group, 1), 0).astype(bf16)
        m, p = soft(nn(k_ref[0, :, c], ql))
        ot = nn(jnp.concatenate([vt_ref[0, c, :], ones], 0), p)
        total = ot[w : w + 1]
        o = ot[:w] * (1.0 / total)
        lt = m + jnp.log(total)
        for j in range(group):
            h = g * group + j
            mt_ref[0, hs * h : hs * h + hs, main:pad] = o[hs * j : hs * j + hs, left * j : left * j + left].astype(bf16)
            lt_ref[0, h // (HEADS // GROUPS), h % (HEADS // GROUPS) : h % (HEADS // GROUPS) + 1, main:pad] = lt[:, left * j : left * j + left]
    so_ref[0] = tn(mt_ref[0], wo_ref[...]) + vec_ref[2:3, :] + xp[...].astype(f32)


def attend(sequence, wq, wk, wv, wo, vec):
    spans, rows, width = sequence.shape
    pad = (rows + 31) // 32 * 32
    per = HEADS // GROUPS
    spec = lambda a, b: pl.BlockSpec((1, a, b), lambda i: (i, 0, 0))
    return pl.pallas_call(
        functools.partial(attend_body, rows, pad),
        grid=(spans,),
        in_specs=[spec(rows, width)] + [whole(w) for w in (wq, wk, wv, wo, vec)],
        out_specs=[spec(width, pad), spec(pad, width), spec(width, pad), spec(width, pad),
                   pl.BlockSpec((1, GROUPS, per, pad), lambda i: (i, 0, 0, 0)), spec(pad, width)],
        out_shape=[shape((spans, width, pad), bf16), shape((spans, pad, width), bf16), shape((spans, width, pad), bf16),
                   shape((spans, width, pad), bf16), shape((spans, GROUPS, per, pad), f32), shape((spans, pad, width), f32)],
        scratch_shapes=[pltpu.VMEM((pad, width), bf16), pltpu.VMEM((width, width), bf16), pltpu.VMEM((width, width), bf16),
                        pltpu.VMEM((width, 8), f32)],
        compiler_params=params(),
        name="attend",
    )(sequence, wq, wk, wv, wo, vec)


def ffn_body(rows, own, slices, so_ref, ct_ref, wi_ref, wb_ref, *refs):
    wi_refs, wb_refs = refs[:slices], refs[slices : 2 * slices]
    (b_ref, vec_ref, wo_ref, lo_ref, h_ref, g_ref, f_ref, nl_ref, gs_ref, ga_ref, dot_ref, col_ref, bin_ref,
     gp, col, binv, wit, wbs) = refs[2 * slices :]
    pad, width = so_ref.shape[1:]
    hidden = wit.shape[0]
    step = pl.program_id(0)

    @pl.when(step == 0)
    def _():
        col[...] = jnp.zeros_like(col)
        binv[...] = jnp.zeros_like(binv)
        wit[:own, :] = wi_ref[...].T
        wbs[:own, :] = wb_ref[...]
        at = own
        for a, b in zip(wi_refs, wb_refs):
            for s in range(a.shape[0]):
                n = a.shape[1]
                wit[at : at + n, :] = a[s]
                wbs[at : at + n, :] = b[s]
                at += n

    bb, g1, s1, g2, s2 = (vec_ref[n : n + 1, :] for n in range(3, 8))
    r = so_ref[0]
    c = r - row_mean(r)
    inv1 = lax.rsqrt(row_mean(c * c) + 1e-5)
    unit1 = c * inv1
    normed = unit1 * g1 + s1
    nl = normed.astype(bf16)
    nl_ref[0] = nl
    acc = normed + bb
    unit = 512
    for j in range(hidden // unit):
        cs = slice(unit * j, unit * j + unit)
        pre = nt(nl, wit[cs, :]) + b_ref[:, cs]
        sq = pre * pre
        t = jnp.tanh(pre * (C0 + C1 * sq))
        half = 0.5 + 0.5 * t
        act = (pre * half).astype(bf16)
        gp[:, cs] = half + pre * (0.5 * C0 + 1.5 * C1 * sq) * (1.0 - t * t)
        h_ref[0, :, cs] = act
        acc = acc + nn(act, wbs[cs, :])
    c = acc - row_mean(acc)
    inv2 = lax.rsqrt(row_mean(c * c) + 1e-5)
    unit2 = c * inv2
    lo_ref[0] = (unit2 * g2 + s2)[:rows].astype(bf16)
    up = jnp.concatenate([ct_ref[0].astype(f32), jnp.zeros((pad - rows, width), f32)], 0)
    gu = up * g2
    gs2 = inv2 * (gu - row_mean(gu) - unit2 * row_mean(gu * unit2))
    f = gs2.astype(bf16)
    f_ref[0] = f
    col[0] += fold(up * unit2)
    col[1] += fold(up)
    col[2] += fold(gs2)
    dn = gs2
    for j in range(hidden // unit):
        cs = slice(unit * j, unit * j + unit)
        g = nt(f, wbs[cs, :]) * gp[:, cs]
        binv[:, cs] += fold(g)
        g = g.astype(bf16)
        g_ref[0, :, cs] = g
        dn = dn + nn(g, wit[cs, :])
    gu = dn * g1
    gs1 = inv1 * (gu - row_mean(gu) - unit1 * row_mean(gu * unit1))
    gs_ref[0] = gs1
    ga = gs1.astype(bf16)
    ga_ref[0] = ga
    dot_ref[0] = nt(wo_ref[...], ga).astype(bf16)
    col[3] += fold(dn * unit1)
    col[4] += fold(dn)
    col[5] += fold(gs1)

    @pl.when(step == pl.num_programs(0) - 1)
    def _():
        col_ref[...] = jnp.sum(col[...], 1)
        bin_ref[...] = jnp.sum(binv[...], 0, keepdims=True)


def ffn(so, cotangent, wi, wb, wis, wbs, bias, vec, wo):
    spans, pad, width = so.shape
    rows = cotangent.shape[1]
    own = wi.shape[1]
    hidden = bias.shape[1]
    ws = (wi, wb, *wis, *wbs, bias, vec, wo)
    spec = lambda a, b: pl.BlockSpec((1, a, b), lambda i: (i, 0, 0))
    one = lambda a, b: pl.BlockSpec((a, b), lambda i: (0, 0))
    st = lambda a, b, t: shape((spans, a, b), t)
    return pl.pallas_call(
        functools.partial(ffn_body, rows, own, len(wis)),
        grid=(spans,),
        in_specs=[spec(pad, width), spec(rows, width)] + [whole(w) for w in ws],
        out_specs=[spec(rows, width), spec(pad, hidden), spec(pad, hidden), spec(pad, width), spec(pad, width),
                   spec(pad, width), spec(pad, width), spec(width, pad), one(8, width), one(1, hidden)],
        out_shape=[st(rows, width, bf16), st(pad, hidden, bf16), st(pad, hidden, bf16), st(pad, width, bf16), st(pad, width, bf16),
                   st(pad, width, f32), st(pad, width, bf16), st(width, pad, bf16), shape((8, width), f32), shape((1, hidden), f32)],
        scratch_shapes=[pltpu.VMEM((pad, hidden), f32), pltpu.VMEM((8, 8, width), f32), pltpu.VMEM((8, hidden), f32),
                        pltpu.VMEM((hidden, width), bf16), pltpu.VMEM((hidden, width), bf16)],
        compiler_params=params(62),
        name="ffn",
    )(so, cotangent, *ws)


def weight_body(own, planes, at_ref, a_ref, b_ref, o0_ref, o1_ref):
    step = pl.program_id(0)
    rows = o0_ref.shape[2]
    block = a_ref.shape[1]
    piece = tn(a_ref[...], b_ref[...]).astype(bf16)
    first = own // block
    for n in range(block // rows):
        part = piece[n * rows : n * rows + rows]
        mine = step * (block // rows) + n
        far = (step - first) * (block // rows) + n
        near = at_ref[0] ^ mine
        is_own = step < first
        q = far // (planes - 1)
        half = jnp.where(is_own, near & 1, q // (INNER // 2))
        peer = jnp.where(is_own, near >> 1, q % (INNER // 2))
        shift = jnp.where(is_own, 0, far % (planes - 1) + 1)

        @pl.when(half == 0)
        def _():
            o0_ref[peer, shift] = part

        @pl.when(half != 0)
        def _():
            o1_ref[peer, shift] = part


def weight(at, a, b, own, planes, name):
    rows, hidden = a.shape
    width = b.shape[1]
    block = 256
    half = (INNER // 2, planes, own // INNER, width)
    out = pl.BlockSpec(half, lambda i, *_: (0, 0, 0, 0))
    return pl.pallas_call(
        functools.partial(weight_body, own, planes),
        grid_spec=pltpu.PrefetchScalarGridSpec(
            num_scalar_prefetch=1,
            grid=(hidden // block,),
            in_specs=[pl.BlockSpec((rows, block), lambda i, *_: (0, i)), whole(b)],
            out_specs=[out, out],
        ),
        out_shape=[shape(half, bf16)] * 2,
        compiler_params=params(),
        name=name,
    )(at, a, b)


def vector_rows(vec, at_ref, peer, plane, planes, count):
    n = vec.shape[1] // planes
    rows = vec[:, pl.ds(pl.multiple_of(plane * n, n), n)]
    slot = lax.broadcasted_iota(jnp.int32, rows.shape, 0) == (at_ref[0] ^ peer)
    row = jnp.sum(jnp.where(slot, rows, 0.0), 0, keepdims=True)
    return jnp.concatenate([row, jnp.zeros((count - 1, n), f32)], 0)


def out_body(planes, at_ref, mt_ref, ga_ref, col_ref, bin_ref, o0_ref, o1_ref, acc):
    step = pl.program_id(0)

    @pl.when(step == 0)
    def _():
        acc[...] = jnp.zeros_like(acc)

    acc[...] += nn(mt_ref[0], ga_ref[0])

    @pl.when(step == pl.num_programs(0) - 1)
    def _():
        width = acc.shape[0]
        rows = width // (planes * INNER)
        n = width // planes
        for half, o_ref in enumerate((o0_ref, o1_ref)):
            for hi in range(INNER // 2):
                for s in range(planes):
                    peer = half + 2 * hi
                    plane = lax.rem(at_ref[1] + planes - s, planes)
                    start = plane * n + (at_ref[0] ^ peer) * rows
                    o_ref[hi, s, :rows, :] = acc[pl.ds(pl.multiple_of(start, rows), rows), :].astype(bf16)
                    o_ref[hi, s, rows:, :] = jnp.zeros((16, width), bf16)
                    o_ref[hi, s, rows:, :n] = vector_rows(col_ref, at_ref, peer, plane, planes, 16).astype(bf16)
                    at = (half * (INNER // 2) + hi) * planes + s
                    m = bin_ref.shape[1]
                    b = jnp.concatenate([bin_ref[at : at + 1, :], jnp.zeros((15, m), f32)], 0)
                    o_ref[hi, s, rows:, n : n + m] = b.astype(bf16)


def out_weight(at, mt, ga, col, bins, planes):
    spans, width, pad = mt.shape
    half = (INNER // 2, planes, width // (planes * INNER) + 16, width)
    out = pl.BlockSpec(half, lambda i, *_: (0, 0, 0, 0))
    return pl.pallas_call(
        functools.partial(out_body, planes),
        grid_spec=pltpu.PrefetchScalarGridSpec(
            num_scalar_prefetch=1,
            grid=(spans,),
            in_specs=[pl.BlockSpec((1, width, pad), lambda i, *_: (i, 0, 0)), pl.BlockSpec((1, pad, width), lambda i, *_: (i, 0, 0)),
                      whole(col), whole(bins)],
            out_specs=[out, out],
            scratch_shapes=[pltpu.VMEM((width, width), f32)],
        ),
        out_shape=[shape(half, bf16)] * 2,
        compiler_params=params(),
        name="w_out",
    )(at, mt, ga, col, bins)


def back_body(rows, planes, group, at_ref, x_ref, qt_ref, k_ref, vt_ref, mt_ref, dt_ref, lt_ref,
              dq_ref, dk_ref, dv_ref, o0_ref, o1_ref, aq, ak, av, ab, xp, vec, turn):
    w, pad = qt_ref.shape[1:]
    width = x_ref.shape[-1]
    hs = width // HEADS
    scale = hs**-0.5
    main = rows // 128 * 128
    left = pad - main
    heads = w // hs
    top = rows // 16 * 16
    step = pl.program_id(0)

    @pl.when(step == 0)
    def _():
        aq[...] = jnp.zeros_like(aq)
        ak[...] = jnp.zeros_like(ak)
        av[...] = jnp.zeros_like(av)
        ab[...] = jnp.zeros_like(ab)
        xp[top:, :] = jnp.zeros((pad - top, width), bf16)

    xp[:rows, :] = x_ref[0]
    k = k_ref[0]
    kt = k.T
    v = vt_ref[0].T
    valid = lax.broadcasted_iota(jnp.int32, (pad - top, 1), 0) < rows - top

    def core(ks, qs, vs, ds, ls, ms):
        delta = jnp.sum(ds.astype(f32) * ms.astype(f32), 0, keepdims=True)
        st = nn(ks, qs)
        st = jnp.concatenate([st[:top], jnp.where(valid, st[top:], NEG)], 0)
        p = jnp.exp(st - ls)
        gsc = (p * (nn(vs, ds) - delta)).astype(bf16)
        return p.astype(bf16), gsc

    same = (lax.broadcasted_iota(jnp.int32, (w, 128), 0) // hs
            == lax.broadcasted_iota(jnp.int32, (w, 128), 1) // left)
    tile = lambda a: jnp.where(same, jnp.concatenate([a] * heads, 1), 0).astype(bf16)
    ql, dl, ml = (tile(ref[0, :, main:pad]) for ref in (qt_ref, dt_ref, mt_ref))
    ll = jnp.concatenate([lt_ref[0, 0, h : h + 1, main:pad] for h in range(heads)], 1)
    p, gsc = core(k, ql, v, dl, ll, ml)
    dv_left = nt(dl, p)
    dk_left = nt(ql, gsc)
    dq_left = nn(kt, gsc)
    for h in range(heads):
        c = slice(hs * h, hs * h + hs)
        q, d = qt_ref[0, c, :main], dt_ref[0, c, :main]
        p, gsc = core(k[:, c], q, v[:, c], d, lt_ref[0, 0, h : h + 1, :main], mt_ref[0, c, :main])
        dv_ref[0, c, :] = (nt(d, p) + dv_left[c]).astype(bf16)
        dk_ref[0, c, :] = (nt(q, gsc) + dk_left[c]).astype(bf16)
        dq_ref[0, c, :main] = (nn(kt[c], gsc) * scale).astype(bf16)
        dq_ref[0, c, main:pad] = (dq_left[c, left * h : left * h + left] * scale).astype(bf16)
    x = xp[...]
    aq[...] += nn(dq_ref[0], x)
    ak[...] += nn(dk_ref[0], x)
    av[...] += nn(dv_ref[0], x)
    ab[:, 0:1] += jnp.sum(dq_ref[0].astype(f32), 1, keepdims=True)
    ab[:, 1:2] += jnp.sum(dv_ref[0].astype(f32), 1, keepdims=True)

    @pl.when(step == pl.num_programs(0) - 1)
    def _():
        size = width // (planes * INNER)
        n = width // planes
        vec[...] = jnp.zeros_like(vec)
        vec[:, group * w : group * w + w] = ab[...].T
        for i, a in enumerate((aq, ak, av)):
            turn[i] = a[...].T
        for half, o_ref in enumerate((o0_ref, o1_ref)):
            for hi in range(INNER // 2):
                for s in range(planes):
                    peer = half + 2 * hi
                    plane = lax.rem(at_ref[1] + planes - s, planes)
                    start = pl.multiple_of(plane * n + (at_ref[0] ^ peer) * size, size)
                    for i in range(3):
                        o_ref[hi, s, size * i : size * i + size, :] = turn[i, pl.ds(start, size), :].astype(bf16)
                    o_ref[hi, s, 3 * size :, :] = jnp.zeros((16, w), bf16)
                    o_ref[hi, s, 3 * size :, :n] = vector_rows(vec, at_ref, peer, plane, planes, 16).astype(bf16)


def back(at, sequence, qt, k, vt, mt, dt, lt, group, planes):
    spans, rows, width = sequence.shape
    pad = k.shape[1]
    w = width // GROUPS
    tr = pl.BlockSpec((1, w, pad), lambda i, *_: (i, group, 0))
    grad = pl.BlockSpec((1, w, pad), lambda i, *_: (i, 0, 0))
    half = (INNER // 2, planes, 3 * width // (planes * INNER) + 16, w)
    out = pl.BlockSpec(half, lambda i, *_: (0, 0, 0, 0))
    return pl.pallas_call(
        functools.partial(back_body, rows, planes, group),
        grid_spec=pltpu.PrefetchScalarGridSpec(
            num_scalar_prefetch=1,
            grid=(spans,),
            in_specs=[pl.BlockSpec((1, rows, width), lambda i, *_: (i, 0, 0)), tr,
                      pl.BlockSpec((1, pad, w), lambda i, *_: (i, 0, group)), tr, tr, tr,
                      pl.BlockSpec((1, 1, HEADS // GROUPS, pad), lambda i, *_: (i, group, 0, 0))],
            out_specs=[grad] * 3 + [out] * 2,
            scratch_shapes=[pltpu.VMEM((w, width), f32)] * 3
            + [pltpu.VMEM((w, 8), f32), pltpu.VMEM((pad, width), bf16), pltpu.VMEM((8, width), f32), pltpu.VMEM((3, width, w), f32)],
        ),
        out_shape=[shape((spans, w, pad), bf16)] * 3 + [shape(half, bf16)] * 2,
        compiler_params=params(),
        name=f"back{group}",
    )(at, sequence, qt, k, vt, mt, dt, lt)


def input_body(rows, groups, *refs):
    gs_ref = refs[0]
    parts = refs[1 : 1 + 3 * groups]
    ws = refs[1 + 3 * groups : 4 + 3 * groups]
    out_ref = refs[4 + 3 * groups]
    wt = refs[5 + 3 * groups :]

    @pl.when(pl.program_id(0) == 0)
    def _():
        for a, b in zip(wt, ws):
            a[...] = b[...].T

    total = gs_ref[0]
    for g in range(groups):
        for n in range(3):
            part = parts[3 * g + n]
            w = part.shape[1]
            total = total + tn(part[0], wt[n][w * g : w * g + w, :])
    out_ref[0] = total[:rows]


def input_grad(rows, gs, parts, wq, wk, wv):
    spans, pad, width = gs.shape
    flat = [a for part in parts for a in part]
    spec = lambda a: pl.BlockSpec((1,) + a.shape[1:], lambda i: (i, 0, 0))
    return pl.pallas_call(
        functools.partial(input_body, rows, len(parts)),
        grid=(spans,),
        in_specs=[spec(gs)] + [spec(a) for a in flat] + [whole(w) for w in (wq, wk, wv)],
        out_specs=pl.BlockSpec((1, rows, width), lambda i: (i, 0, 0)),
        out_shape=shape((spans, rows, width), f32),
        scratch_shapes=[pltpu.VMEM((width, width), bf16)] * 3,
        compiler_params=params(),
        name="input_grad",
    )(gs, *flat, wq, wk, wv)


def ffn_final_body(at_ref, *refs):
    back, rest = refs[:INNER], refs[INNER : 2 * INNER]
    inner = refs[2 * INNER : 3 * INNER]
    wb_ref, wi_ref, wo_ref, vec_ref, bin_ref, turn = refs[3 * INNER :]
    rows = back[0].shape[0]
    size = rest[0].shape[0] - 16
    n = vec_ref.shape[1]
    for q in range(INNER):
        peer = q // (INNER // 2) + 2 * (q % (INNER // 2))
        slot = at_ref[0] ^ peer
        wb_ref[pl.ds(pl.multiple_of(slot * rows, rows), rows), :] = back[q][...].astype(f32)
        turn[pl.ds(pl.multiple_of(slot * rows, rows), rows), :] = inner[q][...].astype(f32)
        wo_ref[pl.ds(pl.multiple_of(slot * size, size), size), :] = rest[q][:size, :].astype(f32)
        tail = rest[q][size:, :].astype(f32)
        vec_ref[pl.ds(slot, 1), :] = tail[0:1, :n]
        bin_ref[pl.ds(slot, 1), :] = tail[0:1, n : n + rows]
    wi_ref[...] = turn[...].T


def ffn_final(at, back, inner, rest, planes):
    rows, width = back[0].shape
    unit = rows * INNER
    ops = (*back, *rest, *inner)
    n = width // planes
    out = [(unit, width), (width, unit), (n, width), (8, n), (8, rows)]
    return pl.pallas_call(
        ffn_final_body,
        grid_spec=pltpu.PrefetchScalarGridSpec(
            num_scalar_prefetch=1,
            grid=(1,),
            in_specs=[whole(a) for a in ops],
            out_specs=[pl.BlockSpec(d, lambda *_: (0, 0)) for d in out],
            scratch_shapes=[pltpu.VMEM((unit, width), f32)],
        ),
        out_shape=[shape(d, f32) for d in out],
        compiler_params=params(),
        name="ffn_final",
    )(at, *ops)


def attend_final_body(at_ref, *refs):
    parts = [refs[INNER * g : INNER * g + INNER] for g in range(GROUPS)]
    wq_ref, wk_ref, wv_ref, vec_ref = refs[INNER * GROUPS :]
    w = parts[0][0].shape[1]
    size = (parts[0][0].shape[0] - 16) // 3
    n = vec_ref.shape[1]
    for q in range(INNER):
        peer = q // (INNER // 2) + 2 * (q % (INNER // 2))
        slot = at_ref[0] ^ peer
        tail = jnp.zeros((1, n), f32)
        for g, part in enumerate(parts):
            for i, o_ref in enumerate((wq_ref, wk_ref, wv_ref)):
                o_ref[pl.ds(pl.multiple_of(slot * size, size), size), w * g : w * g + w] = part[q][size * i : size * i + size, :].astype(f32)
            tail = tail + part[q][3 * size :, :n].astype(f32)[0:1]
        vec_ref[pl.ds(slot, 1), :] = tail


def attend_final(at, parts, width, planes):
    ops = [a for part in parts for a in part]
    n = width // planes
    out = [(n, width)] * 3 + [(8, n)]
    return pl.pallas_call(
        attend_final_body,
        grid_spec=pltpu.PrefetchScalarGridSpec(
            num_scalar_prefetch=1,
            grid=(1,),
            in_specs=[whole(a) for a in ops],
            out_specs=[pl.BlockSpec(d, lambda *_: (0, 0)) for d in out],
        ),
        out_shape=[shape(d, f32) for d in out],
        compiler_params=params(),
        name="attend_final",
    )(at, *ops)


def shards(dp, planes, sequence, cotangent, w_query, b_query, w_key, w_value, b_value, w_out, b_out, gain_attn, shift_attn,
           w_in, b_in, w_back, b_back, gain_ffn, shift_ffn):
    spans, rows, width = sequence.shape
    own = w_in.shape[1]
    cut = own // INNER
    d = lax.axis_index("dp") & (INNER - 1)
    m = lax.axis_index("mp")
    at = jnp.stack([d, m]).astype(jnp.int32)

    def swap(a, k):
        return lax.ppermute(a, "dp", [(i, i ^ k) for i in range(dp)])

    def turn(a, s):
        return lax.ppermute(a, "mp", [(i, (i + s) % planes) for i in range(planes)])

    def by_peer(a):
        a = a.reshape(a.shape[:-2] + (2, 2, 2, a.shape[-1]))
        for axis, bit in ((-4, 2), (-3, 1), (-2, 0)):
            a = jnp.where((d >> bit) & 1 == 1, jnp.flip(a, axis), a)
        return jnp.moveaxis(a, -2, -4)

    def spread(a):
        far = [a] + [swap(a, 2 * k) for k in range(1, INNER // 2)]
        return far + [swap(b, 1) for b in far]

    def gather(piece):
        return spread(jnp.stack([turn(piece, s) for s in range(1, planes)]))

    def reduce(keep, send):
        got = swap(send, 1)
        parts = [(keep[k].astype(f32) + got[k].astype(f32)).astype(bf16) for k in range(INNER // 2)]
        total = parts[0].astype(f32)
        for k in range(1, INNER // 2):
            total = total + swap(parts[k], 2 * k).astype(f32)
        step = INNER
        while step < dp:
            total = total.astype(bf16)
            total = total.astype(f32) + swap(total, step).astype(f32)
            step *= 2
        total = total.astype(bf16)
        mine = total[0].astype(f32)
        for s in range(1, planes):
            mine = mine + turn(total[s], -s).astype(f32)
        return spread(mine.astype(bf16))

    wis = gather(lax.dynamic_slice(w_in, (0, d * cut), (width, cut)).T)
    wbs = gather(lax.dynamic_slice(w_back, (d * cut, 0), (cut, width)))
    far = jnp.stack([turn(b_in, s) for s in range(1, planes)])
    far = by_peer(far.reshape(planes - 1, INNER, cut))
    far = jnp.moveaxis(far, 0, -2).reshape(-1)
    bias = jnp.concatenate([b_in, far]).astype(f32)[None]
    vec = jnp.stack([b_query, b_value, b_out, b_back, gain_attn, shift_attn, gain_ffn, shift_ffn]).astype(f32)

    qt, k, vt, mt, lt, so = attend(sequence, w_query, w_key, w_value, w_out, vec)
    layer_out, act, pre, gf, nl, gs, ga, dt, col, bins = ffn(so, cotangent, w_in, w_back, wis, wbs, bias, vec, w_out)
    flat = lambda a: a.reshape(-1, a.shape[-1])
    back_sum = reduce(*weight(at, flat(act), flat(gf), own, planes, "w_back"))
    in_sum = reduce(*weight(at, flat(pre), flat(nl), own, planes, "w_in"))
    near = by_peer(bins[0, :own].reshape(INNER, cut)).reshape(INNER, 1, cut)
    bins = jnp.concatenate([near, bins[0, own:].reshape(INNER, planes - 1, cut)], 1).reshape(INNER * planes, cut)
    rest_sum = reduce(*out_weight(at, mt, ga, col, bins, planes))
    grads, sums = [], []
    for g in range(GROUPS):
        *grad, keep, send = back(at, sequence, qt, k, vt, mt, dt, lt, g, planes)
        grads.append(grad)
        sums.append(reduce(keep, send))
    by_input = input_grad(rows, gs, grads, w_query, w_key, w_value)
    wb, wi, wo, col, bins = ffn_final(at, back_sum, in_sum, rest_sum, planes)
    wq, wk, wv, pair = attend_final(at, sums, width, planes)
    return (layer_out, by_input, wq, pair[0], wk, wv, pair[1], wo, col[5], col[3], col[4], wi, bins.reshape(-1), wb,
            col[2], col[0], col[1])


def solution(mesh):
    spans, vector = P(("dp", "mp"), None, None), P("mp")
    return jax.shard_map(
        functools.partial(shards, mesh.shape["dp"], mesh.shape["mp"]),
        mesh=mesh,
        in_specs=(spans, spans) + (P(),) * 9 + (P(None, "mp"), vector, P("mp", None)) + (P(),) * 3,
        out_specs=(spans, spans, P("mp", None), vector, P("mp", None), P("mp", None), vector, P("mp", None), vector, vector, vector,
                   P(None, "mp"), vector, P("mp", None), vector, vector, vector),
        check_vma=False,
    )
```

```python
import functools

import jax
import jax.numpy as jnp
from jax import lax
from jax.experimental import pallas as pl
from jax.experimental.pallas import tpu as pltpu
from jax.sharding import PartitionSpec as P

HEADS = 8
GROUPS = 2
INNER = 8
NEG = -1e30
C0 = (2.0 / 3.141592653589793) ** 0.5
C1 = C0 * 0.044715
f32 = jnp.float32
bf16 = jnp.bfloat16


def dot(left, right, a, b):
    return lax.dot_general(left, right, (((a,), (b,)), ((), ())), preferred_element_type=f32)


def nn(left, right):
    return dot(left, right, 1, 0)


def nt(left, right):
    return dot(left, right, 1, 1)


def tn(left, right):
    return dot(left, right, 0, 0)


def fold(v):
    return jnp.sum(v.reshape(v.shape[0] // 8, 8, v.shape[1]), 0)


def row_mean(v):
    return jnp.mean(v, -1, keepdims=True)


def cost(us):
    return pl.CostEstimate(flops=int(us * 1e9), bytes_accessed=int(us * 1e5), transcendentals=0)


def params(mib=60):
    return pltpu.CompilerParams(vmem_limit_bytes=mib * 2**20)


def whole(a):
    return pl.BlockSpec(a.shape, lambda *_: (0,) * len(a.shape), pipeline_mode=pl.Buffered(1))


ANY = pl.BlockSpec(memory_space=pl.ANY)


def shape(dims, dtype):
    return jax.ShapeDtypeStruct(tuple(dims), dtype)


def prep_body(at_ref, wi_ref, wb_ref, bi_ref, *refs):
    vectors, (piece_ref, vec_ref, turn) = refs[:8], refs[8:]
    cut = wi_ref.shape[1] // INNER
    start = pl.multiple_of(at_ref[0] * cut, cut)
    turn[...] = wi_ref[...].T
    piece_ref[:cut, :] = turn[pl.ds(start, cut), :]
    piece_ref[cut : 2 * cut, :] = wb_ref[pl.ds(start, cut), :]
    piece_ref[2 * cut :, :] = jnp.zeros((16, piece_ref.shape[1]), bf16)
    bias = bi_ref[...].astype(f32).reshape(1, -1)
    mine = jnp.zeros((1, cut), f32)
    for j in range(INNER):
        mine = jnp.where(at_ref[0] == j, bias[:, cut * j : cut * j + cut], mine)
    piece_ref[2 * cut :, :cut] = jnp.concatenate([mine, jnp.zeros((15, cut), f32)], 0).astype(bf16)
    for j, v in enumerate(vectors):
        vec_ref[j : j + 1, :] = v[...].astype(f32).reshape(1, -1)


def prep(at, wi, wb, bi, vectors):
    width, own = wi.shape
    out = [shape((2 * own // INNER + 16, width), bf16), shape((8, width), f32)]
    return pl.pallas_call(
        prep_body,
        grid_spec=pltpu.PrefetchScalarGridSpec(
            num_scalar_prefetch=1,
            grid=(1,),
            in_specs=[whole(a) for a in (wi, wb, bi, *vectors)],
            out_specs=[pl.BlockSpec(a.shape, lambda *_: (0, 0)) for a in out],
            scratch_shapes=[pltpu.VMEM((own, width), bf16)],
        ),
        out_shape=out,
        compiler_params=params(),
        cost_estimate=cost(3),
        name="prep",
    )(at, wi, wb, bi, *vectors)


def attend_body(rows, pad, skip, x_ref, wq_ref, wk_ref, wv_ref, wo_ref, vec_ref, *refs):
    qt_ref, k_ref, vt_ref, mt_ref, lt_ref, so_ref, xp, wqt, wvt, cols = refs[skip:]
    width = x_ref.shape[-1]
    hs = width // HEADS
    main = rows // 128 * 128
    left = pad - main
    group = 128 // left
    top = rows // 16 * 16

    @pl.when(pl.program_id(0) == 0)
    def _():
        wqt[...] = wq_ref[...].T
        wvt[...] = wv_ref[...].T
        xp[top:, :] = jnp.zeros((pad - top, width), bf16)
        cols[...] = vec_ref[0:8, :].T

    xp[:rows, :] = x_ref[0]
    x = xp[...]
    scale = hs**-0.5
    qt_ref[0] = (nt(wqt[...], x) + cols[:, 0:1]).astype(bf16) * bf16(scale)
    k_ref[0] = nn(x, wk_ref[...]).astype(bf16)
    vt_ref[0] = (nt(wvt[...], x) + cols[:, 1:2]).astype(bf16)
    valid = lax.broadcasted_iota(jnp.int32, (pad - top, 1), 0) < rows - top
    ones = jnp.ones((16, pad), bf16)

    def soft(st):
        s_top = st[:top]
        s_bot = jnp.where(valid, st[top:], NEG)
        m = jnp.maximum(jnp.max(s_top, 0, keepdims=True), jnp.max(s_bot, 0, keepdims=True))
        p = jnp.concatenate([jnp.exp(s_top - m).astype(bf16), jnp.exp(s_bot - m).astype(bf16)], 0)
        return m, p

    for h in range(HEADS):
        c = slice(hs * h, hs * h + hs)
        m, p = soft(nn(k_ref[0, :, c], qt_ref[0, c, :main]))
        ot = nn(jnp.concatenate([vt_ref[0, c, :], ones], 0), p)
        total = ot[hs : hs + 1]
        mt_ref[0, c, :main] = (ot[:hs] * (1.0 / total)).astype(bf16)
        lt_ref[0, h // (HEADS // GROUPS), h % (HEADS // GROUPS) : h % (HEADS // GROUPS) + 1, :main] = m + jnp.log(total)
    for g in range(HEADS // group):
        w = hs * group
        c = slice(w * g, w * g + w)
        same = (lax.broadcasted_iota(jnp.int32, (w, 128), 0) // hs
                == lax.broadcasted_iota(jnp.int32, (w, 128), 1) // left)
        ql = jnp.where(same, jnp.concatenate([qt_ref[0, c, main:pad]] * group, 1), 0).astype(bf16)
        m, p = soft(nn(k_ref[0, :, c], ql))
        ot = nn(jnp.concatenate([vt_ref[0, c, :], ones], 0), p)
        total = ot[w : w + 1]
        o = ot[:w] * (1.0 / total)
        lt = m + jnp.log(total)
        for j in range(group):
            h = g * group + j
            mt_ref[0, hs * h : hs * h + hs, main:pad] = o[hs * j : hs * j + hs, left * j : left * j + left].astype(bf16)
            lt_ref[0, h // (HEADS // GROUPS), h % (HEADS // GROUPS) : h % (HEADS // GROUPS) + 1, main:pad] = lt[:, left * j : left * j + left]
    so_ref[0] = tn(mt_ref[0], wo_ref[...]) + vec_ref[2:3, :] + xp[...].astype(f32)


def attend(sequence, wq, wk, wv, wo, vec, first, count, before=(), after=()):
    spans, rows, width = sequence.shape
    pad = (rows + 31) // 32 * 32
    per = HEADS // GROUPS
    spec = lambda a, b: pl.BlockSpec((1, a, b), lambda i: (i + first, 0, 0))
    return pl.pallas_call(
        functools.partial(attend_body, rows, pad, len(before) + len(after)),
        grid=(count,),
        in_specs=[spec(rows, width)] + [whole(w) for w in (wq, wk, wv, wo, vec)] + [ANY] * (len(before) + len(after)),
        out_specs=[spec(width, pad), spec(pad, width), spec(width, pad), spec(width, pad),
                   pl.BlockSpec((1, GROUPS, per, pad), lambda i: (i + first, 0, 0, 0)), spec(pad, width)],
        out_shape=[shape((spans, width, pad), bf16), shape((spans, pad, width), bf16), shape((spans, width, pad), bf16),
                   shape((spans, width, pad), bf16), shape((spans, GROUPS, per, pad), f32), shape((spans, pad, width), f32)],
        scratch_shapes=[pltpu.VMEM((pad, width), bf16), pltpu.VMEM((width, width), bf16), pltpu.VMEM((width, width), bf16),
                        pltpu.VMEM((width, 8), f32)],
        input_output_aliases={6 + n: n for n in range(len(before))},
        compiler_params=params(),
        cost_estimate=cost(16),
        name=f"attend{first}",
    )(sequence, wq, wk, wv, wo, vec, *before, *after)


def ffn_body(rows, own, slices, planes, at_ref, so_ref, ct_ref, wi_ref, wb_ref, bi_ref, vec_ref, wo_ref, *refs):
    (lo_ref, h_ref, g_ref, f_ref, nl_ref, gs_ref, ga_ref, dot_ref, col_ref, bin_ref,
     gp, col, binv, wit, wbs, b_ref) = refs[slices:]
    pad, width = so_ref.shape[1:]
    hidden = wit.shape[0]
    step = pl.program_id(0)

    @pl.when(step == 0)
    def _():
        col[...] = jnp.zeros_like(col)
        binv[...] = jnp.zeros_like(binv)
        wit[:own, :] = wi_ref[...].T
        wbs[:own, :] = wb_ref[...]
        b_ref[:, :own] = bi_ref[...].astype(f32).reshape(1, -1)
        at, n = own, own // INNER
        for a in refs[:slices]:
            for s in range(a.shape[0]):
                wit[at : at + n, :] = a[s, :n, :]
                wbs[at : at + n, :] = a[s, n : 2 * n, :]
                b_ref[:, at : at + n] = a[s, 2 * n :, :n].astype(f32)[0:1]
                at += n

    bb, g1, s1, g2, s2 = (vec_ref[n : n + 1, :] for n in range(3, 8))
    r = so_ref[0]
    c = r - row_mean(r)
    inv1 = lax.rsqrt(row_mean(c * c) + 1e-5)
    unit1 = c * inv1
    normed = unit1 * g1 + s1
    nl = normed.astype(bf16)
    nl_ref[0] = nl
    acc = normed + bb
    unit = 512
    for j in range(hidden // unit):
        cs = slice(unit * j, unit * j + unit)
        pre = nt(nl, wit[cs, :]) + b_ref[:, cs]
        sq = pre * pre
        t = jnp.tanh(pre * (C0 + C1 * sq))
        half = 0.5 + 0.5 * t
        act = (pre * half).astype(bf16)
        gp[:, cs] = half + pre * (0.5 * C0 + 1.5 * C1 * sq) * (1.0 - t * t)
        h_ref[0, :, cs] = act
        acc = acc + nn(act, wbs[cs, :])
    c = acc - row_mean(acc)
    inv2 = lax.rsqrt(row_mean(c * c) + 1e-5)
    unit2 = c * inv2
    lo_ref[0] = (unit2 * g2 + s2)[:rows].astype(bf16)
    up = jnp.concatenate([ct_ref[0].astype(f32), jnp.zeros((pad - rows, width), f32)], 0)
    gu = up * g2
    gs2 = inv2 * (gu - row_mean(gu) - unit2 * row_mean(gu * unit2))
    f = gs2.astype(bf16)
    f_ref[0] = f
    col[0] += fold(up * unit2)
    col[1] += fold(up)
    col[2] += fold(gs2)
    dn = gs2
    for j in range(hidden // unit):
        cs = slice(unit * j, unit * j + unit)
        g = nt(f, wbs[cs, :]) * gp[:, cs]
        binv[:, cs] += fold(g)
        g = g.astype(bf16)
        g_ref[0, :, cs] = g
        dn = dn + nn(g, wit[cs, :])
    gu = dn * g1
    gs1 = inv1 * (gu - row_mean(gu) - unit1 * row_mean(gu * unit1))
    gs_ref[0] = gs1
    ga = gs1.astype(bf16)
    ga_ref[0] = ga
    dot_ref[0] = nt(wo_ref[...], ga).astype(bf16)
    col[3] += fold(dn * unit1)
    col[4] += fold(dn)
    col[5] += fold(gs1)

    @pl.when(step == pl.num_programs(0) - 1)
    def _():
        col_ref[...] = jnp.sum(col[...], 1)
        total = jnp.sum(binv[...], 0, keepdims=True)
        n = own // INNER
        for j in range(INNER):
            peer = at_ref[0] ^ j
            row = ((peer & 1) * (INNER // 2) + (peer >> 1)) * planes
            bin_ref[pl.ds(row, 1), :] = total[:, n * j : n * j + n]
        at = own
        for q in range(INNER):
            for s in range(1, planes):
                bin_ref[q * planes + s : q * planes + s + 1, :] = total[:, at : at + n]
                at += n


def ffn(at, so, cotangent, wi, wb, bi, vec, wo, far):
    spans, pad, width = so.shape
    rows = cotangent.shape[1]
    own = wi.shape[1]
    cut = own // INNER
    planes = far[0].shape[0] + 1
    hidden = own * planes
    ws = (wi, wb, bi, vec, wo, *far)
    spec = lambda a, b: pl.BlockSpec((1, a, b), lambda i, *_: (i, 0, 0))
    one = lambda a, b: pl.BlockSpec((a, b), lambda i, *_: (0, 0))
    st = lambda a, b, t: shape((spans, a, b), t)
    return pl.pallas_call(
        functools.partial(ffn_body, rows, own, len(far), planes),
        grid_spec=pltpu.PrefetchScalarGridSpec(
            num_scalar_prefetch=1,
            grid=(spans,),
            in_specs=[spec(pad, width), spec(rows, width)] + [whole(w) for w in ws],
            out_specs=[spec(rows, width), spec(pad, hidden), spec(pad, hidden), spec(pad, width), spec(pad, width),
                       spec(pad, width), spec(pad, width), spec(width, pad), one(8, width), one(INNER * planes, cut)],
            scratch_shapes=[pltpu.VMEM((pad, hidden), f32), pltpu.VMEM((8, 8, width), f32), pltpu.VMEM((8, hidden), f32),
                            pltpu.VMEM((hidden, width), bf16), pltpu.VMEM((hidden, width), bf16), pltpu.VMEM((1, hidden), f32)],
        ),
        out_shape=[st(rows, width, bf16), st(pad, hidden, bf16), st(pad, hidden, bf16), st(pad, width, bf16), st(pad, width, bf16),
                   st(pad, width, f32), st(pad, width, bf16), st(width, pad, bf16), shape((8, width), f32),
                   shape((INNER * planes, cut), f32)],
        compiler_params=params(62),
        cost_estimate=cost(38),
        name="ffn",
    )(at, so, cotangent, *ws)


def vector_rows(vec, at_ref, peer, plane, planes, count):
    n = vec.shape[1] // planes
    rows = vec[:, pl.ds(pl.multiple_of(plane * n, n), n)]
    slot = lax.broadcasted_iota(jnp.int32, rows.shape, 0) == (at_ref[0] ^ peer)
    row = jnp.sum(jnp.where(slot, rows, 0.0), 0, keepdims=True)
    return jnp.concatenate([row, jnp.zeros((count - 1, n), f32)], 0)


def weight_body(own, planes, at_ref, h_ref, g_ref, f_ref, nl_ref, o0_ref, o1_ref):
    step = pl.program_id(0)
    block = h_ref.shape[1]
    cut = own // INNER
    per = block // cut
    blocks = own * planes // block
    first = own // block

    def place(part, mine, far, is_own, base):
        near = at_ref[0] ^ mine
        q = far // (planes - 1)
        half = jnp.where(is_own, near & 1, q // (INNER // 2))
        peer = jnp.where(is_own, near >> 1, q % (INNER // 2))
        shift = jnp.where(is_own, 0, far % (planes - 1) + 1)

        @pl.when(half == 0)
        def _():
            o0_ref[peer, shift, base : base + cut, :] = part

        @pl.when(half != 0)
        def _():
            o1_ref[peer, shift, base : base + cut, :] = part

    def matrix(a_ref, b_ref, at, base):
        piece = tn(a_ref[...], b_ref[...]).astype(bf16)
        for i in range(per):
            place(piece[cut * i : cut * i + cut], at * per + i, (at - first) * per + i, at < first, base)

    @pl.when(step < blocks)
    def _():
        matrix(h_ref, f_ref, step, 0)

    @pl.when(step >= blocks)
    def _():
        matrix(g_ref, nl_ref, step - blocks, cut)


def weight(at, h, g, f, nl, own, planes):
    rows, hidden = h.shape
    width = f.shape[1]
    block = 256
    blocks = hidden // block
    half = (INNER // 2, planes, 2 * own // INNER, width)
    out = pl.BlockSpec(half, lambda i, *_: (0, 0, 0, 0), pipeline_mode=pl.Buffered(1))
    lane = lambda a, b: pl.BlockSpec((rows, block), lambda i, *_: (0, jnp.clip(i - a, 0, b)))
    return pl.pallas_call(
        functools.partial(weight_body, own, planes),
        grid_spec=pltpu.PrefetchScalarGridSpec(
            num_scalar_prefetch=1,
            grid=(2 * blocks,),
            in_specs=[lane(0, blocks - 1), lane(blocks, blocks - 1), whole(f), whole(nl)],
            out_specs=[out, out],
        ),
        out_shape=[shape(half, bf16)] * 2,
        compiler_params=params(),
        cost_estimate=cost(23),
        name="weight",
    )(at, h, g, f, nl)


def out_body(planes, skip, at_ref, mt_ref, ga_ref, col_ref, bin_ref, *refs):
    o0_ref, o1_ref, acc = refs[skip:]
    step = pl.program_id(0)
    width = acc.shape[0]
    n = width // planes
    size = n // INNER
    side = bin_ref.shape[1]

    @pl.when(step == 0)
    def _():
        acc[...] = nn(mt_ref[0], ga_ref[0])

    @pl.when(step > 0)
    def _():
        acc[...] += nn(mt_ref[0], ga_ref[0])

    @pl.when(step == pl.num_programs(0) - 1)
    def _():
        for half, o_ref in enumerate((o0_ref, o1_ref)):
            for hi in range(INNER // 2):
                for s in range(planes):
                    peer = half + 2 * hi
                    plane = lax.rem(at_ref[1] + planes - s, planes)
                    start = plane * n + (at_ref[0] ^ peer) * size
                    o_ref[hi, s, :size, :] = acc[pl.ds(pl.multiple_of(start, size), size), :].astype(bf16)
                    at = (half * (INNER // 2) + hi) * planes + s
                    rows = [vector_rows(col_ref, at_ref, peer, plane, planes, 16),
                            jnp.concatenate([bin_ref[at : at + 1, :], jnp.zeros((15, side), f32)], 0)]
                    if n + side < width:
                        rows.append(jnp.zeros((16, width - n - side), f32))
                    o_ref[hi, s, size:, :] = jnp.concatenate(rows, 1).astype(bf16)


def out_weight(at, mt, ga, col, bins, planes, after):
    spans, width, pad = mt.shape
    half = (INNER // 2, planes, width // (planes * INNER) + 16, width)
    out = pl.BlockSpec(half, lambda i, *_: (0, 0, 0, 0))
    span = lambda a, b: pl.BlockSpec((1, a, b), lambda i, *_: (i, 0, 0))
    return pl.pallas_call(
        functools.partial(out_body, planes, len(after)),
        grid_spec=pltpu.PrefetchScalarGridSpec(
            num_scalar_prefetch=1,
            grid=(spans,),
            in_specs=[span(width, pad), span(pad, width), whole(col), whole(bins)] + [ANY] * len(after),
            out_specs=[out, out],
            scratch_shapes=[pltpu.VMEM((width, width), f32)],
        ),
        out_shape=[shape(half, bf16)] * 2,
        compiler_params=params(),
        cost_estimate=cost(6),
        name="w_out",
    )(at, mt, ga, col, bins, *after)


def join_body(count, *refs):
    for i in range(count):
        refs[-1][i] = refs[i][...]


def join(parts, after):
    return pl.pallas_call(
        functools.partial(join_body, len(parts)),
        in_specs=[pl.BlockSpec(memory_space=pltpu.VMEM)] * len(parts) + [ANY] * len(after),
        out_specs=pl.BlockSpec(memory_space=pltpu.VMEM),
        out_shape=shape((len(parts),) + parts[0].shape, bf16),
        compiler_params=params(),
        cost_estimate=cost(1),
        name="join",
    )(*parts, *after)


def add(*refs):
    total = refs[0][...].astype(f32)
    for ref in refs[1:]:
        total = total + ref[...].astype(f32)
    return total.astype(bf16)


def core_sum_body(pairs, axis, skip, *refs):
    outs = refs[2 * pairs + skip :]
    for p, o_ref in enumerate(outs):
        o_ref[...] = jnp.concatenate([add(refs[2 * i].at[p], refs[2 * i + 1].at[p]) for i in range(pairs)], axis)


def core_sum(pairs, axis, after, name):
    peers, planes, rows, width = pairs[0][0].shape
    if axis == 1:
        rows = sum(a.shape[2] for a, _ in pairs)
    else:
        width = sum(a.shape[3] for a, _ in pairs)
    flat = [a for pair in pairs for a in pair]
    return pl.pallas_call(
        functools.partial(core_sum_body, len(pairs), axis, len(after)),
        grid=(planes,),
        in_specs=[pl.BlockSpec((peers, 1) + a.shape[2:], lambda i: (0, i, 0, 0)) for a in flat] + [ANY] * len(after),
        out_specs=[pl.BlockSpec((1, rows, width), lambda i: (i, 0, 0))] * peers,
        out_shape=[shape((planes, rows, width), bf16)] * peers,
        compiler_params=params(),
        cost_estimate=cost(2),
        name=name,
    )(*flat, *after)


def plane_sum_body(count, skip, *refs):
    outs = refs[count + skip :]
    for s, o_ref in enumerate(outs):
        o_ref[...] = add(*(ref.at[s] for ref in refs[:count]))


def plane_sum(parts, after, name):
    planes, rows, width = parts[0].shape
    return pl.pallas_call(
        functools.partial(plane_sum_body, len(parts), len(after)),
        in_specs=[pl.BlockSpec(memory_space=pltpu.VMEM)] * len(parts) + [ANY] * len(after),
        out_specs=[pl.BlockSpec(memory_space=pltpu.VMEM)] * planes,
        out_shape=[shape((rows, width), bf16)] * planes,
        compiler_params=params(),
        cost_estimate=cost(2),
        name=name,
    )(*parts, *after)


def last_sum_body(count, groups, skip, *refs):
    o_ref = refs[count * groups + skip]
    at = 0
    for g in range(groups):
        part = add(*refs[count * g : count * g + count])
        o_ref[at : at + part.shape[0], :] = part
        at += part.shape[0]


def last_sum(groups, after, name):
    flat = [a for group in groups for a in group]
    rows = sum(group[0].shape[0] for group in groups)
    return pl.pallas_call(
        functools.partial(last_sum_body, len(groups[0]), len(groups), len(after)),
        in_specs=[pl.BlockSpec(memory_space=pltpu.VMEM)] * len(flat) + [ANY] * len(after),
        out_specs=pl.BlockSpec(memory_space=pltpu.VMEM),
        out_shape=shape((rows, flat[0].shape[1]), bf16),
        compiler_params=params(),
        cost_estimate=cost(2),
        name=name,
    )(*flat, *after)


def back_body(rows, planes, group, skip, at_ref, x_ref, qt_ref, k_ref, vt_ref, mt_ref, dt_ref, lt_ref, *refs):
    dq_ref, dk_ref, dv_ref, o0_ref, o1_ref, aq, ak, av, ab, xp, vec, turn = refs[skip:]
    w, pad = qt_ref.shape[1:]
    width = x_ref.shape[-1]
    hs = width // HEADS
    scale = hs**-0.5
    main = rows // 128 * 128
    left = pad - main
    heads = w // hs
    top = rows // 16 * 16
    step = pl.program_id(0)

    @pl.when(step == 0)
    def _():
        aq[...] = jnp.zeros_like(aq)
        ak[...] = jnp.zeros_like(ak)
        av[...] = jnp.zeros_like(av)
        ab[...] = jnp.zeros_like(ab)
        xp[top:, :] = jnp.zeros((pad - top, width), bf16)

    xp[:rows, :] = x_ref[0]
    k = k_ref[0]
    kt = k.T
    v = vt_ref[0].T
    valid = lax.broadcasted_iota(jnp.int32, (pad - top, 1), 0) < rows - top

    def core(ks, qs, vs, ds, ls, ms):
        delta = jnp.sum(ds.astype(f32) * ms.astype(f32), 0, keepdims=True)
        st = nn(ks, qs)
        st = jnp.concatenate([st[:top], jnp.where(valid, st[top:], NEG)], 0)
        p = jnp.exp(st - ls)
        gsc = (p * (nn(vs, ds) - delta)).astype(bf16)
        return p.astype(bf16), gsc

    same = (lax.broadcasted_iota(jnp.int32, (w, 128), 0) // hs
            == lax.broadcasted_iota(jnp.int32, (w, 128), 1) // left)
    tile = lambda a: jnp.where(same, jnp.concatenate([a] * heads, 1), 0).astype(bf16)
    ql, dl, ml = (tile(ref[0, :, main:pad]) for ref in (qt_ref, dt_ref, mt_ref))
    ll = jnp.concatenate([lt_ref[0, 0, h : h + 1, main:pad] for h in range(heads)], 1)
    p, gsc = core(k, ql, v, dl, ll, ml)
    dv_left = nt(dl, p)
    dk_left = nt(ql, gsc)
    dq_left = nn(kt, gsc)
    for h in range(heads):
        c = slice(hs * h, hs * h + hs)
        q, d = qt_ref[0, c, :main], dt_ref[0, c, :main]
        p, gsc = core(k[:, c], q, v[:, c], d, lt_ref[0, 0, h : h + 1, :main], mt_ref[0, c, :main])
        dv_ref[0, c, :] = (nt(d, p) + dv_left[c]).astype(bf16)
        dk_ref[0, c, :] = (nt(q, gsc) + dk_left[c]).astype(bf16)
        dq_ref[0, c, :main] = (nn(kt[c], gsc) * scale).astype(bf16)
        dq_ref[0, c, main:pad] = (dq_left[c, left * h : left * h + left] * scale).astype(bf16)
    x = xp[...]
    aq[...] += nn(dq_ref[0], x)
    ak[...] += nn(dk_ref[0], x)
    av[...] += nn(dv_ref[0], x)
    ab[:, 0:1] += jnp.sum(dq_ref[0].astype(f32), 1, keepdims=True)
    ab[:, 1:2] += jnp.sum(dv_ref[0].astype(f32), 1, keepdims=True)

    @pl.when(step == pl.num_programs(0) - 1)
    def _():
        size = width // (planes * INNER)
        n = width // planes
        vec[...] = jnp.zeros_like(vec)
        vec[:, group * w : group * w + w] = ab[...].T
        for i, a in enumerate((aq, ak, av)):
            turn[i] = a[...].T
        for half, o_ref in enumerate((o0_ref, o1_ref)):
            for hi in range(INNER // 2):
                for s in range(planes):
                    peer = half + 2 * hi
                    plane = lax.rem(at_ref[1] + planes - s, planes)
                    start = pl.multiple_of(plane * n + (at_ref[0] ^ peer) * size, size)
                    for i in range(3):
                        o_ref[hi, s, size * i : size * i + size, :] = turn[i, pl.ds(start, size), :].astype(bf16)
                    o_ref[hi, s, 3 * size :, :] = jnp.zeros((16, w), bf16)
                    o_ref[hi, s, 3 * size :, :n] = vector_rows(vec, at_ref, peer, plane, planes, 16).astype(bf16)


def back(at, sequence, qt, k, vt, mt, dt, lt, group, planes, after=()):
    spans, rows, width = sequence.shape
    pad = k.shape[1]
    w = width // GROUPS
    tr = pl.BlockSpec((1, w, pad), lambda i, *_: (i, group, 0))
    grad = pl.BlockSpec((1, w, pad), lambda i, *_: (i, 0, 0))
    half = (INNER // 2, planes, 3 * width // (planes * INNER) + 16, w)
    out = pl.BlockSpec(half, lambda i, *_: (0, 0, 0, 0))
    return pl.pallas_call(
        functools.partial(back_body, rows, planes, group, len(after)),
        grid_spec=pltpu.PrefetchScalarGridSpec(
            num_scalar_prefetch=1,
            grid=(spans,),
            in_specs=[pl.BlockSpec((1, rows, width), lambda i, *_: (i, 0, 0)), tr,
                      pl.BlockSpec((1, pad, w), lambda i, *_: (i, 0, group)), tr, tr, tr,
                      pl.BlockSpec((1, 1, HEADS // GROUPS, pad), lambda i, *_: (i, group, 0, 0))] + [ANY] * len(after),
            out_specs=[grad] * 3 + [out] * 2,
            scratch_shapes=[pltpu.VMEM((w, width), f32)] * 3
            + [pltpu.VMEM((w, 8), f32), pltpu.VMEM((pad, width), bf16), pltpu.VMEM((8, width), f32), pltpu.VMEM((3, width, w), f32)],
        ),
        out_shape=[shape((spans, w, pad), bf16)] * 3 + [shape(half, bf16)] * 2,
        compiler_params=params(),
        cost_estimate=cost(21),
        name=f"back{group}",
    )(at, sequence, qt, k, vt, mt, dt, lt, *after)


def input_body(rows, groups, skip, *refs):
    refs = refs[skip:]
    gs_ref = refs[0]
    parts = refs[1 : 1 + 3 * groups]
    ws = refs[1 + 3 * groups : 4 + 3 * groups]
    out_ref = refs[4 + 3 * groups]
    wt = refs[5 + 3 * groups :]

    @pl.when(pl.program_id(0) == 0)
    def _():
        for a, b in zip(wt, ws):
            a[...] = b[...].T

    total = gs_ref[0]
    for g in range(groups):
        for n in range(3):
            part = parts[3 * g + n]
            w = part.shape[1]
            total = total + tn(part[0], wt[n][w * g : w * g + w, :])
    out_ref[0] = total[:rows]


def input_grad(rows, gs, parts, wq, wk, wv, after=()):
    spans, pad, width = gs.shape
    flat = [a for part in parts for a in part]
    spec = lambda a: pl.BlockSpec((1,) + a.shape[1:], lambda i: (i, 0, 0))
    return pl.pallas_call(
        functools.partial(input_body, rows, len(parts), len(after)),
        grid=(spans,),
        in_specs=[ANY] * len(after) + [spec(gs)] + [spec(a) for a in flat] + [whole(w) for w in (wq, wk, wv)],
        out_specs=pl.BlockSpec((1, rows, width), lambda i: (i, 0, 0)),
        out_shape=shape((spans, rows, width), f32),
        scratch_shapes=[pltpu.VMEM((width, width), bf16)] * 3,
        compiler_params=params(),
        cost_estimate=cost(10),
        name="input_grad",
    )(*after, gs, *flat, wq, wk, wv)


def final_body(cut, at_ref, *refs):
    pieces = refs[:INNER]
    wb_ref, wi_ref, wo_ref, wq_ref, wk_ref, wv_ref, bin_ref, *vec_refs = refs[INNER:-2]
    turn, bins = refs[-2:]
    n, width = wo_ref.shape
    size = n // INNER
    w = width // GROUPS
    for q in range(INNER):
        slot = at_ref[0] ^ (q // (INNER // 2) + 2 * (q % (INNER // 2)))
        p = pieces[q]
        big = pl.ds(pl.multiple_of(slot * cut, cut), cut)
        small = pl.ds(pl.multiple_of(slot * size, size), size)
        wb_ref[big, :] = p[:cut, :].astype(f32)
        turn[big, :] = p[cut : 2 * cut, :].astype(f32)
        at = 2 * cut
        wo_ref[small, :] = p[at : at + size, :].astype(f32)
        at += size
        tail = p[at : at + 16, :].astype(f32)[0:1]
        bins[pl.ds(slot, 1), :] = tail[:, n : n + cut]
        for i in range(6):
            @pl.when(slot == i)
            def _():
                vec_refs[i][...] = tail[:, :n]
        at += 16
        for o_ref in (wq_ref, wk_ref, wv_ref):
            o_ref[small, :] = p[at : at + size, :].astype(f32)
            at += size
        tail = p[at : at + 16, :].astype(f32)[0:1]
        pair = tail[:, :n]
        for g in range(1, GROUPS):
            pair = pair + tail[:, w * g : w * g + n]
        for i in range(2):
            @pl.when(slot == i)
            def _():
                vec_refs[6 + i][...] = pair
    wi_ref[...] = turn[...].T
    bin_ref[...] = jnp.concatenate([bins[j : j + 1, :] for j in range(INNER)], 1)


def final(at, pieces, cut, planes):
    width = pieces[0].shape[1]
    own = cut * INNER
    n = width // planes
    out = [(own, width), (width, own)] + [(n, width)] * 4 + [(1, own)] + [(1, n)] * 8
    return pl.pallas_call(
        functools.partial(final_body, cut),
        grid_spec=pltpu.PrefetchScalarGridSpec(
            num_scalar_prefetch=1,
            grid=(1,),
            in_specs=[whole(a) for a in pieces],
            out_specs=[pl.BlockSpec(d, lambda *_: (0, 0)) for d in out],
            scratch_shapes=[pltpu.VMEM((own, width), f32), pltpu.VMEM((INNER, cut), f32)],
        ),
        out_shape=[shape(d, f32) for d in out],
        compiler_params=params(),
        cost_estimate=cost(4),
        name="final",
    )(at, *pieces)


def shards(dp, planes, sequence, cotangent, w_query, b_query, w_key, w_value, b_value, w_out, b_out, gain_attn, shift_attn,
           w_in, b_in, w_back, b_back, gain_ffn, shift_ffn):
    spans, rows, width = sequence.shape
    own = w_in.shape[1]
    cut = own // INNER
    at = jnp.stack([lax.axis_index("dp") & (INNER - 1), lax.axis_index("mp")]).astype(jnp.int32)

    def swap(a, k):
        return lax.ppermute(a, "dp", [(i, i ^ k) for i in range(dp)])

    def turn(a, s):
        return lax.ppermute(a, "mp", [(i, (i + s) % planes) for i in range(planes)])

    def spread(a, after=()):
        far = [a] + [swap(a, 2 * k) for k in range(1, INNER // 2)]
        far = lax.optimization_barrier((*far, *after))[: INNER // 2]
        return list(far) + [swap(b, 1) for b in far]

    def in_plane(parts, after, name):
        parts = [parts[0]] + [swap(parts[k], 2 * k) for k in range(1, INNER // 2)]
        totals = plane_sum(parts, after, name)
        step = INNER
        while step < dp:
            totals = [(t.astype(f32) + swap(t, step).astype(f32)).astype(bf16) for t in totals]
            step *= 2
        return totals

    def to_planes(totals):
        return [totals[0]] + [turn(totals[s], -s) for s in range(1, planes)]

    piece, vec = prep(at, w_in, w_back, b_in, (b_query, b_value, b_out, b_back, gain_attn, shift_attn, gain_ffn, shift_ffn))
    far = [turn(piece, s) for s in range(1, planes)]
    common = (sequence, w_query, w_key, w_value, w_out, vec)
    head = 1
    first = attend(*common, 0, head)
    far = join(far, first[:1])
    qt, k, vt, mt, lt, so = attend(*common, head, spans - head, first, (far,))
    layer_out, act, pre, gf, nl, gs, ga, dt, col, bins = ffn(at, so, cotangent, w_in, w_back, b_in, vec, w_out, spread(far, (so,)))
    flat = lambda a: a.reshape(-1, a.shape[-1])
    keep, send = weight(at, flat(act), flat(pre), flat(gf), flat(nl), own, planes)
    keep_o, send_o = out_weight(at, mt, ga, col, bins, planes, (keep,))
    parts = core_sum([(keep, swap(send, 1)), (keep_o, swap(send_o, 1))], 1, (), "core_ffn")
    *grad0, keep0, send0 = back(at, sequence, qt, k, vt, mt, dt, lt, 0, planes, (parts[0],))
    totals = in_plane(parts, (keep0,), "plane_ffn")
    *grad1, keep1, send1 = back(at, sequence, qt, k, vt, mt, dt, lt, 1, planes, (totals[0],))
    parts = core_sum([(keep0, swap(send0, 1)), (keep1, swap(send1, 1))], 2, (), "core_attn")
    ffn_parts = to_planes(totals)
    by_input = input_grad(rows, gs, [grad0, grad1], w_query, w_key, w_value, (parts[0],))
    totals = in_plane(parts, (by_input,), "plane_attn")
    pieces = spread(last_sum([ffn_parts, to_planes(totals)], (), "last"))
    wb, wi, wo, wq, wk, wv, bins, gg2, gs2, bb, gg1, gs1, bo, bq, bv = final(at, pieces, cut, planes)
    row = lambda a: a.reshape(-1)
    return (layer_out, by_input, wq, row(bq), wk, wv, row(bv), wo, row(bo), row(gg1), row(gs1), wi, row(bins), wb,
            row(bb), row(gg2), row(gs2))


def solution(mesh):
    spans, vector = P(("dp", "mp"), None, None), P("mp")
    return jax.shard_map(
        functools.partial(shards, mesh.shape["dp"], mesh.shape["mp"]),
        mesh=mesh,
        in_specs=(spans, spans) + (P(),) * 9 + (P(None, "mp"), vector, P("mp", None)) + (P(),) * 3,
        out_specs=(spans, spans, P("mp", None), vector, P("mp", None), P("mp", None), vector, P("mp", None), vector, vector, vector,
                   P(None, "mp"), vector, P("mp", None), vector, vector, vector),
        check_vma=False,
    )
```

```python
import functools

import jax
import jax.numpy as jnp
from jax import lax
from jax.experimental import pallas as pl
from jax.experimental.pallas import tpu as pltpu
from jax.sharding import PartitionSpec as P

HEADS = 8
GROUPS = 2
INNER = 8
NEG = -1e30
C0 = (2.0 / 3.141592653589793) ** 0.5
C1 = C0 * 0.044715
f32 = jnp.float32
bf16 = jnp.bfloat16


def dot(left, right, a, b):
    return lax.dot_general(left, right, (((a,), (b,)), ((), ())), preferred_element_type=f32)


def nn(left, right):
    return dot(left, right, 1, 0)


def nt(left, right):
    return dot(left, right, 1, 1)


def tn(left, right):
    return dot(left, right, 0, 0)


def fold(v):
    return jnp.sum(v.reshape(v.shape[0] // 8, 8, v.shape[1]), 0)


def row_mean(v):
    return jnp.mean(v, -1, keepdims=True)


def lanes(n):
    return (n + 127) // 128 * 128


def cost(us):
    return pl.CostEstimate(flops=int(us * 1e9), bytes_accessed=int(us * 1e5), transcendentals=0)


def params(mib=60):
    return pltpu.CompilerParams(vmem_limit_bytes=mib * 2**20)


def whole(a):
    return pl.BlockSpec(a.shape, lambda *_: (0,) * len(a.shape), pipeline_mode=pl.Buffered(1))


ANY = pl.BlockSpec(memory_space=pl.ANY)


def shape(dims, dtype):
    return jax.ShapeDtypeStruct(tuple(dims), dtype)


def prep_body(at_ref, wi_ref, wb_ref, bi_ref, piece_ref):
    a, b = wi_ref.shape[0], wb_ref.shape[0]
    piece_ref[:a, :] = wi_ref[...]
    piece_ref[a : a + b, :] = wb_ref[...]
    bias = bi_ref[...].astype(f32).reshape(1, -1)
    piece_ref[a + b :, :] = jnp.concatenate([bias, jnp.zeros((15, bias.shape[1]), f32)], 0).astype(bf16)


def prep(at, wi, wb, bi):
    width, own = wi.shape
    a, b = width // INNER, own // INNER
    return pl.pallas_call(
        prep_body,
        grid_spec=pltpu.PrefetchScalarGridSpec(
            num_scalar_prefetch=1,
            grid=(1,),
            in_specs=[pl.BlockSpec((a, own), lambda i, at: (at[0], 0)), pl.BlockSpec((b, width), lambda i, at: (at[0], 0)), whole(bi)],
            out_specs=pl.BlockSpec((a + b + 16, width), lambda *_: (0, 0)),
        ),
        out_shape=shape((a + b + 16, width), bf16),
        compiler_params=params(),
        cost_estimate=cost(2),
        name="prep",
    )(at, wi, wb, bi)


def vectors_body(*refs):
    for j, v in enumerate(refs[:8]):
        refs[-1][j : j + 1, :] = v[...].astype(f32).reshape(1, -1)


def stack_vectors(vectors, after):
    return pl.pallas_call(
        vectors_body,
        in_specs=[pl.BlockSpec(memory_space=pltpu.VMEM)] * 8 + [ANY] * len(after),
        out_specs=pl.BlockSpec(memory_space=pltpu.VMEM),
        out_shape=shape((8, vectors[0].shape[0]), f32),
        cost_estimate=cost(1),
        name="vectors",
    )(*vectors, *after)


def attend_body(rows, pad, skip, x_ref, wq_ref, wk_ref, wv_ref, wo_ref, vec_ref, *refs):
    qt_ref, k_ref, vt_ref, mt_ref, lt_ref, so_ref, xp, wqt, wvt, cols = refs[skip:]
    width = x_ref.shape[-1]
    hs = width // HEADS
    main = rows // 128 * 128
    left = pad - main
    group = 128 // left
    top = rows // 16 * 16

    @pl.when(pl.program_id(0) == 0)
    def _():
        wqt[...] = wq_ref[...].T
        wvt[...] = wv_ref[...].T
        xp[top:, :] = jnp.zeros((pad - top, width), bf16)
        cols[...] = vec_ref[0:8, :].T

    xp[:rows, :] = x_ref[0]
    x = xp[...]
    scale = hs**-0.5
    qt_ref[0, :, :pad] = (nt(wqt[...], x) + cols[:, 0:1]).astype(bf16) * bf16(scale)
    k_ref[0] = nn(x, wk_ref[...]).astype(bf16)
    vt_ref[0, :, :pad] = (nt(wvt[...], x) + cols[:, 1:2]).astype(bf16)
    valid = lax.broadcasted_iota(jnp.int32, (pad - top, 1), 0) < rows - top
    ones = jnp.ones((16, pad), bf16)

    def soft(st):
        s_top = st[:top]
        s_bot = jnp.where(valid, st[top:], NEG)
        m = jnp.maximum(jnp.max(s_top, 0, keepdims=True), jnp.max(s_bot, 0, keepdims=True))
        p = jnp.concatenate([jnp.exp(s_top - m).astype(bf16), jnp.exp(s_bot - m).astype(bf16)], 0)
        return m, p

    cs = [slice(hs * h, hs * h + hs) for h in range(HEADS)]
    following = nn(k_ref[0, :, cs[0]], qt_ref[0, cs[0], :main])
    for h in range(HEADS):
        c = cs[h]
        st = following
        if h + 1 < HEADS:
            following = nn(k_ref[0, :, cs[h + 1]], qt_ref[0, cs[h + 1], :main])
        m, p = soft(st)
        ot = nn(jnp.concatenate([vt_ref[0, c, :pad], ones], 0), p)
        total = ot[hs : hs + 1]
        mt_ref[0, c, :main] = (ot[:hs] * (1.0 / total)).astype(bf16)
        lt_ref[0, h // (HEADS // GROUPS), h % (HEADS // GROUPS) : h % (HEADS // GROUPS) + 1, :main] = m + jnp.log(total)
    for g in range(HEADS // group):
        w = hs * group
        c = slice(w * g, w * g + w)
        same = (lax.broadcasted_iota(jnp.int32, (w, 128), 0) // hs
                == lax.broadcasted_iota(jnp.int32, (w, 128), 1) // left)
        ql = jnp.where(same, jnp.concatenate([qt_ref[0, c, main:pad]] * group, 1), 0).astype(bf16)
        m, p = soft(nn(k_ref[0, :, c], ql))
        ot = nn(jnp.concatenate([vt_ref[0, c, :pad], ones], 0), p)
        total = ot[w : w + 1]
        o = ot[:w] * (1.0 / total)
        lt = m + jnp.log(total)
        for j in range(group):
            h = g * group + j
            mt_ref[0, hs * h : hs * h + hs, main:pad] = o[hs * j : hs * j + hs, left * j : left * j + left].astype(bf16)
            lt_ref[0, h // (HEADS // GROUPS), h % (HEADS // GROUPS) : h % (HEADS // GROUPS) + 1, main:pad] = lt[:, left * j : left * j + left]
    so_ref[0] = tn(mt_ref[0, :, :pad], wo_ref[...]) + vec_ref[2:3, :] + xp[...].astype(f32)


def attend(sequence, wq, wk, wv, wo, vec, first, count, before=(), after=()):
    spans, rows, width = sequence.shape
    pad = (rows + 31) // 32 * 32
    wide = lanes(pad)
    per = HEADS // GROUPS
    spec = lambda a, b: pl.BlockSpec((1, a, b), lambda i: (i + first, 0, 0))
    return pl.pallas_call(
        functools.partial(attend_body, rows, pad, len(before) + len(after)),
        grid=(count,),
        in_specs=[spec(rows, width)] + [whole(w) for w in (wq, wk, wv, wo, vec)] + [ANY] * (len(before) + len(after)),
        out_specs=[spec(width, wide), spec(pad, width), spec(width, wide), spec(width, wide),
                   pl.BlockSpec((1, GROUPS, per, wide), lambda i: (i + first, 0, 0, 0)), spec(pad, width)],
        out_shape=[shape((spans, width, wide), bf16), shape((spans, pad, width), bf16), shape((spans, width, wide), bf16),
                   shape((spans, width, wide), bf16), shape((spans, GROUPS, per, wide), f32), shape((spans, pad, width), f32)],
        scratch_shapes=[pltpu.VMEM((pad, width), bf16), pltpu.VMEM((width, width), bf16), pltpu.VMEM((width, width), bf16),
                        pltpu.VMEM((width, 8), f32)],
        input_output_aliases={6 + n: n for n in range(len(before))},
        compiler_params=params(),
        cost_estimate=cost(16),
        name=f"attend{first}",
    )(sequence, wq, wk, wv, wo, vec, *before, *after)


def vector_rows(vec, slot, count):
    mine = lax.broadcasted_iota(jnp.int32, vec.shape, 0) == slot
    row = jnp.sum(jnp.where(mine, vec, 0.0), 0, keepdims=True)
    return jnp.concatenate([row, jnp.zeros((count - 1, vec.shape[1]), f32)], 0)


def ffn_body(rows, slices, planes, at_ref, so_ref, ct_ref, mt_ref, vec_ref, wo_ref, bi_ref, bf_ref, wi_ref, wb_ref, *refs):
    (lo_ref, gs_ref, ga_ref, dot_ref, o0_ref, o1_ref,
     col, binv, wi, wb, one, two, inv1, act, pre_grad, low, grad, acc, turn, sem) = refs[slices:]
    pad, width = so_ref.shape[1:]
    own = wb_ref.shape[0]
    hidden = wb.shape[0]
    cut_in, cut_back = width // INNER, own // INNER
    step = pl.program_id(0)

    def slot_of(half, hi):
        return at_ref[0] ^ (half + 2 * hi)

    def loads():
        copies = [pltpu.make_async_copy(wi_ref, wi.at[:, :own], sem.at[0]),
                  pltpu.make_async_copy(wb_ref, wb.at[:own, :], sem.at[1])]
        for q in range(slices):
            slot = slot_of(q // (INNER // 2), q % (INNER // 2))
            for s in range(1, planes):
                n = 2 + 2 * (q * (planes - 1) + s - 1)
                there = wi.at[pl.ds(pl.multiple_of(slot * cut_in, cut_in), cut_in), own * s : own * s + own]
                copies.append(pltpu.make_async_copy(refs[q].at[s - 1, :cut_in, :], there, sem.at[n]))
                there = wb.at[pl.ds(pl.multiple_of(own * s + slot * cut_back, cut_back), cut_back), :]
                copies.append(pltpu.make_async_copy(refs[q].at[s - 1, cut_in : cut_in + cut_back, :], there, sem.at[n + 1]))
        return copies

    @pl.when(step == 0)
    def _():
        for c in loads():
            c.start()
        col[...] = jnp.zeros_like(col)
        binv[...] = jnp.zeros_like(binv)
        acc[...] = jnp.zeros_like(acc)

    bb, g1, s1, g2, s2 = (vec_ref[n : n + 1, :] for n in range(3, 8))
    base = pl.multiple_of(step * pad, pad)
    unit = own
    chunks = [slice(n, n + unit) for n in range(0, hidden, unit)]
    bias = [bi_ref[...].astype(f32).reshape(1, -1)] + [bf_ref[s : s + 1, :] for s in range(planes - 1)]
    zero = [jnp.zeros((8, width), f32)] * 3

    def chain(first, size, tall):
        here = pl.ds(pl.multiple_of(base + first, 16), size)
        blocks = [slice(first + n, first + n + tall) for n in range(0, size, tall)]
        local = lambda b: slice(b.start - first, b.stop - first)
        there = lambda b: pl.ds(pl.multiple_of(base + b.start, 16), tall)

        def norm():
            for b in blocks:
                r = so_ref[0, b, :]
                c = r - row_mean(r)
                inv = lax.rsqrt(row_mean(c * c) + 1e-5)
                unit1 = c * inv
                one[b, :] = unit1
                inv1[b, :] = jnp.broadcast_to(inv, (tall, 128))
                low[there(b), :] = (unit1 * g1 + s1).astype(bf16)

        def hidden_units():
            nl = low[here, :]
            for cs, add_bias in zip(chunks, bias):
                pre = nn(nl, wi[:, cs])
                for b in blocks:
                    v = pre[local(b)] + add_bias
                    sq = v * v
                    t = jnp.tanh(v * (C0 + C1 * sq))
                    half = 0.5 + 0.5 * t
                    act[there(b), cs] = (v * half).astype(bf16)
                    pre_grad[there(b), cs] = (half + v * (0.5 * C0 + 1.5 * C1 * sq) * (1.0 - t * t)).astype(bf16)

        def output():
            out = nn(act[here, :], wb[...])
            sums = zero
            for b in blocks:
                r = out[local(b)] + (one[b, :] * g1 + (s1 + bb))
                c = r - row_mean(r)
                inv = lax.rsqrt(row_mean(c * c) + 1e-5)
                unit2 = c * inv
                last = min(b.stop, rows)
                lo_ref[0, b.start : last, :] = (unit2 * g2 + s2)[: last - b.start].astype(bf16)
                up = ct_ref[0, b.start : last, :].astype(f32)
                if last < b.stop:
                    up = jnp.concatenate([up, jnp.zeros((b.stop - last, width), f32)], 0)
                gu = up * g2
                back = inv * (gu - row_mean(gu) - unit2 * row_mean(gu * unit2))
                two[b, :] = back
                grad[there(b), :] = back.astype(bf16)
                sums = [a + fold(v) for a, v in zip(sums, (up * unit2, up, back))]
            for n in range(3):
                col[n] += sums[n]

        def hidden_grads():
            f = grad[here, :]
            for cs in chunks:
                da = nt(f, wb[cs, :])
                total = jnp.zeros((8, unit), f32)
                for b in blocks:
                    g = da[local(b)] * pre_grad[there(b), cs].astype(f32)
                    total = total + fold(g)
                    pre_grad[there(b), cs] = g.astype(bf16)
                binv[:, cs] += total

        def input_grads():
            out = nt(pre_grad[here, :], wi[...])
            sums = zero
            for b in blocks:
                dn = out[local(b)] + two[b, :]
                unit1 = one[b, :]
                gu = dn * g1
                back = inv1[b, 0:1] * (gu - row_mean(gu) - unit1 * row_mean(gu * unit1))
                gs_ref[0, b, :] = back
                ga_ref[0, b, :] = back.astype(bf16)
                sums = [a + fold(v) for a, v in zip(sums, (dn * unit1, dn, back))]
            for n in range(3):
                col[3 + n] += sums[n]

        return norm, hidden_units, output, hidden_grads, input_grads

    parts, tall = 2, 16
    size = pad // parts
    plan = [[(0, 0), (1, 0)], [(0, 1), (1, 1), (0, 2), (1, 2), (0, 3), (1, 3), (0, 4), (1, 4)]]
    sections = [chain(n * size, size, tall) for n in range(parts)]
    for at, group in enumerate(plan):

        @pl.when(step >= 0)
        def _():
            for p, n in group:
                sections[p][n]()

        if at == 0:

            @pl.when(step == 0)
            def _():
                for c in loads():
                    c.wait()

    ga = ga_ref[0]
    dot_ref[0, :, :pad] = nt(wo_ref[...], ga).astype(bf16)
    acc[...] += nn(mt_ref[0, :, :pad], ga)

    @pl.when(step == pl.num_programs(0) - 1)
    def _():
        n = width // planes
        size = n // INNER
        outs = (o0_ref, o1_ref)
        peers = [(half, hi) for half in range(2) for hi in range(INNER // 2)]
        for m, (at, cut) in enumerate(((0, cut_in), (cut_in, cut_back))):
            for s, cs in enumerate(chunks):
                piece = tn(low[...], pre_grad[:, cs]) if m == 0 else tn(act[:, cs], grad[...])
                turn[m] = piece.astype(bf16)
                for half, hi in peers:
                    start = pl.multiple_of(slot_of(half, hi) * cut, cut)
                    outs[half][hi, s, at : at + cut, :] = turn[m, pl.ds(start, cut), :]
        at = cut_in + cut_back
        totals = jnp.sum(col[...], 1)
        bins = jnp.sum(binv[...], 0, keepdims=True)
        for s, cs in enumerate(chunks):
            plane = lax.rem(at_ref[1] + planes - s, planes)
            mine = jnp.zeros((8, n), f32)
            for p in range(planes):
                mine = jnp.where(plane == p, totals[:, n * p : n * p + n], mine)
            mine = jnp.concatenate([mine, jnp.zeros((8, width - n), f32)], 1)
            mine = jnp.where(lax.broadcasted_iota(jnp.int32, mine.shape, 0) == 6, bins[:, cs], mine)
            for half, hi in peers:
                slot = slot_of(half, hi)
                start = pl.multiple_of(plane * n + slot * size, size)
                outs[half][hi, s, at : at + size, :] = acc[pl.ds(start, size), :].astype(bf16)
                outs[half][hi, s, at + size :, :] = vector_rows(mine, slot, 16).astype(bf16)


def ffn(at, so, cotangent, mt, vec, wo, bi, bias_far, wi, wb, far):
    spans, pad, width = so.shape
    rows = cotangent.shape[1]
    own = wb.shape[0]
    planes = far[0].shape[0] + 1
    hidden = own * planes
    spec = lambda a, b: pl.BlockSpec((1, a, b), lambda i, *_: (i, 0, 0))
    st = lambda a, b, t: shape((spans, a, b), t)
    half = (INNER // 2, planes, (width + own) // INNER + width // (planes * INNER) + 16, width)
    out = pl.BlockSpec(half, lambda i, *_: (0, 0, 0, 0), pipeline_mode=pl.Buffered(1))
    total = spans * pad
    vmem = pltpu.VMEM
    return pl.pallas_call(
        functools.partial(ffn_body, rows, len(far), planes),
        grid_spec=pltpu.PrefetchScalarGridSpec(
            num_scalar_prefetch=1,
            grid=(spans,),
            in_specs=[spec(pad, width), spec(rows, width), spec(width, lanes(pad))] + [whole(w) for w in (vec, wo, bi, bias_far)]
            + [ANY] * (2 + len(far)),
            out_specs=[spec(rows, width), spec(pad, width), spec(pad, width), spec(width, lanes(pad)), out, out],
            scratch_shapes=[vmem((8, 8, width), f32), vmem((8, hidden), f32), vmem((width, hidden), bf16), vmem((hidden, width), bf16),
                            vmem((pad, width), f32), vmem((pad, width), f32), vmem((pad, 128), f32),
                            vmem((total, hidden), bf16), vmem((total, hidden), bf16), vmem((total, width), bf16),
                            vmem((total, width), bf16), vmem((width, width), f32), vmem((2, width, width), bf16),
                            pltpu.SemaphoreType.DMA((2 + 2 * len(far) * (planes - 1),))],
        ),
        out_shape=[st(rows, width, bf16), st(pad, width, f32), st(pad, width, bf16), st(width, lanes(pad), bf16)] + [shape(half, bf16)] * 2,
        compiler_params=params(62),
        cost_estimate=cost(46),
        name="ffn",
    )(at, so, cotangent, mt, vec, wo, bi, bias_far, wi, wb, *far)


def join_body(count, *refs):
    o_ref, b_ref = refs[-2:]
    rows = o_ref.shape[1]
    for i in range(count):
        o_ref[i] = refs[i][:rows, :]
        b_ref[i : i + 1, :] = refs[i][rows:, :].astype(f32)[0:1]


def join(parts, after):
    rows, width = parts[0].shape
    return pl.pallas_call(
        functools.partial(join_body, len(parts)),
        in_specs=[pl.BlockSpec(memory_space=pltpu.VMEM)] * len(parts) + [ANY] * len(after),
        out_specs=[pl.BlockSpec(memory_space=pltpu.VMEM)] * 2,
        out_shape=[shape((len(parts), rows - 16, width), bf16), shape((len(parts), width), f32)],
        compiler_params=params(),
        cost_estimate=cost(1),
        name="join",
    )(*parts, *after)


def add(*refs):
    total = refs[0][...].astype(f32)
    for ref in refs[1:]:
        total = total + ref[...].astype(f32)
    return total.astype(bf16)


def core_sum_body(pairs, axis, skip, *refs):
    outs = refs[2 * pairs + skip :]
    for p, o_ref in enumerate(outs):
        o_ref[...] = jnp.concatenate([add(refs[2 * i].at[p], refs[2 * i + 1].at[p]) for i in range(pairs)], axis)


def core_sum(pairs, axis, after, name):
    peers, planes, rows, width = pairs[0][0].shape
    if axis == 1:
        rows = sum(a.shape[2] for a, _ in pairs)
    else:
        width = sum(a.shape[3] for a, _ in pairs)
    flat = [a for pair in pairs for a in pair]
    return pl.pallas_call(
        functools.partial(core_sum_body, len(pairs), axis, len(after)),
        grid=(planes,),
        in_specs=[pl.BlockSpec((peers, 1) + a.shape[2:], lambda i: (0, i, 0, 0)) for a in flat] + [ANY] * len(after),
        out_specs=[pl.BlockSpec((1, rows, width), lambda i: (i, 0, 0))] * peers,
        out_shape=[shape((planes, rows, width), bf16)] * peers,
        compiler_params=params(),
        cost_estimate=cost(2),
        name=name,
    )(*flat, *after)


def plane_sum_body(count, skip, *refs):
    outs = refs[count + skip :]
    for s, o_ref in enumerate(outs):
        o_ref[...] = add(*(ref.at[s] for ref in refs[:count]))


def plane_sum(parts, after, name):
    planes, rows, width = parts[0].shape
    return pl.pallas_call(
        functools.partial(plane_sum_body, len(parts), len(after)),
        in_specs=[pl.BlockSpec(memory_space=pltpu.VMEM)] * len(parts) + [ANY] * len(after),
        out_specs=[pl.BlockSpec(memory_space=pltpu.VMEM)] * planes,
        out_shape=[shape((rows, width), bf16)] * planes,
        compiler_params=params(),
        cost_estimate=cost(2),
        name=name,
    )(*parts, *after)


def last_sum_body(count, groups, skip, *refs):
    o_ref = refs[count * groups + skip]
    at = 0
    for g in range(groups):
        part = add(*refs[count * g : count * g + count])
        o_ref[at : at + part.shape[0], :] = part
        at += part.shape[0]


def last_sum(groups, after, name):
    flat = [a for group in groups for a in group]
    rows = sum(group[0].shape[0] for group in groups)
    return pl.pallas_call(
        functools.partial(last_sum_body, len(groups[0]), len(groups), len(after)),
        in_specs=[pl.BlockSpec(memory_space=pltpu.VMEM)] * len(flat) + [ANY] * len(after),
        out_specs=pl.BlockSpec(memory_space=pltpu.VMEM),
        out_shape=shape((rows, flat[0].shape[1]), bf16),
        compiler_params=params(),
        cost_estimate=cost(2),
        name=name,
    )(*flat, *after)


def back_body(rows, planes, group, skip, at_ref, x_ref, qt_ref, k_ref, vt_ref, mt_ref, dt_ref, lt_ref, *refs):
    dq_ref, dk_ref, dv_ref, o0_ref, o1_ref, aq, ak, av, ab, xp, vec, turn = refs[skip:]
    w, pad = k_ref.shape[2], k_ref.shape[1]
    width = x_ref.shape[-1]
    hs = width // HEADS
    scale = hs**-0.5
    main = rows // 128 * 128
    left = pad - main
    heads = w // hs
    top = rows // 16 * 16
    step = pl.program_id(0)

    @pl.when(step == 0)
    def _():
        aq[...] = jnp.zeros_like(aq)
        ak[...] = jnp.zeros_like(ak)
        av[...] = jnp.zeros_like(av)
        ab[...] = jnp.zeros_like(ab)
        xp[top:, :] = jnp.zeros((pad - top, width), bf16)

    xp[:rows, :] = x_ref[0]
    k = k_ref[0]
    kt = k.T
    v = vt_ref[0, :, :pad].T
    valid = lax.broadcasted_iota(jnp.int32, (pad - top, 1), 0) < rows - top

    def core(ks, qs, vs, ds, ls, ms):
        delta = jnp.sum(ds.astype(f32) * ms.astype(f32), 0, keepdims=True)
        st = nn(ks, qs)
        st = jnp.concatenate([st[:top], jnp.where(valid, st[top:], NEG)], 0)
        p = jnp.exp(st - ls)
        gsc = (p * (nn(vs, ds) - delta)).astype(bf16)
        return p.astype(bf16), gsc

    same = (lax.broadcasted_iota(jnp.int32, (w, 128), 0) // hs
            == lax.broadcasted_iota(jnp.int32, (w, 128), 1) // left)
    tile = lambda a: jnp.where(same, jnp.concatenate([a] * heads, 1), 0).astype(bf16)
    ql, dl, ml = (tile(ref[0, :, main:pad]) for ref in (qt_ref, dt_ref, mt_ref))
    ll = jnp.concatenate([lt_ref[0, 0, h : h + 1, main:pad] for h in range(heads)], 1)
    p, gsc = core(k, ql, v, dl, ll, ml)
    dv_left = nt(dl, p)
    dk_left = nt(ql, gsc)
    dq_left = nn(kt, gsc)
    for h in range(heads):
        c = slice(hs * h, hs * h + hs)
        q, d = qt_ref[0, c, :main], dt_ref[0, c, :main]
        p, gsc = core(k[:, c], q, v[:, c], d, lt_ref[0, 0, h : h + 1, :main], mt_ref[0, c, :main])
        dv_ref[0, c, :pad] = (nt(d, p) + dv_left[c]).astype(bf16)
        dk_ref[0, c, :pad] = (nt(q, gsc) + dk_left[c]).astype(bf16)
        dq_ref[0, c, :main] = (nn(kt[c], gsc) * scale).astype(bf16)
        dq_ref[0, c, main:pad] = (dq_left[c, left * h : left * h + left] * scale).astype(bf16)
    x = xp[...]
    aq[...] += nn(dq_ref[0, :, :pad], x)
    ak[...] += nn(dk_ref[0, :, :pad], x)
    av[...] += nn(dv_ref[0, :, :pad], x)
    ab[:, 0:1] += jnp.sum(dq_ref[0, :, :pad].astype(f32), 1, keepdims=True)
    ab[:, 1:2] += jnp.sum(dv_ref[0, :, :pad].astype(f32), 1, keepdims=True)

    @pl.when(step == pl.num_programs(0) - 1)
    def _():
        size = width // (planes * INNER)
        n = width // planes
        vec[...] = jnp.zeros_like(vec)
        vec[:, group * w : group * w + w] = ab[...].T
        for i, a in enumerate((aq, ak, av)):
            turn[i] = a[...].T
        for half, o_ref in enumerate((o0_ref, o1_ref)):
            for hi in range(INNER // 2):
                for s in range(planes):
                    peer = half + 2 * hi
                    plane = lax.rem(at_ref[1] + planes - s, planes)
                    start = pl.multiple_of(plane * n + (at_ref[0] ^ peer) * size, size)
                    for i in range(3):
                        o_ref[hi, s, size * i : size * i + size, :] = turn[i, pl.ds(start, size), :].astype(bf16)
                    o_ref[hi, s, 3 * size :, :] = jnp.zeros((16, w), bf16)
                    mine = vec[:, pl.ds(pl.multiple_of(plane * n, n), n)]
                    o_ref[hi, s, 3 * size :, :n] = vector_rows(mine, at_ref[0] ^ peer, 16).astype(bf16)


def back(at, sequence, qt, k, vt, mt, dt, lt, group, planes, after=()):
    spans, rows, width = sequence.shape
    pad = k.shape[1]
    wide = qt.shape[2]
    w = width // GROUPS
    tr = pl.BlockSpec((1, w, wide), lambda i, *_: (i, group, 0))
    grad = pl.BlockSpec((1, w, wide), lambda i, *_: (i, 0, 0))
    half = (INNER // 2, planes, 3 * width // (planes * INNER) + 16, w)
    out = pl.BlockSpec(half, lambda i, *_: (0, 0, 0, 0))
    return pl.pallas_call(
        functools.partial(back_body, rows, planes, group, len(after)),
        grid_spec=pltpu.PrefetchScalarGridSpec(
            num_scalar_prefetch=1,
            grid=(spans,),
            in_specs=[pl.BlockSpec((1, rows, width), lambda i, *_: (i, 0, 0)), tr,
                      pl.BlockSpec((1, pad, w), lambda i, *_: (i, 0, group)), tr, tr, tr,
                      pl.BlockSpec((1, 1, HEADS // GROUPS, wide), lambda i, *_: (i, group, 0, 0))] + [ANY] * len(after),
            out_specs=[grad] * 3 + [out] * 2,
            scratch_shapes=[pltpu.VMEM((w, width), f32)] * 3
            + [pltpu.VMEM((w, 8), f32), pltpu.VMEM((pad, width), bf16), pltpu.VMEM((8, width), f32), pltpu.VMEM((3, width, w), f32)],
        ),
        out_shape=[shape((spans, w, wide), bf16)] * 3 + [shape(half, bf16)] * 2,
        compiler_params=params(),
        cost_estimate=cost(21),
        name=f"back{group}",
    )(at, sequence, qt, k, vt, mt, dt, lt, *after)


def input_body(rows, groups, skip, *refs):
    refs = refs[skip:]
    gs_ref = refs[0]
    parts = refs[1 : 1 + 3 * groups]
    ws = refs[1 + 3 * groups : 4 + 3 * groups]
    out_ref = refs[4 + 3 * groups]
    wt = refs[5 + 3 * groups :]

    @pl.when(pl.program_id(0) == 0)
    def _():
        for a, b in zip(wt, ws):
            a[...] = b[...].T

    total = gs_ref[0]
    for g in range(groups):
        for n in range(3):
            part = parts[3 * g + n]
            w = part.shape[1]
            total = total + tn(part[0, :, : total.shape[0]], wt[n][w * g : w * g + w, :])
    out_ref[0] = total[:rows]


def input_grad(rows, gs, parts, wq, wk, wv, after=()):
    spans, pad, width = gs.shape
    flat = [a for part in parts for a in part]
    spec = lambda a: pl.BlockSpec((1,) + a.shape[1:], lambda i: (i, 0, 0))
    return pl.pallas_call(
        functools.partial(input_body, rows, len(parts), len(after)),
        grid=(spans,),
        in_specs=[ANY] * len(after) + [spec(gs)] + [spec(a) for a in flat] + [whole(w) for w in (wq, wk, wv)],
        out_specs=pl.BlockSpec((1, rows, width), lambda i: (i, 0, 0)),
        out_shape=shape((spans, rows, width), f32),
        scratch_shapes=[pltpu.VMEM((width, width), bf16)] * 3,
        compiler_params=params(),
        cost_estimate=cost(10),
        name="input_grad",
    )(*after, gs, *flat, wq, wk, wv)


def ffn_final_body(cut_in, cut_back, skip, at_ref, *refs):
    pieces = refs[:INNER]
    wi_ref, wb_ref, wo_ref, bin_ref, *vec_refs = refs[INNER + skip :]
    n, width = wo_ref.shape
    size = n // INNER
    for q in range(INNER):
        slot = at_ref[0] ^ (q // (INNER // 2) + 2 * (q % (INNER // 2)))
        p = pieces[q]
        wi_ref[pl.ds(pl.multiple_of(slot * cut_in, cut_in), cut_in), :] = p[:cut_in, :].astype(f32)
        at = cut_in
        wb_ref[pl.ds(pl.multiple_of(slot * cut_back, cut_back), cut_back), :] = p[at : at + cut_back, :].astype(f32)
        at += cut_back
        wo_ref[pl.ds(pl.multiple_of(slot * size, size), size), :] = p[at : at + size, :].astype(f32)
        tail = p[at + size :, :].astype(f32)[0:1]
        for i, v_ref in enumerate(vec_refs):

            @pl.when(slot == i)
            def _():
                v_ref[...] = tail[:, :n]

        @pl.when(slot == len(vec_refs))
        def _():
            bin_ref[...] = tail


def attend_final_body(skip, at_ref, *refs):
    pieces = refs[:INNER]
    wq_ref, wk_ref, wv_ref, *vec_refs = refs[INNER + skip :]
    n, width = wq_ref.shape
    size = n // INNER
    w = width // GROUPS
    for q in range(INNER):
        slot = at_ref[0] ^ (q // (INNER // 2) + 2 * (q % (INNER // 2)))
        p = pieces[q]
        for i, o_ref in enumerate((wq_ref, wk_ref, wv_ref)):
            o_ref[pl.ds(pl.multiple_of(slot * size, size), size), :] = p[size * i : size * i + size, :].astype(f32)
        tail = p[3 * size :, :].astype(f32)[0:1]
        pair = tail[:, :n]
        for g in range(1, GROUPS):
            pair = pair + tail[:, w * g : w * g + n]
        for i, v_ref in enumerate(vec_refs):

            @pl.when(slot == i)
            def _():
                v_ref[...] = pair


def final(body, at, pieces, out, after, name):
    return pl.pallas_call(
        functools.partial(body, len(after)),
        grid_spec=pltpu.PrefetchScalarGridSpec(
            num_scalar_prefetch=1,
            grid=(1,),
            in_specs=[whole(a) for a in pieces] + [ANY] * len(after),
            out_specs=[pl.BlockSpec(d, lambda *_: (0, 0)) for d in out],
        ),
        out_shape=[shape(d, f32) for d in out],
        compiler_params=params(),
        cost_estimate=cost(3),
        name=name,
    )(at, *pieces, *after)


def shards(dp, planes, sequence, cotangent, w_query, b_query, w_key, w_value, b_value, w_out, b_out, gain_attn, shift_attn,
           w_in, b_in, w_back, b_back, gain_ffn, shift_ffn):
    spans, rows, width = sequence.shape
    own = w_in.shape[1]
    at = jnp.stack([lax.axis_index("dp") & (INNER - 1), lax.axis_index("mp")]).astype(jnp.int32)

    def swap(a, k):
        return lax.ppermute(a, "dp", [(i, i ^ k) for i in range(dp)])

    def turn(a, s):
        return lax.ppermute(a, "mp", [(i, (i + s) % planes) for i in range(planes)])

    def spread(a, after=()):
        far = [a] + [swap(a, 2 * k) for k in range(1, INNER // 2)]
        far = lax.optimization_barrier((*far, *after))[: INNER // 2]
        return list(far) + [swap(b, 1) for b in far]

    def in_plane(parts, after, name):
        parts = [parts[0]] + [swap(parts[k], 2 * k) for k in range(1, INNER // 2)]
        totals = plane_sum(parts, after, name)
        step = INNER
        while step < dp:
            totals = [(t.astype(f32) + swap(t, step).astype(f32)).astype(bf16) for t in totals]
            step *= 2
        return totals

    def to_planes(totals):
        return [totals[0]] + [turn(totals[s], -s) for s in range(1, planes)]

    piece = prep(at, w_in, w_back, b_in)
    far = [turn(piece, s) for s in range(1, planes)]
    vec = stack_vectors((b_query, b_value, b_out, b_back, gain_attn, shift_attn, gain_ffn, shift_ffn), (piece,))
    common = (sequence, w_query, w_key, w_value, w_out, vec)
    head = 1
    first = attend(*common, 0, head)
    far, bias_far = join(far, first[:1])
    qt, k, vt, mt, lt, so = attend(*common, head, spans - head, first, (far,))
    far = spread(far, (so,))
    layer_out, gs, ga, dt, keep, send = ffn(at, so, cotangent, mt, vec, w_out, b_in, bias_far, w_in, w_back, far)
    parts = core_sum([(keep, swap(send, 1))], 1, (), "core_ffn")
    *grad0, keep0, send0 = back(at, sequence, qt, k, vt, mt, dt, lt, 0, planes, (parts[0],))
    totals = in_plane(parts, (keep0,), "plane_ffn")
    *grad1, keep1, send1 = back(at, sequence, qt, k, vt, mt, dt, lt, 1, planes, (totals[0],))
    parts = core_sum([(keep0, swap(send0, 1)), (keep1, swap(send1, 1))], 2, (), "core_attn")
    ffn_parts = to_planes(totals)
    by_input = input_grad(rows, gs, [grad0, grad1], w_query, w_key, w_value, (parts[0],))
    totals = in_plane(parts, (by_input,), "plane_attn")
    ffn_sum = last_sum([ffn_parts], (totals[0],), "last_ffn")
    ffn_pieces = spread(ffn_sum)
    attn_sum = last_sum([to_planes(totals)], (ffn_sum,), "last_attn")
    attn_pieces = spread(attn_sum)
    n = width // planes
    wi, wb, wo, bins, gg2, gs2, bb, gg1, gs1, bo = final(
        functools.partial(ffn_final_body, width // INNER, own // INNER), at, ffn_pieces,
        [(width, own), (own, width), (n, width), (1, own)] + [(1, n)] * 6, (attn_sum,), "ffn_final")
    wq, wk, wv, bq, bv = final(attend_final_body, at, attn_pieces, [(n, width)] * 3 + [(1, n)] * 2, (wi,), "attend_final")
    row = lambda a: a.reshape(-1)
    return (layer_out, by_input, wq, row(bq), wk, wv, row(bv), wo, row(bo), row(gg1), row(gs1), wi, row(bins), wb,
            row(bb), row(gg2), row(gs2))


def solution(mesh):
    spans, vector = P(("dp", "mp"), None, None), P("mp")
    return jax.shard_map(
        functools.partial(shards, mesh.shape["dp"], mesh.shape["mp"]),
        mesh=mesh,
        in_specs=(spans, spans) + (P(),) * 9 + (P(None, "mp"), vector, P("mp", None)) + (P(),) * 3,
        out_specs=(spans, spans, P("mp", None), vector, P("mp", None), P("mp", None), vector, P("mp", None), vector, vector, vector,
                   P(None, "mp"), vector, P("mp", None), vector, vector, vector),
        check_vma=False,
    )
```

```python
import functools

import jax
import jax.numpy as jnp
from jax import lax
from jax.experimental import pallas as pl
from jax.experimental.pallas import tpu as pltpu
from jax.sharding import PartitionSpec as P

HEADS = 8
GROUPS = 2
INNER = 8
NEG = -1e30
C0 = (2.0 / 3.141592653589793) ** 0.5
C1 = C0 * 0.044715
LOG2E = 1.4426950408889634
f32 = jnp.float32
bf16 = jnp.bfloat16


def dot(left, right, a, b):
    return lax.dot_general(left, right, (((a,), (b,)), ((), ())), preferred_element_type=f32)


def nn(left, right):
    return dot(left, right, 1, 0)


def nt(left, right):
    return dot(left, right, 1, 1)


def tn(left, right):
    return dot(left, right, 0, 0)


def fold(v):
    return jnp.sum(v.reshape(v.shape[0] // 8, 8, v.shape[1]), 0)


def row_mean(v):
    return jnp.mean(v, -1, keepdims=True)


def lanes(n):
    return (n + 127) // 128 * 128


def cost(us):
    return pl.CostEstimate(flops=int(us * 1e9), bytes_accessed=int(us * 1e5), transcendentals=0)


def params(mib=60):
    return pltpu.CompilerParams(vmem_limit_bytes=mib * 2**20)


def whole(a):
    return pl.BlockSpec(a.shape, lambda *_: (0,) * len(a.shape), pipeline_mode=pl.Buffered(1))


ANY = pl.BlockSpec(memory_space=pl.ANY)


def shape(dims, dtype):
    return jax.ShapeDtypeStruct(tuple(dims), dtype)


def prep_body(at_ref, wi_ref, wb_ref, bi_ref, piece_ref):
    a, b = wi_ref.shape[0], wb_ref.shape[0]
    piece_ref[:a, :] = wi_ref[...]
    piece_ref[a : a + b, :] = wb_ref[...]
    bias = bi_ref[...].astype(f32).reshape(1, -1)
    piece_ref[a + b :, :] = jnp.concatenate([bias, jnp.zeros((15, bias.shape[1]), f32)], 0).astype(bf16)


def prep(at, wi, wb, bi):
    width, own = wi.shape
    a, b = width // INNER, own // INNER
    return pl.pallas_call(
        prep_body,
        grid_spec=pltpu.PrefetchScalarGridSpec(
            num_scalar_prefetch=1,
            grid=(1,),
            in_specs=[pl.BlockSpec((a, own), lambda i, at: (at[0], 0)), pl.BlockSpec((b, width), lambda i, at: (at[0], 0)), whole(bi)],
            out_specs=pl.BlockSpec((a + b + 16, width), lambda *_: (0, 0)),
        ),
        out_shape=shape((a + b + 16, width), bf16),
        compiler_params=params(),
        cost_estimate=cost(2),
        name="prep",
    )(at, wi, wb, bi)


def vectors_body(*refs):
    for j, v in enumerate(refs[:8]):
        refs[-1][j : j + 1, :] = v[...].astype(f32).reshape(1, -1)


def stack_vectors(vectors, after):
    return pl.pallas_call(
        vectors_body,
        in_specs=[pl.BlockSpec(memory_space=pltpu.VMEM)] * 8 + [ANY] * len(after),
        out_specs=pl.BlockSpec(memory_space=pltpu.VMEM),
        out_shape=shape((8, vectors[0].shape[0]), f32),
        cost_estimate=cost(1),
        name="vectors",
    )(*vectors, *after)


def attend_body(rows, pad, skip, x_ref, wq_ref, wk_ref, wv_ref, wo_ref, vec_ref, *refs):
    qt_ref, k_ref, v_ref, mt_ref, lt_ref, so_ref, xp, vt = refs[skip:]
    width = x_ref.shape[-1]
    hs = width // HEADS
    main = rows // 128 * 128
    left = pad - main
    group = 128 // left
    top = rows // 16 * 16

    @pl.when(pl.program_id(0) == 0)
    def _():
        xp[top:, :] = jnp.zeros((pad - top, width), bf16)

    xp[:rows, :] = x_ref[0]
    x = xp[...]
    scale = hs**-0.5
    qt_ref[0, :, :pad] = ((nn(x, wq_ref[...]) + vec_ref[0:1, :]) * (scale * LOG2E)).astype(bf16).T
    k_ref[0] = nn(x, wk_ref[...]).astype(bf16)
    v = (nn(x, wv_ref[...]) + vec_ref[1:2, :]).astype(bf16)
    v_ref[0] = v
    vt[...] = v.T
    valid = lax.broadcasted_iota(jnp.int32, (pad - top, 1), 0) < rows - top
    ones = jnp.ones((16, pad), bf16)

    def soft(st):
        s_top = st[:top]
        s_bot = jnp.where(valid, st[top:], NEG)
        m = jnp.maximum(jnp.max(s_top, 0, keepdims=True), jnp.max(s_bot, 0, keepdims=True))
        p = jnp.concatenate([jnp.exp2(s_top - m).astype(bf16), jnp.exp2(s_bot - m).astype(bf16)], 0)
        return m, p

    cs = [slice(hs * h, hs * h + hs) for h in range(HEADS)]
    following = nn(k_ref[0, :, cs[0]], qt_ref[0, cs[0], :main])
    for h in range(HEADS):
        c = cs[h]
        st = following
        if h + 1 < HEADS:
            following = nn(k_ref[0, :, cs[h + 1]], qt_ref[0, cs[h + 1], :main])
        m, p = soft(st)
        ot = nn(jnp.concatenate([vt[c, :], ones], 0), p)
        total = ot[hs : hs + 1]
        mt_ref[0, c, :main] = (ot[:hs] * (1.0 / total)).astype(bf16)
        lt_ref[0, h // (HEADS // GROUPS), h % (HEADS // GROUPS) : h % (HEADS // GROUPS) + 1, :main] = m + jnp.log2(total)
    for g in range(HEADS // group):
        w = hs * group
        c = slice(w * g, w * g + w)
        same = (lax.broadcasted_iota(jnp.int32, (w, 128), 0) // hs
                == lax.broadcasted_iota(jnp.int32, (w, 128), 1) // left)
        ql = jnp.where(same, jnp.concatenate([qt_ref[0, c, main:pad]] * group, 1), 0).astype(bf16)
        m, p = soft(nn(k_ref[0, :, c], ql))
        ot = nn(jnp.concatenate([vt[c, :], ones], 0), p)
        total = ot[w : w + 1]
        o = ot[:w] * (1.0 / total)
        lt = m + jnp.log2(total)
        for j in range(group):
            h = g * group + j
            mt_ref[0, hs * h : hs * h + hs, main:pad] = o[hs * j : hs * j + hs, left * j : left * j + left].astype(bf16)
            lt_ref[0, h // (HEADS // GROUPS), h % (HEADS // GROUPS) : h % (HEADS // GROUPS) + 1, main:pad] = lt[:, left * j : left * j + left]
    so_ref[0] = tn(mt_ref[0, :, :pad], wo_ref[...]) + vec_ref[2:3, :] + xp[...].astype(f32)


def attend(sequence, wq, wk, wv, wo, vec, first, count, before=(), after=()):
    spans, rows, width = sequence.shape
    pad = (rows + 31) // 32 * 32
    wide = lanes(pad)
    per = HEADS // GROUPS
    spec = lambda a, b: pl.BlockSpec((1, a, b), lambda i: (i + first, 0, 0))
    return pl.pallas_call(
        functools.partial(attend_body, rows, pad, len(before) + len(after)),
        grid=(count,),
        in_specs=[spec(rows, width)] + [whole(w) for w in (wq, wk, wv, wo, vec)] + [ANY] * (len(before) + len(after)),
        out_specs=[spec(width, wide), spec(pad, width), spec(pad, width), spec(width, wide),
                   pl.BlockSpec((1, GROUPS, per, wide), lambda i: (i + first, 0, 0, 0)), spec(pad, width)],
        out_shape=[shape((spans, width, wide), bf16), shape((spans, pad, width), bf16), shape((spans, pad, width), bf16),
                   shape((spans, width, wide), bf16), shape((spans, GROUPS, per, wide), f32), shape((spans, pad, width), f32)],
        scratch_shapes=[pltpu.VMEM((pad, width), bf16), pltpu.VMEM((width, pad), bf16)],
        input_output_aliases={6 + n: n for n in range(len(before))},
        compiler_params=params(),
        cost_estimate=cost(16),
        name=f"attend{first}",
    )(sequence, wq, wk, wv, wo, vec, *before, *after)


def vector_rows(vec, slot, count):
    mine = lax.broadcasted_iota(jnp.int32, vec.shape, 0) == slot
    row = jnp.sum(jnp.where(mine, vec, 0.0), 0, keepdims=True)
    return jnp.concatenate([row, jnp.zeros((count - 1, vec.shape[1]), f32)], 0)


def ffn_body(rows, slices, planes, at_ref, so_ref, ct_ref, mt_ref, vec_ref, wo_ref, bi_ref, bf_ref, wi_ref, wb_ref, *refs):
    (lo_ref, gs_ref, ga_ref, dot_ref, o0_ref, o1_ref,
     col, binv, wi, wb, one, two, inv1, act, pre_grad, low, grad, acc, turn, sem) = refs[slices:]
    pad, width = so_ref.shape[1:]
    own = wb_ref.shape[0]
    hidden = wb.shape[0]
    cut_in, cut_back = width // INNER, own // INNER
    step = pl.program_id(0)

    def slot_of(half, hi):
        return at_ref[0] ^ (half + 2 * hi)

    def loads():
        copies = [pltpu.make_async_copy(wi_ref, wi.at[:, :own], sem.at[0]),
                  pltpu.make_async_copy(wb_ref, wb.at[:own, :], sem.at[1])]
        for q in range(slices):
            slot = slot_of(q // (INNER // 2), q % (INNER // 2))
            for s in range(1, planes):
                n = 2 + 2 * (q * (planes - 1) + s - 1)
                there = wi.at[pl.ds(pl.multiple_of(slot * cut_in, cut_in), cut_in), own * s : own * s + own]
                copies.append(pltpu.make_async_copy(refs[q].at[s - 1, :cut_in, :], there, sem.at[n]))
                there = wb.at[pl.ds(pl.multiple_of(own * s + slot * cut_back, cut_back), cut_back), :]
                copies.append(pltpu.make_async_copy(refs[q].at[s - 1, cut_in : cut_in + cut_back, :], there, sem.at[n + 1]))
        return copies

    @pl.when(step == 0)
    def _():
        for c in loads():
            c.start()
        col[...] = jnp.zeros_like(col)
        binv[...] = jnp.zeros_like(binv)
        acc[...] = jnp.zeros_like(acc)

    bb, g1, s1, g2, s2 = (vec_ref[n : n + 1, :] for n in range(3, 8))
    base = pl.multiple_of(step * pad, pad)
    unit = own
    chunks = [slice(n, n + unit) for n in range(0, hidden, unit)]
    bias = [bi_ref[...].astype(f32).reshape(1, -1)] + [bf_ref[s : s + 1, :] for s in range(planes - 1)]
    zero = [jnp.zeros((8, width), f32)] * 3

    def chain(first, size, tall):
        here = pl.ds(pl.multiple_of(base + first, 16), size)
        blocks = [slice(first + n, first + n + tall) for n in range(0, size, tall)]
        local = lambda b: slice(b.start - first, b.stop - first)
        there = lambda b: pl.ds(pl.multiple_of(base + b.start, 16), tall)

        def norm():
            for b in blocks:
                r = so_ref[0, b, :]
                c = r - row_mean(r)
                inv = lax.rsqrt(row_mean(c * c) + 1e-5)
                unit1 = c * inv
                one[b, :] = unit1
                inv1[b, :] = jnp.broadcast_to(inv, (tall, 128))
                low[there(b), :] = (unit1 * g1 + s1).astype(bf16)

        def hidden_units():
            nl = low[here, :]
            for cs, add_bias in zip(chunks, bias):
                pre = nn(nl, wi[:, cs])
                for b in blocks:
                    v = pre[local(b)] + add_bias
                    cube = (v * v) * C1
                    t = jnp.tanh(v * (cube + C0))
                    double = (v * (1.0 + t)).astype(bf16)
                    act[there(b), cs] = double
                    t = t.astype(bf16)
                    slope = cube.astype(bf16) * bf16(3.0) + bf16(C0)
                    pre_grad[there(b), cs] = (bf16(1.0) + t) + double * ((bf16(1.0) - t) * slope)

        def output():
            out = nn(act[here, :], wb[...])
            sums = zero
            for b in blocks:
                r = out[local(b)] + (one[b, :] * g1 + (s1 + bb))
                c = r - row_mean(r)
                inv = lax.rsqrt(row_mean(c * c) + 1e-5)
                unit2 = c * inv
                last = min(b.stop, rows)
                lo_ref[0, b.start : last, :] = (unit2 * g2 + s2)[: last - b.start].astype(bf16)
                up = ct_ref[0, b.start : last, :].astype(f32)
                if last < b.stop:
                    up = jnp.concatenate([up, jnp.zeros((b.stop - last, width), f32)], 0)
                gu = up * g2
                back = inv * (gu - row_mean(gu) - unit2 * row_mean(gu * unit2))
                two[b, :] = back
                grad[there(b), :] = back.astype(bf16)
                sums = [a + fold(v) for a, v in zip(sums, (up * unit2, up, back))]
            for n in range(3):
                col[n] += sums[n]

        def hidden_grads():
            f = grad[here, :]
            for cs in chunks:
                da = nt(f, wb[cs, :])
                total = jnp.zeros((8, unit), f32)
                for b in blocks:
                    g = da[local(b)] * pre_grad[there(b), cs].astype(f32)
                    total = total + fold(g)
                    pre_grad[there(b), cs] = g.astype(bf16)
                binv[:, cs] += total

        def input_grads():
            out = nt(pre_grad[here, :], wi[...])
            sums = zero
            for b in blocks:
                dn = out[local(b)] + two[b, :]
                unit1 = one[b, :]
                gu = dn * g1
                back = inv1[b, 0:1] * (gu - row_mean(gu) - unit1 * row_mean(gu * unit1))
                gs_ref[0, b, :] = back
                ga_ref[0, b, :] = back.astype(bf16)
                sums = [a + fold(v) for a, v in zip(sums, (dn * unit1, dn, back))]
            for n in range(3):
                col[3 + n] += sums[n]

        return norm, hidden_units, output, hidden_grads, input_grads

    parts, tall = 2, 16
    size = pad // parts
    plan = [[(0, 0), (1, 0)], [(0, 1), (1, 1), (0, 2), (1, 2), (0, 3), (1, 3), (0, 4), (1, 4)]]
    sections = [chain(n * size, size, tall) for n in range(parts)]
    for at, group in enumerate(plan):

        @pl.when(step >= 0)
        def _():
            for p, n in group:
                sections[p][n]()

        if at == 0:

            @pl.when(step == 0)
            def _():
                for c in loads():
                    c.wait()
                wb[...] = wb[...] * bf16(0.5)

    ga = ga_ref[0]
    dot_ref[0, :, :pad] = nt(wo_ref[...], ga).astype(bf16)
    acc[...] += nn(mt_ref[0, :, :pad], ga)

    @pl.when(step == pl.num_programs(0) - 1)
    def _():
        n = width // planes
        size = n // INNER
        outs = (o0_ref, o1_ref)
        peers = [(half, hi) for half in range(2) for hi in range(INNER // 2)]
        for m, (at, cut) in enumerate(((0, cut_in), (cut_in, cut_back))):
            for s, cs in enumerate(chunks):
                piece = tn(low[...], pre_grad[:, cs]) if m == 0 else tn(act[:, cs], grad[...])
                turn[m] = piece.astype(bf16) if m == 0 else (0.5 * piece).astype(bf16)
                for half, hi in peers:
                    start = pl.multiple_of(slot_of(half, hi) * cut, cut)
                    outs[half][hi, s, at : at + cut, :] = turn[m, pl.ds(start, cut), :]
        at = cut_in + cut_back
        totals = jnp.sum(col[...], 1)
        bins = jnp.sum(binv[...], 0, keepdims=True)
        for s, cs in enumerate(chunks):
            plane = lax.rem(at_ref[1] + planes - s, planes)
            mine = jnp.zeros((8, n), f32)
            for p in range(planes):
                mine = jnp.where(plane == p, totals[:, n * p : n * p + n], mine)
            mine = jnp.concatenate([mine, jnp.zeros((8, width - n), f32)], 1)
            mine = jnp.where(lax.broadcasted_iota(jnp.int32, mine.shape, 0) == 6, bins[:, cs], mine)
            for half, hi in peers:
                slot = slot_of(half, hi)
                start = pl.multiple_of(plane * n + slot * size, size)
                outs[half][hi, s, at : at + size, :] = acc[pl.ds(start, size), :].astype(bf16)
                outs[half][hi, s, at + size :, :] = vector_rows(mine, slot, 16).astype(bf16)


def ffn(at, so, cotangent, mt, vec, wo, bi, bias_far, wi, wb, far):
    spans, pad, width = so.shape
    rows = cotangent.shape[1]
    own = wb.shape[0]
    planes = far[0].shape[0] + 1
    hidden = own * planes
    spec = lambda a, b: pl.BlockSpec((1, a, b), lambda i, *_: (i, 0, 0))
    st = lambda a, b, t: shape((spans, a, b), t)
    half = (INNER // 2, planes, (width + own) // INNER + width // (planes * INNER) + 16, width)
    out = pl.BlockSpec(half, lambda i, *_: (0, 0, 0, 0), pipeline_mode=pl.Buffered(1))
    total = spans * pad
    vmem = pltpu.VMEM
    return pl.pallas_call(
        functools.partial(ffn_body, rows, len(far), planes),
        grid_spec=pltpu.PrefetchScalarGridSpec(
            num_scalar_prefetch=1,
            grid=(spans,),
            in_specs=[spec(pad, width), spec(rows, width), spec(width, lanes(pad))] + [whole(w) for w in (vec, wo, bi, bias_far)]
            + [ANY] * (2 + len(far)),
            out_specs=[spec(rows, width), spec(pad, width), spec(pad, width), spec(width, lanes(pad)), out, out],
            scratch_shapes=[vmem((8, 8, width), f32), vmem((8, hidden), f32), vmem((width, hidden), bf16), vmem((hidden, width), bf16),
                            vmem((pad, width), f32), vmem((pad, width), f32), vmem((pad, 128), f32),
                            vmem((total, hidden), bf16), vmem((total, hidden), bf16), vmem((total, width), bf16),
                            vmem((total, width), bf16), vmem((width, width), f32), vmem((2, width, width), bf16),
                            pltpu.SemaphoreType.DMA((2 + 2 * len(far) * (planes - 1),))],
        ),
        out_shape=[st(rows, width, bf16), st(pad, width, f32), st(pad, width, bf16), st(width, lanes(pad), bf16)] + [shape(half, bf16)] * 2,
        compiler_params=params(62),
        cost_estimate=cost(46),
        name="ffn",
    )(at, so, cotangent, mt, vec, wo, bi, bias_far, wi, wb, *far)


def join_body(count, *refs):
    o_ref, b_ref = refs[-2:]
    rows = o_ref.shape[1]
    for i in range(count):
        o_ref[i] = refs[i][:rows, :]
        b_ref[i : i + 1, :] = refs[i][rows:, :].astype(f32)[0:1]


def join(parts, after):
    rows, width = parts[0].shape
    return pl.pallas_call(
        functools.partial(join_body, len(parts)),
        in_specs=[pl.BlockSpec(memory_space=pltpu.VMEM)] * len(parts) + [ANY] * len(after),
        out_specs=[pl.BlockSpec(memory_space=pltpu.VMEM)] * 2,
        out_shape=[shape((len(parts), rows - 16, width), bf16), shape((len(parts), width), f32)],
        compiler_params=params(),
        cost_estimate=cost(1),
        name="join",
    )(*parts, *after)


def add(*refs):
    total = refs[0][...].astype(f32)
    for ref in refs[1:]:
        total = total + ref[...].astype(f32)
    return total.astype(bf16)


def core_sum_body(pairs, axis, skip, *refs):
    outs = refs[2 * pairs + skip :]
    for p, o_ref in enumerate(outs):
        o_ref[...] = jnp.concatenate([add(refs[2 * i].at[p], refs[2 * i + 1].at[p]) for i in range(pairs)], axis)


def core_sum(pairs, axis, after, name):
    peers, planes, rows, width = pairs[0][0].shape
    if axis == 1:
        rows = sum(a.shape[2] for a, _ in pairs)
    else:
        width = sum(a.shape[3] for a, _ in pairs)
    flat = [a for pair in pairs for a in pair]
    return pl.pallas_call(
        functools.partial(core_sum_body, len(pairs), axis, len(after)),
        grid=(planes,),
        in_specs=[pl.BlockSpec((peers, 1) + a.shape[2:], lambda i: (0, i, 0, 0)) for a in flat] + [ANY] * len(after),
        out_specs=[pl.BlockSpec((1, rows, width), lambda i: (i, 0, 0))] * peers,
        out_shape=[shape((planes, rows, width), bf16)] * peers,
        compiler_params=params(),
        cost_estimate=cost(2),
        name=name,
    )(*flat, *after)


def plane_sum_body(count, skip, *refs):
    outs = refs[count + skip :]
    for s, o_ref in enumerate(outs):
        o_ref[...] = add(*(ref.at[s] for ref in refs[:count]))


def plane_sum(parts, after, name):
    planes, rows, width = parts[0].shape
    return pl.pallas_call(
        functools.partial(plane_sum_body, len(parts), len(after)),
        in_specs=[pl.BlockSpec(memory_space=pltpu.VMEM)] * len(parts) + [ANY] * len(after),
        out_specs=[pl.BlockSpec(memory_space=pltpu.VMEM)] * planes,
        out_shape=[shape((rows, width), bf16)] * planes,
        compiler_params=params(),
        cost_estimate=cost(2),
        name=name,
    )(*parts, *after)


def last_sum_body(count, groups, skip, *refs):
    o_ref = refs[count * groups + skip]
    at = 0
    for g in range(groups):
        part = add(*refs[count * g : count * g + count])
        o_ref[at : at + part.shape[0], :] = part
        at += part.shape[0]


def last_sum(groups, after, name):
    flat = [a for group in groups for a in group]
    rows = sum(group[0].shape[0] for group in groups)
    return pl.pallas_call(
        functools.partial(last_sum_body, len(groups[0]), len(groups), len(after)),
        in_specs=[pl.BlockSpec(memory_space=pltpu.VMEM)] * len(flat) + [ANY] * len(after),
        out_specs=pl.BlockSpec(memory_space=pltpu.VMEM),
        out_shape=shape((rows, flat[0].shape[1]), bf16),
        compiler_params=params(),
        cost_estimate=cost(2),
        name=name,
    )(*flat, *after)


def back_body(rows, planes, group, skip, at_ref, x_ref, qt_ref, k_ref, v_ref, mt_ref, dt_ref, lt_ref, *refs):
    dq_ref, dk_ref, dv_ref, o0_ref, o1_ref, aq, ak, av, ab, xp, vec, turn = refs[skip:]
    w, pad = k_ref.shape[2], k_ref.shape[1]
    width = x_ref.shape[-1]
    hs = width // HEADS
    scale = hs**-0.5
    main = rows // 128 * 128
    left = pad - main
    heads = w // hs
    top = rows // 16 * 16
    step = pl.program_id(0)

    @pl.when(step == 0)
    def _():
        aq[...] = jnp.zeros_like(aq)
        ak[...] = jnp.zeros_like(ak)
        av[...] = jnp.zeros_like(av)
        ab[...] = jnp.zeros_like(ab)
        xp[top:, :] = jnp.zeros((pad - top, width), bf16)

    xp[:rows, :] = x_ref[0]
    k = k_ref[0]
    kt = k.T
    v = v_ref[0]
    valid = lax.broadcasted_iota(jnp.int32, (pad - top, 1), 0) < rows - top

    def core(ks, qs, vs, ds, ls, ms):
        delta = jnp.sum(ds.astype(f32) * ms.astype(f32), 0, keepdims=True)
        st = nn(ks, qs)
        st = jnp.concatenate([st[:top], jnp.where(valid, st[top:], NEG)], 0)
        p = jnp.exp2(st - ls)
        gsc = (p * (nn(vs, ds) - delta)).astype(bf16)
        return p.astype(bf16), gsc

    same = (lax.broadcasted_iota(jnp.int32, (w, 128), 0) // hs
            == lax.broadcasted_iota(jnp.int32, (w, 128), 1) // left)
    tile = lambda a: jnp.where(same, jnp.concatenate([a] * heads, 1), 0).astype(bf16)
    ql, dl, ml = (tile(ref[0, :, main:pad]) for ref in (qt_ref, dt_ref, mt_ref))
    ll = jnp.concatenate([lt_ref[0, 0, h : h + 1, main:pad] for h in range(heads)], 1)
    p, gsc = core(k, ql, v, dl, ll, ml)
    dv_left = nt(dl, p)
    dk_left = nt(ql, gsc) * (1.0 / LOG2E)
    dq_left = nn(kt, gsc)
    for h in range(heads):
        c = slice(hs * h, hs * h + hs)
        q, d = qt_ref[0, c, :main], dt_ref[0, c, :main]
        p, gsc = core(k[:, c], q, v[:, c], d, lt_ref[0, 0, h : h + 1, :main], mt_ref[0, c, :main])
        dv_ref[0, c, :pad] = (nt(d, p) + dv_left[c]).astype(bf16)
        dk_ref[0, c, :pad] = (nt(q, gsc) * (1.0 / LOG2E) + dk_left[c]).astype(bf16)
        dq_ref[0, c, :main] = (nn(kt[c], gsc) * scale).astype(bf16)
        dq_ref[0, c, main:pad] = (dq_left[c, left * h : left * h + left] * scale).astype(bf16)
    x = xp[...]
    aq[...] += nn(dq_ref[0, :, :pad], x)
    ak[...] += nn(dk_ref[0, :, :pad], x)
    av[...] += nn(dv_ref[0, :, :pad], x)
    ab[:, 0:1] += jnp.sum(dq_ref[0, :, :pad].astype(f32), 1, keepdims=True)
    ab[:, 1:2] += jnp.sum(dv_ref[0, :, :pad].astype(f32), 1, keepdims=True)

    @pl.when(step == pl.num_programs(0) - 1)
    def _():
        size = width // (planes * INNER)
        n = width // planes
        vec[...] = jnp.zeros_like(vec)
        vec[:, group * w : group * w + w] = ab[...].T
        for i, a in enumerate((aq, ak, av)):
            turn[i] = a[...].T
        for half, o_ref in enumerate((o0_ref, o1_ref)):
            for hi in range(INNER // 2):
                for s in range(planes):
                    peer = half + 2 * hi
                    plane = lax.rem(at_ref[1] + planes - s, planes)
                    start = pl.multiple_of(plane * n + (at_ref[0] ^ peer) * size, size)
                    for i in range(3):
                        o_ref[hi, s, size * i : size * i + size, :] = turn[i, pl.ds(start, size), :].astype(bf16)
                    o_ref[hi, s, 3 * size :, :] = jnp.zeros((16, w), bf16)
                    mine = vec[:, pl.ds(pl.multiple_of(plane * n, n), n)]
                    o_ref[hi, s, 3 * size :, :n] = vector_rows(mine, at_ref[0] ^ peer, 16).astype(bf16)


def back(at, sequence, qt, k, v, mt, dt, lt, group, planes, after=()):
    spans, rows, width = sequence.shape
    pad = k.shape[1]
    wide = qt.shape[2]
    w = width // GROUPS
    tr = pl.BlockSpec((1, w, wide), lambda i, *_: (i, group, 0))
    nat = pl.BlockSpec((1, pad, w), lambda i, *_: (i, 0, group))
    grad = pl.BlockSpec((1, w, wide), lambda i, *_: (i, 0, 0))
    half = (INNER // 2, planes, 3 * width // (planes * INNER) + 16, w)
    out = pl.BlockSpec(half, lambda i, *_: (0, 0, 0, 0))
    return pl.pallas_call(
        functools.partial(back_body, rows, planes, group, len(after)),
        grid_spec=pltpu.PrefetchScalarGridSpec(
            num_scalar_prefetch=1,
            grid=(spans,),
            in_specs=[pl.BlockSpec((1, rows, width), lambda i, *_: (i, 0, 0)), tr,
                      nat, nat, tr, tr,
                      pl.BlockSpec((1, 1, HEADS // GROUPS, wide), lambda i, *_: (i, group, 0, 0))] + [ANY] * len(after),
            out_specs=[grad] * 3 + [out] * 2,
            scratch_shapes=[pltpu.VMEM((w, width), f32)] * 3
            + [pltpu.VMEM((w, 8), f32), pltpu.VMEM((pad, width), bf16), pltpu.VMEM((8, width), f32), pltpu.VMEM((3, width, w), f32)],
        ),
        out_shape=[shape((spans, w, wide), bf16)] * 3 + [shape(half, bf16)] * 2,
        compiler_params=params(),
        cost_estimate=cost(21),
        name=f"back{group}",
    )(at, sequence, qt, k, v, mt, dt, lt, *after)


def input_body(rows, groups, skip, *refs):
    refs = refs[skip:]
    gs_ref = refs[0]
    parts = refs[1 : 1 + 3 * groups]
    ws = refs[1 + 3 * groups : 4 + 3 * groups]
    out_ref = refs[4 + 3 * groups]
    wt = refs[5 + 3 * groups :]

    @pl.when(pl.program_id(0) == 0)
    def _():
        for a, b in zip(wt, ws):
            a[...] = b[...].T

    total = gs_ref[0]
    for g in range(groups):
        for n in range(3):
            part = parts[3 * g + n]
            w = part.shape[1]
            total = total + tn(part[0, :, : total.shape[0]], wt[n][w * g : w * g + w, :])
    out_ref[0] = total[:rows]


def input_grad(rows, gs, parts, wq, wk, wv, after=()):
    spans, pad, width = gs.shape
    flat = [a for part in parts for a in part]
    spec = lambda a: pl.BlockSpec((1,) + a.shape[1:], lambda i: (i, 0, 0))
    return pl.pallas_call(
        functools.partial(input_body, rows, len(parts), len(after)),
        grid=(spans,),
        in_specs=[ANY] * len(after) + [spec(gs)] + [spec(a) for a in flat] + [whole(w) for w in (wq, wk, wv)],
        out_specs=pl.BlockSpec((1, rows, width), lambda i: (i, 0, 0)),
        out_shape=shape((spans, rows, width), f32),
        scratch_shapes=[pltpu.VMEM((width, width), bf16)] * 3,
        compiler_params=params(),
        cost_estimate=cost(10),
        name="input_grad",
    )(*after, gs, *flat, wq, wk, wv)


def ffn_final_body(cut_in, cut_back, skip, at_ref, *refs):
    pieces = refs[:INNER]
    wi_ref, wb_ref, wo_ref, bin_ref, *vec_refs = refs[INNER + skip :]
    n, width = wo_ref.shape
    size = n // INNER
    for q in range(INNER):
        slot = at_ref[0] ^ (q // (INNER // 2) + 2 * (q % (INNER // 2)))
        p = pieces[q]
        wi_ref[pl.ds(pl.multiple_of(slot * cut_in, cut_in), cut_in), :] = p[:cut_in, :].astype(f32)
        at = cut_in
        wb_ref[pl.ds(pl.multiple_of(slot * cut_back, cut_back), cut_back), :] = p[at : at + cut_back, :].astype(f32)
        at += cut_back
        wo_ref[pl.ds(pl.multiple_of(slot * size, size), size), :] = p[at : at + size, :].astype(f32)
        tail = p[at + size :, :].astype(f32)[0:1]
        for i, v_ref in enumerate(vec_refs):

            @pl.when(slot == i)
            def _():
                v_ref[...] = tail[:, :n]

        @pl.when(slot == len(vec_refs))
        def _():
            bin_ref[...] = tail


def attend_final_body(skip, at_ref, *refs):
    pieces = refs[:INNER]
    wq_ref, wk_ref, wv_ref, *vec_refs = refs[INNER + skip :]
    n, width = wq_ref.shape
    size = n // INNER
    w = width // GROUPS
    for q in range(INNER):
        slot = at_ref[0] ^ (q // (INNER // 2) + 2 * (q % (INNER // 2)))
        p = pieces[q]
        for i, o_ref in enumerate((wq_ref, wk_ref, wv_ref)):
            o_ref[pl.ds(pl.multiple_of(slot * size, size), size), :] = p[size * i : size * i + size, :].astype(f32)
        tail = p[3 * size :, :].astype(f32)[0:1]
        pair = tail[:, :n]
        for g in range(1, GROUPS):
            pair = pair + tail[:, w * g : w * g + n]
        for i, v_ref in enumerate(vec_refs):

            @pl.when(slot == i)
            def _():
                v_ref[...] = pair


def final(body, at, pieces, out, after, name):
    return pl.pallas_call(
        functools.partial(body, len(after)),
        grid_spec=pltpu.PrefetchScalarGridSpec(
            num_scalar_prefetch=1,
            grid=(1,),
            in_specs=[whole(a) for a in pieces] + [ANY] * len(after),
            out_specs=[pl.BlockSpec(d, lambda *_: (0, 0)) for d in out],
        ),
        out_shape=[shape(d, f32) for d in out],
        compiler_params=params(),
        cost_estimate=cost(3),
        name=name,
    )(at, *pieces, *after)


def shards(dp, planes, sequence, cotangent, w_query, b_query, w_key, w_value, b_value, w_out, b_out, gain_attn, shift_attn,
           w_in, b_in, w_back, b_back, gain_ffn, shift_ffn):
    spans, rows, width = sequence.shape
    own = w_in.shape[1]
    at = jnp.stack([lax.axis_index("dp") & (INNER - 1), lax.axis_index("mp")]).astype(jnp.int32)

    def swap(a, k):
        return lax.ppermute(a, "dp", [(i, i ^ k) for i in range(dp)])

    def turn(a, s):
        return lax.ppermute(a, "mp", [(i, (i + s) % planes) for i in range(planes)])

    def spread(a, after=()):
        far = [a] + [swap(a, 2 * k) for k in range(1, INNER // 2)]
        far = lax.optimization_barrier((*far, *after))[: INNER // 2]
        return list(far) + [swap(b, 1) for b in far]

    def in_plane(parts, after, name):
        parts = [parts[0]] + [swap(parts[k], 2 * k) for k in range(1, INNER // 2)]
        totals = plane_sum(parts, after, name)
        step = INNER
        while step < dp:
            totals = [(t.astype(f32) + swap(t, step).astype(f32)).astype(bf16) for t in totals]
            step *= 2
        return totals

    def to_planes(totals):
        return [totals[0]] + [turn(totals[s], -s) for s in range(1, planes)]

    piece = prep(at, w_in, w_back, b_in)
    far = [turn(piece, s) for s in range(1, planes)]
    vec = stack_vectors((b_query, b_value, b_out, b_back, gain_attn, shift_attn, gain_ffn, shift_ffn), (piece,))
    common = (sequence, w_query, w_key, w_value, w_out, vec)
    head = 1
    first = attend(*common, 0, head)
    far, bias_far = join(far, first[:1])
    qt, k, v, mt, lt, so = attend(*common, head, spans - head, first, (far,))
    far = spread(far, (so,))
    layer_out, gs, ga, dt, keep, send = ffn(at, so, cotangent, mt, vec, w_out, b_in, bias_far, w_in, w_back, far)
    *grad0, keep0, send0 = back(at, sequence, qt, k, v, mt, dt, lt, 0, planes)
    ffn_parts = core_sum([(keep, swap(send, 1))], 1, (keep0,), "core_ffn")
    *grad1, keep1, send1 = back(at, sequence, qt, k, v, mt, dt, lt, 1, planes, (ffn_parts[0],))
    ffn_parts = to_planes(in_plane(ffn_parts, (keep1,), "plane_ffn"))
    parts = core_sum([(keep0, swap(send0, 1)), (keep1, swap(send1, 1))], 2, (ffn_parts[0],), "core_attn")
    by_input = input_grad(rows, gs, [grad0, grad1], w_query, w_key, w_value, (ffn_parts[0],))
    layer_out = lax.optimization_barrier(jnp.transpose(layer_out, (1, 0, 2)))
    totals = in_plane(parts, (by_input, layer_out), "plane_attn")
    ffn_sum = last_sum([ffn_parts], (totals[0],), "last_ffn")
    by_input = lax.optimization_barrier((by_input, ffn_sum))[0]
    by_input = lax.optimization_barrier(jnp.transpose(by_input, (1, 0, 2)))
    ffn_pieces = spread(ffn_sum)
    attn_sum = last_sum([to_planes(totals)], (ffn_sum, by_input), "last_attn")
    n = width // planes
    wi, wb, wo, bins, gg2, gs2, bb, gg1, gs1, bo = final(
        functools.partial(ffn_final_body, width // INNER, own // INNER), at, ffn_pieces,
        [(width, own), (own, width), (n, width), (1, own)] + [(1, n)] * 6, (attn_sum,), "ffn_final")
    attn_pieces = spread(attn_sum, (wi,))
    wq, wk, wv, bq, bv = final(attend_final_body, at, attn_pieces, [(n, width)] * 3 + [(1, n)] * 2, (), "attend_final")
    row = lambda a: a.reshape(-1)
    layer_out, by_input = (jnp.transpose(a, (1, 0, 2)) for a in (layer_out, by_input))
    return (layer_out, by_input, wq, row(bq), wk, wv, row(bv), wo, row(bo), row(gg1), row(gs1), wi, row(bins), wb,
            row(bb), row(gg2), row(gs2))


def solution(mesh):
    spans, vector = P(("dp", "mp"), None, None), P("mp")
    return jax.shard_map(
        functools.partial(shards, mesh.shape["dp"], mesh.shape["mp"]),
        mesh=mesh,
        in_specs=(spans, spans) + (P(),) * 9 + (P(None, "mp"), vector, P("mp", None)) + (P(),) * 3,
        out_specs=(spans, spans, P("mp", None), vector, P("mp", None), P("mp", None), vector, P("mp", None), vector, vector, vector,
                   P(None, "mp"), vector, P("mp", None), vector, vector, vector),
        check_vma=False,
    )
```

```python
import functools

import jax
import jax.numpy as jnp
from jax import lax
from jax.experimental import pallas as pl
from jax.experimental.pallas import tpu as pltpu
from jax.sharding import PartitionSpec as P

HEADS = 8
GROUPS = 2
INNER = 8
NEG = -1e30
C0 = (2.0 / 3.141592653589793) ** 0.5
C1 = C0 * 0.044715
LOG2E = 1.4426950408889634
f32 = jnp.float32
bf16 = jnp.bfloat16


def dot(left, right, a, b):
    return lax.dot_general(left, right, (((a,), (b,)), ((), ())), preferred_element_type=f32)


def nn(left, right):
    return dot(left, right, 1, 0)


def nt(left, right):
    return dot(left, right, 1, 1)


def tn(left, right):
    return dot(left, right, 0, 0)


def fold(v):
    return jnp.sum(v.reshape(v.shape[0] // 8, 8, v.shape[1]), 0)


def row_mean(v):
    return jnp.mean(v, -1, keepdims=True)


def lanes(n):
    return (n + 127) // 128 * 128


def cost(us):
    return pl.CostEstimate(flops=int(us * 1e9), bytes_accessed=int(us * 1e5), transcendentals=0)


def params(mib=60):
    return pltpu.CompilerParams(vmem_limit_bytes=mib * 2**20)


def whole(a):
    return pl.BlockSpec(a.shape, lambda *_: (0,) * len(a.shape), pipeline_mode=pl.Buffered(1))


ANY = pl.BlockSpec(memory_space=pl.ANY)


def shape(dims, dtype):
    return jax.ShapeDtypeStruct(tuple(dims), dtype)


def prep_body(at_ref, wi_ref, wb_ref, bi_ref, piece_ref):
    a, b = wi_ref.shape[0], wb_ref.shape[0]
    piece_ref[:a, :] = wi_ref[...]
    piece_ref[a : a + b, :] = wb_ref[...]
    bias = bi_ref[...].astype(f32).reshape(1, -1)
    piece_ref[a + b :, :] = jnp.concatenate([bias, jnp.zeros((15, bias.shape[1]), f32)], 0).astype(bf16)


def prep(at, wi, wb, bi):
    width, own = wi.shape
    a, b = width // INNER, own // INNER
    return pl.pallas_call(
        prep_body,
        grid_spec=pltpu.PrefetchScalarGridSpec(
            num_scalar_prefetch=1,
            grid=(1,),
            in_specs=[pl.BlockSpec((a, own), lambda i, at: (at[0], 0)), pl.BlockSpec((b, width), lambda i, at: (at[0], 0)), whole(bi)],
            out_specs=pl.BlockSpec((a + b + 16, width), lambda *_: (0, 0)),
        ),
        out_shape=shape((a + b + 16, width), bf16),
        compiler_params=params(),
        cost_estimate=cost(2),
        name="prep",
    )(at, wi, wb, bi)


def vectors_body(*refs):
    for j, v in enumerate(refs[:8]):
        refs[-1][j : j + 1, :] = v[...].astype(f32).reshape(1, -1)


def stack_vectors(vectors, after):
    return pl.pallas_call(
        vectors_body,
        in_specs=[pl.BlockSpec(memory_space=pltpu.VMEM)] * 8 + [ANY] * len(after),
        out_specs=pl.BlockSpec(memory_space=pltpu.VMEM),
        out_shape=shape((8, vectors[0].shape[0]), f32),
        cost_estimate=cost(1),
        name="vectors",
    )(*vectors, *after)


def attend_body(rows, pad, skip, x_ref, wq_ref, wk_ref, wv_ref, wo_ref, vec_ref, *refs):
    qt_ref, k_ref, v_ref, mt_ref, lt_ref, so_ref, q_ref, xp, vt = refs[skip:]
    width = x_ref.shape[-1]
    hs = width // HEADS
    main = rows // 128 * 128
    left = pad - main
    group = 128 // left
    top = rows // 16 * 16

    @pl.when(pl.program_id(0) == 0)
    def _():
        xp[top:, :] = jnp.zeros((pad - top, width), bf16)

    xp[:rows, :] = x_ref[0]
    x = xp[...]
    scale = hs**-0.5
    q = ((nn(x, wq_ref[...]) + vec_ref[0:1, :]) * (scale * LOG2E)).astype(bf16)
    q_ref[0] = q
    qt_ref[0, :, :pad] = q.T
    k_ref[0] = nn(x, wk_ref[...]).astype(bf16)
    v = (nn(x, wv_ref[...]) + vec_ref[1:2, :]).astype(bf16)
    v_ref[0] = v
    vt[...] = v.T
    valid = lax.broadcasted_iota(jnp.int32, (pad - top, 1), 0) < rows - top
    ones = jnp.ones((16, pad), bf16)

    def soft(st):
        s_top = st[:top]
        s_bot = jnp.where(valid, st[top:], NEG)
        m = jnp.maximum(jnp.max(s_top, 0, keepdims=True), jnp.max(s_bot, 0, keepdims=True))
        p = jnp.concatenate([jnp.exp2(s_top - m).astype(bf16), jnp.exp2(s_bot - m).astype(bf16)], 0)
        return m, p

    cs = [slice(hs * h, hs * h + hs) for h in range(HEADS)]
    following = nn(k_ref[0, :, cs[0]], qt_ref[0, cs[0], :main])
    for h in range(HEADS):
        c = cs[h]
        st = following
        if h + 1 < HEADS:
            following = nn(k_ref[0, :, cs[h + 1]], qt_ref[0, cs[h + 1], :main])
        m, p = soft(st)
        ot = nn(jnp.concatenate([vt[c, :], ones], 0), p)
        total = ot[hs : hs + 1]
        mt_ref[0, c, :main] = (ot[:hs] * (1.0 / total)).astype(bf16)
        lt_ref[0, h // (HEADS // GROUPS), h % (HEADS // GROUPS) : h % (HEADS // GROUPS) + 1, :main] = m + jnp.log2(total)
    for g in range(HEADS // group):
        w = hs * group
        c = slice(w * g, w * g + w)
        same = (lax.broadcasted_iota(jnp.int32, (w, 128), 0) // hs
                == lax.broadcasted_iota(jnp.int32, (w, 128), 1) // left)
        ql = jnp.where(same, jnp.concatenate([qt_ref[0, c, main:pad]] * group, 1), 0).astype(bf16)
        m, p = soft(nn(k_ref[0, :, c], ql))
        ot = nn(jnp.concatenate([vt[c, :], ones], 0), p)
        total = ot[w : w + 1]
        o = ot[:w] * (1.0 / total)
        lt = m + jnp.log2(total)
        for j in range(group):
            h = g * group + j
            mt_ref[0, hs * h : hs * h + hs, main:pad] = o[hs * j : hs * j + hs, left * j : left * j + left].astype(bf16)
            lt_ref[0, h // (HEADS // GROUPS), h % (HEADS // GROUPS) : h % (HEADS // GROUPS) + 1, main:pad] = lt[:, left * j : left * j + left]
    so_ref[0] = tn(mt_ref[0, :, :pad], wo_ref[...]) + vec_ref[2:3, :] + xp[...].astype(f32)


def attend(sequence, wq, wk, wv, wo, vec, first, count, before=(), after=()):
    spans, rows, width = sequence.shape
    pad = (rows + 31) // 32 * 32
    wide = lanes(pad)
    per = HEADS // GROUPS
    spec = lambda a, b: pl.BlockSpec((1, a, b), lambda i: (i + first, 0, 0))
    return pl.pallas_call(
        functools.partial(attend_body, rows, pad, len(before) + len(after)),
        grid=(count,),
        in_specs=[spec(rows, width)] + [whole(w) for w in (wq, wk, wv, wo, vec)] + [ANY] * (len(before) + len(after)),
        out_specs=[spec(width, wide), spec(pad, width), spec(pad, width), spec(width, wide),
                   pl.BlockSpec((1, GROUPS, per, wide), lambda i: (i + first, 0, 0, 0)), spec(pad, width), spec(pad, width)],
        out_shape=[shape((spans, width, wide), bf16), shape((spans, pad, width), bf16), shape((spans, pad, width), bf16),
                   shape((spans, width, wide), bf16), shape((spans, GROUPS, per, wide), f32), shape((spans, pad, width), f32),
                   shape((spans, pad, width), bf16)],
        scratch_shapes=[pltpu.VMEM((pad, width), bf16), pltpu.VMEM((width, pad), bf16)],
        input_output_aliases={6 + n: n for n in range(len(before))},
        compiler_params=params(),
        cost_estimate=cost(16),
        name=f"attend{first}",
    )(sequence, wq, wk, wv, wo, vec, *before, *after)


def vector_rows(vec, slot, count):
    mine = lax.broadcasted_iota(jnp.int32, vec.shape, 0) == slot
    row = jnp.sum(jnp.where(mine, vec, 0.0), 0, keepdims=True)
    return jnp.concatenate([row, jnp.zeros((count - 1, vec.shape[1]), f32)], 0)


def ffn_body(rows, slices, planes, at_ref, so_ref, ct_ref, mt_ref, vec_ref, wo_ref, bi_ref, bf_ref, wi_ref, wb_ref, *refs):
    (lo_ref, gs_ref, d_ref, dot_ref, o0_ref, o1_ref,
     col, binv, wi, wb, one, two, inv1, act, pre_grad, low, grad, acc, turn, low_grad, sem) = refs[slices:]
    pad, width = so_ref.shape[1:]
    own = wb_ref.shape[0]
    hidden = wb.shape[0]
    cut_in, cut_back = width // INNER, own // INNER
    step = pl.program_id(0)

    def slot_of(half, hi):
        return at_ref[0] ^ (half + 2 * hi)

    def loads():
        copies = [pltpu.make_async_copy(wi_ref, wi.at[:, :own], sem.at[0]),
                  pltpu.make_async_copy(wb_ref, wb.at[:own, :], sem.at[1])]
        for q in range(slices):
            slot = slot_of(q // (INNER // 2), q % (INNER // 2))
            for s in range(1, planes):
                n = 2 + 2 * (q * (planes - 1) + s - 1)
                there = wi.at[pl.ds(pl.multiple_of(slot * cut_in, cut_in), cut_in), own * s : own * s + own]
                copies.append(pltpu.make_async_copy(refs[q].at[s - 1, :cut_in, :], there, sem.at[n]))
                there = wb.at[pl.ds(pl.multiple_of(own * s + slot * cut_back, cut_back), cut_back), :]
                copies.append(pltpu.make_async_copy(refs[q].at[s - 1, cut_in : cut_in + cut_back, :], there, sem.at[n + 1]))
        return copies

    @pl.when(step == 0)
    def _():
        for c in loads():
            c.start()
        col[...] = jnp.zeros_like(col)
        binv[...] = jnp.zeros_like(binv)
        acc[...] = jnp.zeros_like(acc)

    bb, g1, s1, g2, s2 = (vec_ref[n : n + 1, :] for n in range(3, 8))
    base = pl.multiple_of(step * pad, pad)
    unit = own
    chunks = [slice(n, n + unit) for n in range(0, hidden, unit)]
    bias = [bi_ref[...].astype(f32).reshape(1, -1)] + [bf_ref[s : s + 1, :] for s in range(planes - 1)]
    zero = [jnp.zeros((8, width), f32)] * 3

    def chain(first, size, tall):
        here = pl.ds(pl.multiple_of(base + first, 16), size)
        blocks = [slice(first + n, first + n + tall) for n in range(0, size, tall)]
        local = lambda b: slice(b.start - first, b.stop - first)
        there = lambda b: pl.ds(pl.multiple_of(base + b.start, 16), tall)

        def norm():
            for b in blocks:
                r = so_ref[0, b, :]
                c = r - row_mean(r)
                inv = lax.rsqrt(row_mean(c * c) + 1e-5)
                unit1 = c * inv
                one[b, :] = unit1
                inv1[b, :] = jnp.broadcast_to(inv, (tall, 128))
                low[there(b), :] = (unit1 * g1 + s1).astype(bf16)

        def hidden_units():
            nl = low[here, :]
            for cs, add_bias in zip(chunks, bias):
                pre = nn(nl, wi[:, cs])
                for b in blocks:
                    v = (pre[local(b)] + add_bias).astype(bf16)
                    cube = (v * v) * bf16(C1)
                    t = jnp.tanh(v * (cube + bf16(C0)))
                    double = v * (bf16(1.0) + t)
                    act[there(b), cs] = double
                    slope = cube * bf16(3.0) + bf16(C0)
                    pre_grad[there(b), cs] = (bf16(1.0) + t) + double * ((bf16(1.0) - t) * slope)

        def output():
            out = nn(act[here, :], wb[...])
            sums = zero
            for b in blocks:
                r = out[local(b)] + (one[b, :] * g1 + (s1 + bb))
                c = r - row_mean(r)
                inv = lax.rsqrt(row_mean(c * c) + 1e-5)
                unit2 = c * inv
                last = min(b.stop, rows)
                lo_ref[0, b.start : last, :] = (unit2 * g2 + s2)[: last - b.start].astype(bf16)
                up = ct_ref[0, b.start : last, :].astype(f32)
                if last < b.stop:
                    up = jnp.concatenate([up, jnp.zeros((b.stop - last, width), f32)], 0)
                gu = up * g2
                back = inv * (gu - row_mean(gu) - unit2 * row_mean(gu * unit2))
                two[b, :] = back
                grad[there(b), :] = back.astype(bf16)
                sums = [a + fold(v) for a, v in zip(sums, (up * unit2, up, back))]
            for n in range(3):
                col[n] += sums[n]

        def hidden_grads():
            f = grad[here, :]
            for cs in chunks:
                da = nt(f, wb[cs, :])
                total = jnp.zeros((8, unit), f32)
                for b in blocks:
                    g = da[local(b)] * pre_grad[there(b), cs].astype(f32)
                    total = total + fold(g)
                    pre_grad[there(b), cs] = g.astype(bf16)
                binv[:, cs] += total

        def input_grads():
            out = nt(pre_grad[here, :], wi[...])
            sums = zero
            for b in blocks:
                dn = out[local(b)] + two[b, :]
                unit1 = one[b, :]
                gu = dn * g1
                back = inv1[b, 0:1] * (gu - row_mean(gu) - unit1 * row_mean(gu * unit1))
                gs_ref[0, b, :] = back
                low_grad[b, :] = back.astype(bf16)
                sums = [a + fold(v) for a, v in zip(sums, (dn * unit1, dn, back))]
            for n in range(3):
                col[3 + n] += sums[n]

        return norm, hidden_units, output, hidden_grads, input_grads

    parts, tall = 2, 16
    size = pad // parts
    plan = [[(0, 0), (1, 0)], [(0, 1), (1, 1), (0, 2), (1, 2), (0, 3), (1, 3), (0, 4), (1, 4)]]
    sections = [chain(n * size, size, tall) for n in range(parts)]
    for at, group in enumerate(plan):

        @pl.when(step >= 0)
        def _():
            for p, n in group:
                sections[p][n]()

        if at == 0:

            @pl.when(step == 0)
            def _():
                for c in loads():
                    c.wait()
                wb[...] = wb[...] * bf16(0.5)

    ga = low_grad[...]
    d = nt(ga, wo_ref[...]).astype(bf16)
    d_ref[0] = d
    dot_ref[0, :, :pad] = d.T
    acc[...] += nn(mt_ref[0, :, :pad], ga)

    @pl.when(step == pl.num_programs(0) - 1)
    def _():
        n = width // planes
        size = n // INNER
        outs = (o0_ref, o1_ref)
        peers = [(half, hi) for half in range(2) for hi in range(INNER // 2)]
        for m, (at, cut) in enumerate(((0, cut_in), (cut_in, cut_back))):
            for s, cs in enumerate(chunks):
                piece = tn(low[...], pre_grad[:, cs]) if m == 0 else tn(act[:, cs], grad[...])
                turn[m] = piece.astype(bf16) if m == 0 else (0.5 * piece).astype(bf16)
                for half, hi in peers:
                    start = pl.multiple_of(slot_of(half, hi) * cut, cut)
                    outs[half][hi, s, at : at + cut, :] = turn[m, pl.ds(start, cut), :]
        at = cut_in + cut_back
        totals = jnp.sum(col[...], 1)
        bins = jnp.sum(binv[...], 0, keepdims=True)
        for s, cs in enumerate(chunks):
            plane = lax.rem(at_ref[1] + planes - s, planes)
            mine = jnp.zeros((8, n), f32)
            for p in range(planes):
                mine = jnp.where(plane == p, totals[:, n * p : n * p + n], mine)
            mine = jnp.concatenate([mine, jnp.zeros((8, width - n), f32)], 1)
            mine = jnp.where(lax.broadcasted_iota(jnp.int32, mine.shape, 0) == 6, bins[:, cs], mine)
            for half, hi in peers:
                slot = slot_of(half, hi)
                start = pl.multiple_of(plane * n + slot * size, size)
                outs[half][hi, s, at : at + size, :] = acc[pl.ds(start, size), :].astype(bf16)
                outs[half][hi, s, at + size :, :] = vector_rows(mine, slot, 16).astype(bf16)


def ffn(at, so, cotangent, mt, vec, wo, bi, bias_far, wi, wb, far):
    spans, pad, width = so.shape
    rows = cotangent.shape[1]
    own = wb.shape[0]
    planes = far[0].shape[0] + 1
    hidden = own * planes
    spec = lambda a, b: pl.BlockSpec((1, a, b), lambda i, *_: (i, 0, 0))
    st = lambda a, b, t: shape((spans, a, b), t)
    half = (INNER // 2, planes, (width + own) // INNER + width // (planes * INNER) + 16, width)
    out = pl.BlockSpec(half, lambda i, *_: (0, 0, 0, 0), pipeline_mode=pl.Buffered(1))
    total = spans * pad
    vmem = pltpu.VMEM
    return pl.pallas_call(
        functools.partial(ffn_body, rows, len(far), planes),
        grid_spec=pltpu.PrefetchScalarGridSpec(
            num_scalar_prefetch=1,
            grid=(spans,),
            in_specs=[spec(pad, width), spec(rows, width), spec(width, lanes(pad))] + [whole(w) for w in (vec, wo, bi, bias_far)]
            + [ANY] * (2 + len(far)),
            out_specs=[spec(rows, width), spec(pad, width), spec(pad, width), spec(width, lanes(pad)), out, out],
            scratch_shapes=[vmem((8, 8, width), f32), vmem((8, hidden), f32), vmem((width, hidden), bf16), vmem((hidden, width), bf16),
                            vmem((pad, width), f32), vmem((pad, width), f32), vmem((pad, 128), f32),
                            vmem((total, hidden), bf16), vmem((total, hidden), bf16), vmem((total, width), bf16),
                            vmem((total, width), bf16), vmem((width, width), f32), vmem((2, width, width), bf16),
                            vmem((pad, width), bf16),
                            pltpu.SemaphoreType.DMA((2 + 2 * len(far) * (planes - 1),))],
        ),
        out_shape=[st(rows, width, bf16), st(pad, width, f32), st(pad, width, bf16), st(width, lanes(pad), bf16)] + [shape(half, bf16)] * 2,
        compiler_params=params(62),
        cost_estimate=cost(46),
        name="ffn",
    )(at, so, cotangent, mt, vec, wo, bi, bias_far, wi, wb, *far)


def join_body(count, *refs):
    o_ref, b_ref = refs[-2:]
    rows = o_ref.shape[1]
    for i in range(count):
        o_ref[i] = refs[i][:rows, :]
        b_ref[i : i + 1, :] = refs[i][rows:, :].astype(f32)[0:1]


def join(parts, after):
    rows, width = parts[0].shape
    return pl.pallas_call(
        functools.partial(join_body, len(parts)),
        in_specs=[pl.BlockSpec(memory_space=pltpu.VMEM)] * len(parts) + [ANY] * len(after),
        out_specs=[pl.BlockSpec(memory_space=pltpu.VMEM)] * 2,
        out_shape=[shape((len(parts), rows - 16, width), bf16), shape((len(parts), width), f32)],
        compiler_params=params(),
        cost_estimate=cost(1),
        name="join",
    )(*parts, *after)


def add(*refs):
    total = refs[0][...].astype(f32)
    for ref in refs[1:]:
        total = total + ref[...].astype(f32)
    return total.astype(bf16)


def core_sum_body(pairs, skip, *refs):
    outs = refs[2 * pairs + skip :]
    for p, o_ref in enumerate(outs):
        o_ref[...] = jnp.concatenate([add(refs[2 * i].at[p], refs[2 * i + 1].at[p]) for i in range(pairs)], 1)


def core_sum(pairs, after, name):
    peers, planes, _, width = pairs[0][0].shape
    rows = sum(a.shape[2] for a, _ in pairs)
    flat = [a for pair in pairs for a in pair]
    return pl.pallas_call(
        functools.partial(core_sum_body, len(pairs), len(after)),
        grid=(planes,),
        in_specs=[pl.BlockSpec((peers, 1) + a.shape[2:], lambda i: (0, i, 0, 0)) for a in flat] + [ANY] * len(after),
        out_specs=[pl.BlockSpec((1, rows, width), lambda i: (i, 0, 0))] * peers,
        out_shape=[shape((planes, rows, width), bf16)] * peers,
        compiler_params=params(),
        cost_estimate=cost(0.001),
        name=name,
    )(*flat, *after)


def plane_sum_body(count, skip, *refs):
    outs = refs[count + skip :]
    for s, o_ref in enumerate(outs):
        o_ref[...] = add(*(ref.at[s] for ref in refs[:count]))


def plane_sum(parts, after, name):
    planes, rows, width = parts[0].shape
    return pl.pallas_call(
        functools.partial(plane_sum_body, len(parts), len(after)),
        in_specs=[pl.BlockSpec(memory_space=pltpu.VMEM)] * len(parts) + [ANY] * len(after),
        out_specs=[pl.BlockSpec(memory_space=pltpu.VMEM)] * planes,
        out_shape=[shape((rows, width), bf16)] * planes,
        compiler_params=params(),
        cost_estimate=cost(0.001),
        name=name,
    )(*parts, *after)


def last_sum_body(count, groups, skip, *refs):
    o_ref = refs[count * groups + skip]
    at = 0
    for g in range(groups):
        total = add(*refs[count * g : count * g + count])
        o_ref[at : at + total.shape[0], :] = total
        at += total.shape[0]


def last_sum(groups, after, name):
    flat = [a for group in groups for a in group]
    rows = sum(group[0].shape[0] for group in groups)
    return pl.pallas_call(
        functools.partial(last_sum_body, len(groups[0]), len(groups), len(after)),
        in_specs=[pl.BlockSpec(memory_space=pltpu.VMEM)] * len(flat) + [ANY] * len(after),
        out_specs=pl.BlockSpec(memory_space=pltpu.VMEM),
        out_shape=shape((rows, flat[0].shape[1]), bf16),
        compiler_params=params(),
        cost_estimate=cost(0.001),
        name=name,
    )(*flat, *after)


def back_body(rows, planes, group, skip, at_ref, x_ref, qt_ref, q_ref, k_ref, v_ref, mt_ref, dt_ref, d_ref, lt_ref, *refs):
    dq_ref, dk_ref, dv_ref, o0_ref, o1_ref, aq, ak, av, ab, row, xp, vec, turn = refs[skip:]
    w, pad = k_ref.shape[2], k_ref.shape[1]
    width = x_ref.shape[-1]
    hs = width // HEADS
    scale = hs**-0.5
    main = rows // 128 * 128
    left = pad - main
    heads = w // hs
    top = rows // 16 * 16
    step = pl.program_id(0)

    @pl.when(step == 0)
    def _():
        for a in (aq, ak, av, ab, row):
            a[...] = jnp.zeros_like(a)
        xp[top:, :] = jnp.zeros((pad - top, width), bf16)

    xp[:rows, :] = x_ref[0]
    k = k_ref[0]
    kt = k.T
    v = v_ref[0]
    valid = lax.broadcasted_iota(jnp.int32, (pad - top, 1), 0) < rows - top

    def core(ks, qs, vs, ds, ls, ms):
        delta = jnp.sum(ds.astype(f32) * ms.astype(f32), 0, keepdims=True)
        st = nn(ks, qs)
        st = jnp.concatenate([st[:top], jnp.where(valid, st[top:], NEG)], 0)
        p = jnp.exp2(st - ls)
        gsc = (p * (nn(vs, ds) - delta)).astype(bf16)
        return p.astype(bf16), gsc

    def own_block(shape, rows_per, lanes_per):
        return (lax.broadcasted_iota(jnp.int32, shape, 0) // rows_per
                == lax.broadcasted_iota(jnp.int32, shape, 1) // lanes_per)

    flat = own_block((w, 128), hs, left)
    tall = own_block((128, w), left, hs)
    tile = lambda a: jnp.where(flat, jnp.concatenate([a] * heads, 1), 0).astype(bf16)
    pile = lambda a: jnp.where(tall, jnp.concatenate([a] * heads, 0), 0).astype(bf16)
    ql, dl, ml = (tile(ref[0, :, main:pad]) for ref in (qt_ref, dt_ref, mt_ref))
    ll = jnp.concatenate([lt_ref[0, 0, h : h + 1, main:pad] for h in range(heads)], 1)
    p, gsc = core(k, ql, v, dl, ll, ml)
    dv_left = nn(p, pile(d_ref[0, main:pad, :]))
    dk_left = nn(gsc, pile(q_ref[0, main:pad, :]))
    dq_left = nn(kt, gsc)
    even = lax.broadcasted_iota(jnp.int32, (pad, 2 * hs), 1) < hs
    for pair in range(heads // 2):
        both = slice(2 * hs * pair, 2 * hs * pair + 2 * hs)
        q, d = q_ref[0, :main, both], d_ref[0, :main, both]
        dk, dv = [], []
        for h in (2 * pair, 2 * pair + 1):
            c = slice(hs * h, hs * h + hs)
            p, gsc = core(k[:, c], qt_ref[0, c, :main], v[:, c], dt_ref[0, c, :main], lt_ref[0, 0, h : h + 1, :main], mt_ref[0, c, :main])
            dv.append(nn(p, d))
            dk.append(nn(gsc, q))
            dq_ref[0, c, :main] = (nn(kt[c], gsc) * scale).astype(bf16)
            dq_ref[0, c, main:pad] = (dq_left[c, left * h : left * h + left] * scale).astype(bf16)
        dv = jnp.where(even, *dv) + dv_left[:, both]
        row[:, both] += fold(dv)
        dv_ref[0, :, both] = dv.astype(bf16)
        dk_ref[0, :, both] = ((jnp.where(even, *dk) + dk_left[:, both]) * (1.0 / LOG2E)).astype(bf16)
    x = xp[...]
    aq[...] += nn(dq_ref[0, :, :pad], x)
    ak[...] += tn(dk_ref[0], x)
    av[...] += tn(dv_ref[0], x)
    ab[:, 0:1] += jnp.sum(dq_ref[0, :, :pad].astype(f32), 1, keepdims=True)

    @pl.when(step == pl.num_programs(0) - 1)
    def _():
        size = width // (planes * INNER)
        n = width // planes
        vec[...] = jnp.zeros_like(vec)
        vec[0:1, group * w : group * w + w] = ab[...].T[0:1]
        vec[1:2, group * w : group * w + w] = jnp.sum(row[...], 0, keepdims=True)
        for i, a in enumerate((aq, ak, av)):
            turn[i] = a[...].T
        for half, o_ref in enumerate((o0_ref, o1_ref)):
            for hi in range(INNER // 2):
                for s in range(planes):
                    peer = half + 2 * hi
                    plane = lax.rem(at_ref[1] + planes - s, planes)
                    start = pl.multiple_of(plane * n + (at_ref[0] ^ peer) * size, size)
                    for i in range(3):
                        r, c = size * (i // 2), w * (i % 2)
                        o_ref[hi, s, r : r + size, c : c + w] = turn[i, pl.ds(start, size), :].astype(bf16)
                    mine = vec[:, pl.ds(pl.multiple_of(plane * n, n), n)]
                    mine = jnp.concatenate([vector_rows(mine, at_ref[0] ^ peer, size), jnp.zeros((size, w - n), f32)], 1)
                    o_ref[hi, s, size:, w:] = mine.astype(bf16)


def back(at, sequence, qt, q, k, v, mt, dt, d, lt, group, planes, after=()):
    spans, rows, width = sequence.shape
    pad = k.shape[1]
    wide = qt.shape[2]
    w = width // GROUPS
    tr = pl.BlockSpec((1, w, wide), lambda i, *_: (i, group, 0))
    nat = pl.BlockSpec((1, pad, w), lambda i, *_: (i, 0, group))
    grad = pl.BlockSpec((1, w, wide), lambda i, *_: (i, 0, 0))
    nat_grad = pl.BlockSpec((1, pad, w), lambda i, *_: (i, 0, 0))
    half = (INNER // 2, planes, 2 * width // (planes * INNER), 2 * w)
    out = pl.BlockSpec(half, lambda i, *_: (0, 0, 0, 0))
    return pl.pallas_call(
        functools.partial(back_body, rows, planes, group, len(after)),
        grid_spec=pltpu.PrefetchScalarGridSpec(
            num_scalar_prefetch=1,
            grid=(spans,),
            in_specs=[pl.BlockSpec((1, rows, width), lambda i, *_: (i, 0, 0)), tr, nat, nat, nat, tr, tr, nat,
                      pl.BlockSpec((1, 1, HEADS // GROUPS, wide), lambda i, *_: (i, group, 0, 0))] + [ANY] * len(after),
            out_specs=[grad, nat_grad, nat_grad] + [out] * 2,
            scratch_shapes=[pltpu.VMEM((w, width), f32)] * 3
            + [pltpu.VMEM((w, 8), f32), pltpu.VMEM((8, w), f32), pltpu.VMEM((pad, width), bf16), pltpu.VMEM((8, width), f32),
               pltpu.VMEM((3, width, w), f32)],
        ),
        out_shape=[shape((spans, w, wide), bf16)] + [shape((spans, pad, w), bf16)] * 2 + [shape(half, bf16)] * 2,
        compiler_params=params(),
        cost_estimate=cost(21),
        name=f"back{group}",
    )(at, sequence, qt, q, k, v, mt, dt, d, lt, *after)


def input_body(rows, groups, skip, *refs):
    refs = refs[skip:]
    gs_ref = refs[0]
    parts = refs[1 : 1 + 3 * groups]
    ws = refs[1 + 3 * groups : 4 + 3 * groups]
    out_ref = refs[4 + 3 * groups]
    wt = refs[5 + 3 * groups :]

    @pl.when(pl.program_id(0) == 0)
    def _():
        wt[0][...] = ws[0][...].T

    total = gs_ref[0]
    for g in range(groups):
        dq, dk, dv = (ref[0] for ref in parts[3 * g : 3 * g + 3])
        cols = slice(dq.shape[0] * g, dq.shape[0] * g + dq.shape[0])
        total = total + tn(dq[:, : total.shape[0]], wt[0][cols, :])
        total = total + nt(dk, ws[1][:, cols])
        total = total + nt(dv, ws[2][:, cols])
    out_ref[0] = total[:rows]


def input_grad(rows, gs, parts, wq, wk, wv, after=()):
    spans, pad, width = gs.shape
    flat = [a for part in parts for a in part]
    spec = lambda a: pl.BlockSpec((1,) + a.shape[1:], lambda i: (i, 0, 0))
    return pl.pallas_call(
        functools.partial(input_body, rows, len(parts), len(after)),
        grid=(spans,),
        in_specs=[ANY] * len(after) + [spec(gs)] + [spec(a) for a in flat] + [whole(w) for w in (wq, wk, wv)],
        out_specs=pl.BlockSpec((1, rows, width), lambda i: (i, 0, 0)),
        out_shape=shape((spans, rows, width), f32),
        scratch_shapes=[pltpu.VMEM((width, width), bf16)],
        compiler_params=params(),
        cost_estimate=cost(10),
        name="input_grad",
    )(*after, gs, *flat, wq, wk, wv)


def final_body(cut_in, cut_back, at_ref, *refs):
    pieces = refs[:INNER]
    wi_ref, wb_ref, wo_ref, wq_ref, wk_ref, wv_ref, bin_ref, *vec_refs = refs[INNER:]
    n, width = wo_ref.shape
    size = n // INNER
    w = width // GROUPS
    for q in range(INNER):
        slot = at_ref[0] ^ (q // (INNER // 2) + 2 * (q % (INNER // 2)))
        small = pl.ds(pl.multiple_of(slot * size, size), size)
        p = pieces[q]
        wi_ref[pl.ds(pl.multiple_of(slot * cut_in, cut_in), cut_in), :] = p[:cut_in, :].astype(f32)
        at = cut_in
        wb_ref[pl.ds(pl.multiple_of(slot * cut_back, cut_back), cut_back), :] = p[at : at + cut_back, :].astype(f32)
        at += cut_back
        wo_ref[small, :] = p[at : at + size, :].astype(f32)
        at += size
        tail = p[at : at + 16, :].astype(f32)[0:1]
        at += 16
        pair = jnp.zeros((1, n), f32)
        for g in range(GROUPS):
            for i, o_ref in enumerate((wq_ref, wk_ref, wv_ref)):
                r, c = at + size * (i // 2), w * (i % 2)
                o_ref[small, w * g : w * g + w] = p[r : r + size, c : c + w].astype(f32)
            pair = pair + p[at + size : at + 2 * size, w : w + n].astype(f32)[0:1]
            at += 2 * size
        for i, v_ref in enumerate(vec_refs):

            @pl.when(slot == i % 6)
            def _():
                v_ref[...] = tail[:, :n] if i < 6 else pair

        @pl.when(slot == 6)
        def _():
            bin_ref[...] = tail


def final(at, pieces, own, planes):
    width = pieces[0].shape[1]
    n = width // planes
    out = [(width, own), (own, width)] + [(n, width)] * 4 + [(1, own)] + [(1, n)] * 8
    return pl.pallas_call(
        functools.partial(final_body, width // INNER, own // INNER),
        grid_spec=pltpu.PrefetchScalarGridSpec(
            num_scalar_prefetch=1,
            grid=(1,),
            in_specs=[whole(a) for a in pieces],
            out_specs=[pl.BlockSpec(d, lambda *_: (0, 0)) for d in out],
        ),
        out_shape=[shape(d, f32) for d in out],
        compiler_params=params(),
        cost_estimate=cost(3),
        name="final",
    )(at, *pieces)


def shards(dp, planes, sequence, cotangent, w_query, b_query, w_key, w_value, b_value, w_out, b_out, gain_attn, shift_attn,
           w_in, b_in, w_back, b_back, gain_ffn, shift_ffn):
    spans, rows, width = sequence.shape
    own = w_in.shape[1]
    at = jnp.stack([lax.axis_index("dp") & (INNER - 1), lax.axis_index("mp")]).astype(jnp.int32)

    def swap(a, k):
        return lax.ppermute(a, "dp", [(i, i ^ k) for i in range(dp)])

    def turn(a, s):
        return lax.ppermute(a, "mp", [(i, (i + s) % planes) for i in range(planes)])

    def spread(a, after=()):
        far = [a] + [swap(a, 2 * k) for k in range(1, INNER // 2)]
        far = lax.optimization_barrier((*far, *after))[: INNER // 2]
        return list(far) + [swap(b, 1) for b in far]

    def from_plane(parts):
        return [parts[0]] + [swap(parts[k], 2 * k) for k in range(1, INNER // 2)]

    def outer(totals):
        totals = list(totals)
        step = INNER
        while step < dp:
            totals = [(t.astype(f32) + swap(t, step).astype(f32)).astype(bf16) for t in totals]
            step *= 2
        return totals

    def to_planes(totals):
        return [totals[0]] + [turn(totals[s], -s) for s in range(1, planes)]

    piece = prep(at, w_in, w_back, b_in)
    far = [turn(piece, s) for s in range(1, planes)]
    vec = stack_vectors((b_query, b_value, b_out, b_back, gain_attn, shift_attn, gain_ffn, shift_ffn), (piece,))
    common = (sequence, w_query, w_key, w_value, w_out, vec)
    head = 1
    first = attend(*common, 0, head)
    far, bias_far = join(far, first[:1])
    qt, k, v, mt, lt, so, q = attend(*common, head, spans - head, first, (far,))
    far = spread(far, (so,))
    layer_out, gs, d, dt, keep, send = ffn(at, so, cotangent, mt, vec, w_out, b_in, bias_far, w_in, w_back, far)
    *grad0, keep0, send0 = back(at, sequence, qt, q, k, v, mt, dt, d, lt, 0, planes)
    got0 = swap(send0, 1)
    ffn_parts = core_sum([(keep, swap(send, 1))], (keep0,), "core_ffn")
    *grad1, keep1, send1 = back(at, sequence, qt, q, k, v, mt, dt, d, lt, 1, planes, (ffn_parts[0], got0))
    ffn_parts = from_plane(ffn_parts)
    parts = core_sum([(keep0, got0), (keep1, swap(send1, 1))], ffn_parts[1:], "core_attn")
    ffn_totals = to_planes(outer(plane_sum(ffn_parts, (parts[0],), "plane_ffn")))
    by_input = input_grad(rows, gs, [grad0, grad1], w_query, w_key, w_value, (ffn_totals[0],))
    totals = to_planes(outer(plane_sum(from_plane(parts), (by_input,), "plane_attn")))
    layer_out, by_input = lax.optimization_barrier((layer_out, by_input, totals[0]))[:2]
    layer_out, by_input = (lax.optimization_barrier(jnp.transpose(a, (1, 0, 2))) for a in (layer_out, by_input))
    pieces = spread(last_sum([ffn_totals, totals], (by_input, layer_out), "last"))
    wi, wb, wo, wq, wk, wv, bins, gg2, gs2, bb, gg1, gs1, bo, bq, bv = final(at, pieces, own, planes)
    row = lambda a: a.reshape(-1)
    layer_out, by_input = (jnp.transpose(a, (1, 0, 2)) for a in (layer_out, by_input))
    return (layer_out, by_input, wq, row(bq), wk, wv, row(bv), wo, row(bo), row(gg1), row(gs1), wi, row(bins), wb,
            row(bb), row(gg2), row(gs2))


def solution(mesh):
    spans, vector = P(("dp", "mp"), None, None), P("mp")
    return jax.shard_map(
        functools.partial(shards, mesh.shape["dp"], mesh.shape["mp"]),
        mesh=mesh,
        in_specs=(spans, spans) + (P(),) * 9 + (P(None, "mp"), vector, P("mp", None)) + (P(),) * 3,
        out_specs=(spans, spans, P("mp", None), vector, P("mp", None), P("mp", None), vector, P("mp", None), vector, vector, vector,
                   P(None, "mp"), vector, P("mp", None), vector, vector, vector),
        check_vma=False,
    )
```

```python
import functools

import jax
import jax.numpy as jnp
from jax import lax
from jax.experimental import pallas as pl
from jax.experimental.pallas import tpu as pltpu
from jax.sharding import PartitionSpec as P

HEADS = 8
GROUPS = 2
INNER = 8
NEG = -1e30
C0 = (2.0 / 3.141592653589793) ** 0.5
C1 = C0 * 0.044715
LOG2E = 1.4426950408889634
f32 = jnp.float32
bf16 = jnp.bfloat16


def dot(left, right, a, b):
    return lax.dot_general(left, right, (((a,), (b,)), ((), ())), preferred_element_type=f32)


def nn(left, right):
    return dot(left, right, 1, 0)


def nt(left, right):
    return dot(left, right, 1, 1)


def tn(left, right):
    return dot(left, right, 0, 0)


def fold(v):
    return jnp.sum(v.reshape(v.shape[0] // 8, 8, v.shape[1]), 0)


def row_mean(v):
    return jnp.mean(v, -1, keepdims=True)


def lanes(n):
    return (n + 127) // 128 * 128


def cost(us):
    return pl.CostEstimate(flops=int(us * 1e9), bytes_accessed=int(us * 1e5), transcendentals=0)


def params(mib=60):
    return pltpu.CompilerParams(vmem_limit_bytes=mib * 2**20)


def whole(a):
    return pl.BlockSpec(a.shape, lambda *_: (0,) * len(a.shape), pipeline_mode=pl.Buffered(1))


ANY = pl.BlockSpec(memory_space=pl.ANY)


def shape(dims, dtype):
    return jax.ShapeDtypeStruct(tuple(dims), dtype)


def prep_body(at_ref, wi_ref, wb_ref, bi_ref, piece_ref):
    a, b = wi_ref.shape[0], wb_ref.shape[0]
    piece_ref[:a, :] = wi_ref[...]
    piece_ref[a : a + b, :] = wb_ref[...]
    bias = bi_ref[...].astype(f32).reshape(1, -1)
    piece_ref[a + b :, :] = jnp.concatenate([bias, jnp.zeros((15, bias.shape[1]), f32)], 0).astype(bf16)


def prep(at, wi, wb, bi):
    width, own = wi.shape
    a, b = width // INNER, own // INNER
    return pl.pallas_call(
        prep_body,
        grid_spec=pltpu.PrefetchScalarGridSpec(
            num_scalar_prefetch=1,
            grid=(1,),
            in_specs=[pl.BlockSpec((a, own), lambda i, at: (at[0], 0)), pl.BlockSpec((b, width), lambda i, at: (at[0], 0)), whole(bi)],
            out_specs=pl.BlockSpec((a + b + 16, width), lambda *_: (0, 0)),
        ),
        out_shape=shape((a + b + 16, width), bf16),
        compiler_params=params(),
        cost_estimate=cost(2),
        name="prep",
    )(at, wi, wb, bi)


def vectors_body(*refs):
    for j, v in enumerate(refs[:8]):
        refs[-1][j : j + 1, :] = v[...].astype(f32).reshape(1, -1)


def stack_vectors(vectors, after):
    return pl.pallas_call(
        vectors_body,
        in_specs=[pl.BlockSpec(memory_space=pltpu.VMEM)] * 8 + [ANY] * len(after),
        out_specs=pl.BlockSpec(memory_space=pltpu.VMEM),
        out_shape=shape((8, vectors[0].shape[0]), f32),
        cost_estimate=cost(1),
        name="vectors",
    )(*vectors, *after)


def attend_body(rows, pad, skip, x_ref, wq_ref, wk_ref, wv_ref, wo_ref, vec_ref, *refs):
    qt_ref, k_ref, v_ref, mt_ref, lt_ref, so_ref, q_ref, xp, vt = refs[skip:]
    width = x_ref.shape[-1]
    hs = width // HEADS
    main = rows // 128 * 128
    left = pad - main
    group = 128 // left
    top = rows // 16 * 16

    @pl.when(pl.program_id(0) == 0)
    def _():
        xp[top:, :] = jnp.zeros((pad - top, width), bf16)

    xp[:rows, :] = x_ref[0]
    x = xp[...]
    scale = hs**-0.5
    q = ((nn(x, wq_ref[...]) + vec_ref[0:1, :]) * (scale * LOG2E)).astype(bf16)
    q_ref[0] = q
    qt_ref[0, :, :pad] = q.T
    k_ref[0] = nn(x, wk_ref[...]).astype(bf16)
    v = (nn(x, wv_ref[...]) + vec_ref[1:2, :]).astype(bf16)
    v_ref[0] = v
    vt[...] = v.T
    valid = lax.broadcasted_iota(jnp.int32, (pad - top, 1), 0) < rows - top
    ones = jnp.ones((16, pad), bf16)

    def soft(st):
        s_top = st[:top]
        s_bot = jnp.where(valid, st[top:], NEG)
        m = jnp.maximum(jnp.max(s_top, 0, keepdims=True), jnp.max(s_bot, 0, keepdims=True))
        p = jnp.concatenate([jnp.exp2(s_top - m).astype(bf16), jnp.exp2(s_bot - m).astype(bf16)], 0)
        return m, p

    cs = [slice(hs * h, hs * h + hs) for h in range(HEADS)]
    following = nn(k_ref[0, :, cs[0]], qt_ref[0, cs[0], :main])
    for h in range(HEADS):
        c = cs[h]
        st = following
        if h + 1 < HEADS:
            following = nn(k_ref[0, :, cs[h + 1]], qt_ref[0, cs[h + 1], :main])
        m, p = soft(st)
        ot = nn(jnp.concatenate([vt[c, :], ones], 0), p)
        total = ot[hs : hs + 1]
        mt_ref[0, c, :main] = (ot[:hs] * (1.0 / total)).astype(bf16)
        lt_ref[0, h // (HEADS // GROUPS), h % (HEADS // GROUPS) : h % (HEADS // GROUPS) + 1, :main] = m + jnp.log2(total)
    for g in range(HEADS // group):
        w = hs * group
        c = slice(w * g, w * g + w)
        same = (lax.broadcasted_iota(jnp.int32, (w, 128), 0) // hs
                == lax.broadcasted_iota(jnp.int32, (w, 128), 1) // left)
        ql = jnp.where(same, jnp.concatenate([qt_ref[0, c, main:pad]] * group, 1), 0).astype(bf16)
        m, p = soft(nn(k_ref[0, :, c], ql))
        ot = nn(jnp.concatenate([vt[c, :], ones], 0), p)
        total = ot[w : w + 1]
        o = ot[:w] * (1.0 / total)
        lt = m + jnp.log2(total)
        for j in range(group):
            h = g * group + j
            mt_ref[0, hs * h : hs * h + hs, main:pad] = o[hs * j : hs * j + hs, left * j : left * j + left].astype(bf16)
            lt_ref[0, h // (HEADS // GROUPS), h % (HEADS // GROUPS) : h % (HEADS // GROUPS) + 1, main:pad] = lt[:, left * j : left * j + left]
    so_ref[0] = tn(mt_ref[0, :, :pad], wo_ref[...]) + vec_ref[2:3, :] + xp[...].astype(f32)


def attend(sequence, wq, wk, wv, wo, vec, first, count, before=(), after=()):
    spans, rows, width = sequence.shape
    pad = (rows + 31) // 32 * 32
    wide = lanes(pad)
    per = HEADS // GROUPS
    spec = lambda a, b: pl.BlockSpec((1, a, b), lambda i: (i + first, 0, 0))
    return pl.pallas_call(
        functools.partial(attend_body, rows, pad, len(before) + len(after)),
        grid=(count,),
        in_specs=[spec(rows, width)] + [whole(w) for w in (wq, wk, wv, wo, vec)] + [ANY] * (len(before) + len(after)),
        out_specs=[spec(width, wide), spec(pad, width), spec(pad, width), spec(width, wide),
                   pl.BlockSpec((1, GROUPS, per, wide), lambda i: (i + first, 0, 0, 0)), spec(pad, width), spec(pad, width)],
        out_shape=[shape((spans, width, wide), bf16), shape((spans, pad, width), bf16), shape((spans, pad, width), bf16),
                   shape((spans, width, wide), bf16), shape((spans, GROUPS, per, wide), f32), shape((spans, pad, width), f32),
                   shape((spans, pad, width), bf16)],
        scratch_shapes=[pltpu.VMEM((pad, width), bf16), pltpu.VMEM((width, pad), bf16)],
        input_output_aliases={6 + n: n for n in range(len(before))},
        compiler_params=params(),
        cost_estimate=cost(16),
        name=f"attend{first}",
    )(sequence, wq, wk, wv, wo, vec, *before, *after)


def vector_rows(vec, slot, count):
    mine = lax.broadcasted_iota(jnp.int32, vec.shape, 0) == slot
    row = jnp.sum(jnp.where(mine, vec, 0.0), 0, keepdims=True)
    return jnp.concatenate([row, jnp.zeros((count - 1, vec.shape[1]), f32)], 0)


def ffn_body(rows, slices, planes, at_ref, so_ref, ct_ref, mt_ref, vec_ref, wo_ref, bi_ref, bf_ref, wi_ref, wb_ref, *refs):
    (lo_ref, gs_ref, d_ref, dot_ref, o0_ref, o1_ref, side_ref,
     col, binv, wi, wb, one, two, inv1, act, pre_grad, low, grad, acc, turn, low_grad, sem) = refs[slices:]
    pad, width = so_ref.shape[1:]
    own = wb_ref.shape[0]
    hidden = wb.shape[0]
    cut_in, cut_back = width // INNER, own // INNER
    step = pl.program_id(0)

    def slot_of(half, hi):
        return at_ref[0] ^ (half + 2 * hi)

    def loads():
        copies = [pltpu.make_async_copy(wi_ref, wi.at[:, :own], sem.at[0]),
                  pltpu.make_async_copy(wb_ref, wb.at[:own, :], sem.at[1])]
        for q in range(slices):
            slot = slot_of(q // (INNER // 2), q % (INNER // 2))
            for s in range(1, planes):
                n = 2 + 2 * (q * (planes - 1) + s - 1)
                there = wi.at[pl.ds(pl.multiple_of(slot * cut_in, cut_in), cut_in), own * s : own * s + own]
                copies.append(pltpu.make_async_copy(refs[q].at[s - 1, :cut_in, :], there, sem.at[n]))
                there = wb.at[pl.ds(pl.multiple_of(own * s + slot * cut_back, cut_back), cut_back), :]
                copies.append(pltpu.make_async_copy(refs[q].at[s - 1, cut_in : cut_in + cut_back, :], there, sem.at[n + 1]))
        return copies

    @pl.when(step == 0)
    def _():
        for c in loads():
            c.start()
        col[...] = jnp.zeros_like(col)
        binv[...] = jnp.zeros_like(binv)
        acc[...] = jnp.zeros_like(acc)

    bb, g1, s1, g2, s2 = (vec_ref[n : n + 1, :] for n in range(3, 8))
    base = pl.multiple_of(step * pad, pad)
    unit = own
    chunks = [slice(n, n + unit) for n in range(0, hidden, unit)]
    bias = [bi_ref[...].astype(f32).reshape(1, -1)] + [bf_ref[s : s + 1, :] for s in range(planes - 1)]
    zero = [jnp.zeros((8, width), f32)] * 3

    def chain(first, size, tall):
        here = pl.ds(pl.multiple_of(base + first, 16), size)
        blocks = [slice(first + n, first + n + tall) for n in range(0, size, tall)]
        local = lambda b: slice(b.start - first, b.stop - first)
        there = lambda b: pl.ds(pl.multiple_of(base + b.start, 16), tall)

        def norm():
            for b in blocks:
                r = so_ref[0, b, :]
                c = r - row_mean(r)
                inv = lax.rsqrt(row_mean(c * c) + 1e-5)
                unit1 = c * inv
                one[b, :] = unit1
                inv1[b, :] = jnp.broadcast_to(inv, (tall, 128))
                low[there(b), :] = (unit1 * g1 + s1).astype(bf16)

        def hidden_units():
            nl = low[here, :]
            for cs, add_bias in zip(chunks, bias):
                pre = nn(nl, wi[:, cs])
                for b in blocks:
                    v = (pre[local(b)] + add_bias).astype(bf16)
                    cube = (v * v) * bf16(C1)
                    t = jnp.tanh(v * (cube + bf16(C0)))
                    double = v * (bf16(1.0) + t)
                    act[there(b), cs] = double
                    slope = cube * bf16(3.0) + bf16(C0)
                    pre_grad[there(b), cs] = (bf16(1.0) + t) + double * ((bf16(1.0) - t) * slope)

        def output():
            out = nn(act[here, :], wb[...])
            sums = zero
            for b in blocks:
                r = out[local(b)] + (one[b, :] * g1 + (s1 + bb))
                c = r - row_mean(r)
                inv = lax.rsqrt(row_mean(c * c) + 1e-5)
                unit2 = c * inv
                last = min(b.stop, rows)
                lo_ref[0, b.start : last, :] = (unit2 * g2 + s2)[: last - b.start].astype(bf16)
                up = ct_ref[0, b.start : last, :].astype(f32)
                if last < b.stop:
                    up = jnp.concatenate([up, jnp.zeros((b.stop - last, width), f32)], 0)
                gu = up * g2
                back = inv * (gu - row_mean(gu) - unit2 * row_mean(gu * unit2))
                two[b, :] = back
                grad[there(b), :] = back.astype(bf16)
                sums = [a + fold(v) for a, v in zip(sums, (up * unit2, up, back))]
            for n in range(3):
                col[n] += sums[n]

        def hidden_grads():
            f = grad[here, :]
            for cs in chunks:
                da = nt(f, wb[cs, :])
                total = jnp.zeros((8, unit), f32)
                for b in blocks:
                    g = da[local(b)] * pre_grad[there(b), cs].astype(f32)
                    total = total + fold(g)
                    pre_grad[there(b), cs] = g.astype(bf16)
                binv[:, cs] += total

        def input_grads():
            out = nt(pre_grad[here, :], wi[...])
            sums = zero
            for b in blocks:
                dn = out[local(b)] + two[b, :]
                unit1 = one[b, :]
                gu = dn * g1
                back = inv1[b, 0:1] * (gu - row_mean(gu) - unit1 * row_mean(gu * unit1))
                gs_ref[0, b, :] = back
                low_grad[b, :] = back.astype(bf16)
                sums = [a + fold(v) for a, v in zip(sums, (dn * unit1, dn, back))]
            for n in range(3):
                col[3 + n] += sums[n]

        return norm, hidden_units, output, hidden_grads, input_grads

    parts, tall = 2, 16
    size = pad // parts
    plan = [[(0, 0), (1, 0)], [(0, 1), (1, 1), (0, 2), (1, 2), (0, 3), (1, 3), (0, 4), (1, 4)]]
    sections = [chain(n * size, size, tall) for n in range(parts)]
    for at, group in enumerate(plan):

        @pl.when(step >= 0)
        def _():
            for p, n in group:
                sections[p][n]()

        if at == 0:

            @pl.when(step == 0)
            def _():
                for c in loads():
                    c.wait()
                wb[...] = wb[...] * bf16(0.5)

    ga = low_grad[...]
    d = nt(ga, wo_ref[...]).astype(bf16)
    d_ref[0] = d
    dot_ref[0, :, :pad] = d.T
    acc[...] += nn(mt_ref[0, :, :pad], ga)

    @pl.when(step == pl.num_programs(0) - 1)
    def _():
        n = width // planes
        size = n // INNER
        outs = (o0_ref, o1_ref)
        peers = [(half, hi) for half in range(2) for hi in range(INNER // 2)]
        for m, (at, cut) in enumerate(((0, cut_in), (cut_in, cut_back))):
            for s, cs in enumerate(chunks):
                piece = tn(low[...], pre_grad[:, cs]) if m == 0 else tn(act[:, cs], grad[...])
                turn[m] = piece.astype(bf16) if m == 0 else (0.5 * piece).astype(bf16)
                for half, hi in peers:
                    start = pl.multiple_of(slot_of(half, hi) * cut, cut)
                    outs[half][hi, s, at : at + cut, :] = turn[m, pl.ds(start, cut), :]
        at = cut_in + cut_back
        totals = jnp.sum(col[...], 1)
        bins = jnp.sum(binv[...], 0, keepdims=True)
        for s, cs in enumerate(chunks):
            plane = lax.rem(at_ref[1] + planes - s, planes)
            mine = jnp.zeros((8, n), f32)
            for p in range(planes):
                mine = jnp.where(plane == p, totals[:, n * p : n * p + n], mine)
            mine = jnp.concatenate([mine, jnp.zeros((8, width - n), f32)], 1)
            mine = jnp.where(lax.broadcasted_iota(jnp.int32, mine.shape, 0) == 6, bins[:, cs], mine)
            for half, hi in peers:
                slot = slot_of(half, hi)
                start = pl.multiple_of(plane * n + slot * size, size)
                outs[half][hi, s, at : at + size, :] = acc[pl.ds(start, size), :].astype(bf16)
                row = vector_rows(mine, slot, 8)
                w = width // 2
                side_ref[half, hi, s] = jnp.concatenate([row[0:1, :w], row[0:1, w:], jnp.zeros((6, w), f32)], 0)


def ffn(at, so, cotangent, mt, vec, wo, bi, bias_far, wi, wb, far):
    spans, pad, width = so.shape
    rows = cotangent.shape[1]
    own = wb.shape[0]
    planes = far[0].shape[0] + 1
    hidden = own * planes
    spec = lambda a, b: pl.BlockSpec((1, a, b), lambda i, *_: (i, 0, 0))
    st = lambda a, b, t: shape((spans, a, b), t)
    half = (INNER // 2, planes, (width + own) // INNER + width // (planes * INNER), width)
    side = (2, INNER // 2, planes, 8, width // 2)
    out = pl.BlockSpec(half, lambda i, *_: (0, 0, 0, 0), pipeline_mode=pl.Buffered(1))
    total = spans * pad
    vmem = pltpu.VMEM
    return pl.pallas_call(
        functools.partial(ffn_body, rows, len(far), planes),
        grid_spec=pltpu.PrefetchScalarGridSpec(
            num_scalar_prefetch=1,
            grid=(spans,),
            in_specs=[spec(pad, width), spec(rows, width), spec(width, lanes(pad))] + [whole(w) for w in (vec, wo, bi, bias_far)]
            + [ANY] * (2 + len(far)),
            out_specs=[spec(rows, width), spec(pad, width), spec(pad, width), spec(width, lanes(pad)), out, out,
                       pl.BlockSpec(side, lambda i, *_: (0,) * 5)],
            scratch_shapes=[vmem((8, 8, width), f32), vmem((8, hidden), f32), vmem((width, hidden), bf16), vmem((hidden, width), bf16),
                            vmem((pad, width), f32), vmem((pad, width), f32), vmem((pad, 128), f32),
                            vmem((total, hidden), bf16), vmem((total, hidden), bf16), vmem((total, width), bf16),
                            vmem((total, width), bf16), vmem((width, width), f32), vmem((2, width, width), bf16),
                            vmem((pad, width), bf16),
                            pltpu.SemaphoreType.DMA((2 + 2 * len(far) * (planes - 1),))],
        ),
        out_shape=[st(rows, width, bf16), st(pad, width, f32), st(pad, width, bf16), st(width, lanes(pad), bf16)] + [shape(half, bf16)] * 2
        + [shape(side, f32)],
        compiler_params=params(62),
        cost_estimate=cost(46),
        name="ffn",
    )(at, so, cotangent, mt, vec, wo, bi, bias_far, wi, wb, *far)


def join_body(count, *refs):
    o_ref, b_ref = refs[-2:]
    rows = o_ref.shape[1]
    for i in range(count):
        o_ref[i] = refs[i][:rows, :]
        b_ref[i : i + 1, :] = refs[i][rows:, :].astype(f32)[0:1]


def join(parts, after):
    rows, width = parts[0].shape
    return pl.pallas_call(
        functools.partial(join_body, len(parts)),
        in_specs=[pl.BlockSpec(memory_space=pltpu.VMEM)] * len(parts) + [ANY] * len(after),
        out_specs=[pl.BlockSpec(memory_space=pltpu.VMEM)] * 2,
        out_shape=[shape((len(parts), rows - 16, width), bf16), shape((len(parts), width), f32)],
        compiler_params=params(),
        cost_estimate=cost(1),
        name="join",
    )(*parts, *after)


def add(*refs):
    total = refs[0][...].astype(f32)
    for ref in refs[1:]:
        total = total + ref[...].astype(f32)
    return total.astype(bf16)


def core_sum_body(pairs, skip, *refs):
    outs = refs[2 * pairs + skip :]
    for p, o_ref in enumerate(outs):
        o_ref[...] = jnp.concatenate([add(refs[2 * i].at[p], refs[2 * i + 1].at[p]) for i in range(pairs)], 1)


def core_sum(pairs, after, name):
    peers, planes, _, width = pairs[0][0].shape
    rows = sum(a.shape[2] for a, _ in pairs)
    flat = [a for pair in pairs for a in pair]
    return pl.pallas_call(
        functools.partial(core_sum_body, len(pairs), len(after)),
        grid=(planes,),
        in_specs=[pl.BlockSpec((peers, 1) + a.shape[2:], lambda i: (0, i, 0, 0)) for a in flat] + [ANY] * len(after),
        out_specs=[pl.BlockSpec((1, rows, width), lambda i: (i, 0, 0))] * peers,
        out_shape=[shape((planes, rows, width), bf16)] * peers,
        compiler_params=params(),
        cost_estimate=cost(0.001),
        name=name,
    )(*flat, *after)


def plane_sum_body(count, skip, *refs):
    outs = refs[count + skip :]
    for s, o_ref in enumerate(outs):
        o_ref[...] = add(*(ref.at[s] for ref in refs[:count]))


def plane_sum(parts, after, name):
    planes, rows, width = parts[0].shape
    return pl.pallas_call(
        functools.partial(plane_sum_body, len(parts), len(after)),
        in_specs=[pl.BlockSpec(memory_space=pltpu.VMEM)] * len(parts) + [ANY] * len(after),
        out_specs=[pl.BlockSpec(memory_space=pltpu.VMEM)] * planes,
        out_shape=[shape((rows, width), bf16)] * planes,
        compiler_params=params(),
        cost_estimate=cost(0.001),
        name=name,
    )(*parts, *after)


def last_sum_body(count, groups, skip, *refs):
    o_ref = refs[count * groups + skip]
    at = 0
    for g in range(groups):
        total = add(*refs[count * g : count * g + count])
        o_ref[at : at + total.shape[0], :] = total
        at += total.shape[0]


def last_sum(groups, after, name):
    flat = [a for group in groups for a in group]
    rows = sum(group[0].shape[0] for group in groups)
    return pl.pallas_call(
        functools.partial(last_sum_body, len(groups[0]), len(groups), len(after)),
        in_specs=[pl.BlockSpec(memory_space=pltpu.VMEM)] * len(flat) + [ANY] * len(after),
        out_specs=pl.BlockSpec(memory_space=pltpu.VMEM),
        out_shape=shape((rows, flat[0].shape[1]), bf16),
        compiler_params=params(),
        cost_estimate=cost(0.001),
        name=name,
    )(*flat, *after)


def back_body(rows, planes, group, skip, sides, at_ref, x_ref, qt_ref, q_ref, k_ref, v_ref, mt_ref, dt_ref, d_ref, lt_ref, *refs):
    dq_ref, dk_ref, dv_ref, o0_ref, o1_ref, aq, ak, av, ab, row, xp, vec, turn = refs[sides + skip :]
    w, pad = k_ref.shape[2], k_ref.shape[1]
    width = x_ref.shape[-1]
    hs = width // HEADS
    scale = hs**-0.5
    main = rows // 128 * 128
    left = pad - main
    heads = w // hs
    top = rows // 16 * 16
    step = pl.program_id(0)

    @pl.when(step == 0)
    def _():
        for a in (aq, ak, av, ab, row):
            a[...] = jnp.zeros_like(a)
        xp[top:, :] = jnp.zeros((pad - top, width), bf16)

    xp[:rows, :] = x_ref[0]
    k = k_ref[0]
    kt = k.T
    v = v_ref[0]
    valid = lax.broadcasted_iota(jnp.int32, (pad - top, 1), 0) < rows - top

    def core(ks, qs, vs, ds, ls, ms):
        delta = jnp.sum(ds.astype(f32) * ms.astype(f32), 0, keepdims=True)
        st = nn(ks, qs)
        st = jnp.concatenate([st[:top], jnp.where(valid, st[top:], NEG)], 0)
        p = jnp.exp2(st - ls)
        gsc = (p * (nn(vs, ds) - delta)).astype(bf16)
        return p.astype(bf16), gsc

    def own_block(shape, rows_per, lanes_per):
        return (lax.broadcasted_iota(jnp.int32, shape, 0) // rows_per
                == lax.broadcasted_iota(jnp.int32, shape, 1) // lanes_per)

    flat = own_block((w, 128), hs, left)
    tall = own_block((128, w), left, hs)
    tile = lambda a: jnp.where(flat, jnp.concatenate([a] * heads, 1), 0).astype(bf16)
    pile = lambda a: jnp.where(tall, jnp.concatenate([a] * heads, 0), 0).astype(bf16)
    ql, dl, ml = (tile(ref[0, :, main:pad]) for ref in (qt_ref, dt_ref, mt_ref))
    ll = jnp.concatenate([lt_ref[0, 0, h : h + 1, main:pad] for h in range(heads)], 1)
    p, gsc = core(k, ql, v, dl, ll, ml)
    dv_left = nn(p, pile(d_ref[0, main:pad, :]))
    dk_left = nn(gsc, pile(q_ref[0, main:pad, :]))
    dq_left = nn(kt, gsc)
    even = lax.broadcasted_iota(jnp.int32, (pad, 2 * hs), 1) < hs
    for pair in range(heads // 2):
        both = slice(2 * hs * pair, 2 * hs * pair + 2 * hs)
        q, d = q_ref[0, :main, both], d_ref[0, :main, both]
        dk, dv = [], []
        for h in (2 * pair, 2 * pair + 1):
            c = slice(hs * h, hs * h + hs)
            p, gsc = core(k[:, c], qt_ref[0, c, :main], v[:, c], dt_ref[0, c, :main], lt_ref[0, 0, h : h + 1, :main], mt_ref[0, c, :main])
            dv.append(nn(p, d))
            dk.append(nn(gsc, q))
            dq_ref[0, c, :main] = (nn(kt[c], gsc) * scale).astype(bf16)
            dq_ref[0, c, main:pad] = (dq_left[c, left * h : left * h + left] * scale).astype(bf16)
        dv = jnp.where(even, *dv) + dv_left[:, both]
        row[:, both] += fold(dv)
        dv_ref[0, :, both] = dv.astype(bf16)
        dk_ref[0, :, both] = ((jnp.where(even, *dk) + dk_left[:, both]) * (1.0 / LOG2E)).astype(bf16)
    x = xp[...]
    aq[...] += nn(dq_ref[0, :, :pad], x)
    ak[...] += tn(dk_ref[0], x)
    av[...] += tn(dv_ref[0], x)
    ab[:, 0:1] += jnp.sum(dq_ref[0, :, :pad].astype(f32), 1, keepdims=True)

    @pl.when(step == pl.num_programs(0) - 1)
    def _():
        size = width // (planes * INNER)
        n = width // planes
        vec[...] = jnp.zeros_like(vec)
        vec[0:1, group * w : group * w + w] = ab[...].T[0:1]
        vec[1:2, group * w : group * w + w] = jnp.sum(row[...], 0, keepdims=True)
        for i, a in enumerate((aq, ak, av)):
            turn[i] = a[...].T
        for half, o_ref in enumerate((o0_ref, o1_ref)):
            for hi in range(INNER // 2):
                for s in range(planes):
                    peer = half + 2 * hi
                    plane = lax.rem(at_ref[1] + planes - s, planes)
                    start = pl.multiple_of(plane * n + (at_ref[0] ^ peer) * size, size)
                    for i in range(3):
                        r, c = size * (i // 2), w * (i % 2)
                        o_ref[hi, s, r : r + size, c : c + w] = turn[i, pl.ds(start, size), :].astype(bf16)
                    mine = vec[:, pl.ds(pl.multiple_of(plane * n, n), n)]
                    mine = jnp.concatenate([vector_rows(mine, at_ref[0] ^ peer, size), jnp.zeros((size, w - n), f32)], 1)
                    if sides:
                        mine = jnp.concatenate([mine[0:1], refs[0][half, hi, s, 0:2, :], mine[3:]], 0)
                    o_ref[hi, s, size:, w:] = mine.astype(bf16)


def back(at, sequence, qt, q, k, v, mt, dt, d, lt, group, planes, sides=(), after=()):
    spans, rows, width = sequence.shape
    pad = k.shape[1]
    wide = qt.shape[2]
    w = width // GROUPS
    tr = pl.BlockSpec((1, w, wide), lambda i, *_: (i, group, 0))
    nat = pl.BlockSpec((1, pad, w), lambda i, *_: (i, 0, group))
    grad = pl.BlockSpec((1, w, wide), lambda i, *_: (i, 0, 0))
    nat_grad = pl.BlockSpec((1, pad, w), lambda i, *_: (i, 0, 0))
    half = (INNER // 2, planes, 2 * width // (planes * INNER), 2 * w)
    out = pl.BlockSpec(half, lambda i, *_: (0, 0, 0, 0))
    return pl.pallas_call(
        functools.partial(back_body, rows, planes, group, len(after), len(sides)),
        grid_spec=pltpu.PrefetchScalarGridSpec(
            num_scalar_prefetch=1,
            grid=(spans,),
            in_specs=[pl.BlockSpec((1, rows, width), lambda i, *_: (i, 0, 0)), tr, nat, nat, nat, tr, tr, nat,
                      pl.BlockSpec((1, 1, HEADS // GROUPS, wide), lambda i, *_: (i, group, 0, 0))] + [whole(a) for a in sides]
            + [ANY] * len(after),
            out_specs=[grad, nat_grad, nat_grad] + [out] * 2,
            scratch_shapes=[pltpu.VMEM((w, width), f32)] * 3
            + [pltpu.VMEM((w, 8), f32), pltpu.VMEM((8, w), f32), pltpu.VMEM((pad, width), bf16), pltpu.VMEM((8, width), f32),
               pltpu.VMEM((3, width, w), f32)],
        ),
        out_shape=[shape((spans, w, wide), bf16)] + [shape((spans, pad, w), bf16)] * 2 + [shape(half, bf16)] * 2,
        compiler_params=params(),
        cost_estimate=cost(21),
        name=f"back{group}",
    )(at, sequence, qt, q, k, v, mt, dt, d, lt, *sides, *after)


def input_body(rows, groups, skip, *refs):
    refs = refs[skip:]
    gs_ref = refs[0]
    parts = refs[1 : 1 + 3 * groups]
    ws = refs[1 + 3 * groups : 4 + 3 * groups]
    out_ref = refs[4 + 3 * groups]
    wt = refs[5 + 3 * groups :]

    @pl.when(pl.program_id(0) == 0)
    def _():
        wt[0][...] = ws[0][...].T

    total = gs_ref[0]
    for g in range(groups):
        dq, dk, dv = (ref[0] for ref in parts[3 * g : 3 * g + 3])
        cols = slice(dq.shape[0] * g, dq.shape[0] * g + dq.shape[0])
        total = total + tn(dq[:, : total.shape[0]], wt[0][cols, :])
        total = total + nt(dk, ws[1][:, cols])
        total = total + nt(dv, ws[2][:, cols])
    out_ref[0] = total[:rows]


def input_grad(rows, gs, parts, wq, wk, wv, after=()):
    spans, pad, width = gs.shape
    flat = [a for part in parts for a in part]
    spec = lambda a: pl.BlockSpec((1,) + a.shape[1:], lambda i: (i, 0, 0))
    return pl.pallas_call(
        functools.partial(input_body, rows, len(parts), len(after)),
        grid=(spans,),
        in_specs=[ANY] * len(after) + [spec(gs)] + [spec(a) for a in flat] + [whole(w) for w in (wq, wk, wv)],
        out_specs=pl.BlockSpec((1, rows, width), lambda i: (i, 0, 0)),
        out_shape=shape((spans, rows, width), f32),
        scratch_shapes=[pltpu.VMEM((width, width), bf16)],
        compiler_params=params(),
        cost_estimate=cost(10),
        name="input_grad",
    )(*after, gs, *flat, wq, wk, wv)


def final_body(cut_in, cut_back, at_ref, *refs):
    pieces = refs[:INNER]
    wi_ref, wb_ref, wo_ref, wq_ref, wk_ref, wv_ref, bin_ref, *vec_refs = refs[INNER:]
    n, width = wo_ref.shape
    size = n // INNER
    w = width // GROUPS
    for q in range(INNER):
        slot = at_ref[0] ^ (q // (INNER // 2) + 2 * (q % (INNER // 2)))
        small = pl.ds(pl.multiple_of(slot * size, size), size)
        p = pieces[q]
        wi_ref[pl.ds(pl.multiple_of(slot * cut_in, cut_in), cut_in), :] = p[:cut_in, :].astype(f32)
        at = cut_in
        wb_ref[pl.ds(pl.multiple_of(slot * cut_back, cut_back), cut_back), :] = p[at : at + cut_back, :].astype(f32)
        at += cut_back
        wo_ref[small, :] = p[at : at + size, :].astype(f32)
        at += size
        tail = p[at + size : at + 2 * size, w : 2 * w].astype(f32)
        tail = jnp.concatenate([tail[1:2], tail[2:3]], 1)
        pair = jnp.zeros((1, n), f32)
        for g in range(GROUPS):
            for i, o_ref in enumerate((wq_ref, wk_ref, wv_ref)):
                r, c = at + size * (i // 2), w * (i % 2)
                o_ref[small, w * g : w * g + w] = p[r : r + size, c : c + w].astype(f32)
            pair = pair + p[at + size : at + 2 * size, w : w + n].astype(f32)[0:1]
            at += 2 * size
        for i, v_ref in enumerate(vec_refs):

            @pl.when(slot == i % 6)
            def _():
                v_ref[...] = tail[:, :n] if i < 6 else pair

        @pl.when(slot == 6)
        def _():
            bin_ref[...] = tail


def final(at, pieces, own, planes):
    width = pieces[0].shape[1]
    n = width // planes
    out = [(width, own), (own, width)] + [(n, width)] * 4 + [(1, own)] + [(1, n)] * 8
    return pl.pallas_call(
        functools.partial(final_body, width // INNER, own // INNER),
        grid_spec=pltpu.PrefetchScalarGridSpec(
            num_scalar_prefetch=1,
            grid=(1,),
            in_specs=[whole(a) for a in pieces],
            out_specs=[pl.BlockSpec(d, lambda *_: (0, 0)) for d in out],
        ),
        out_shape=[shape(d, f32) for d in out],
        compiler_params=params(),
        cost_estimate=cost(3),
        name="final",
    )(at, *pieces)


def shards(dp, planes, sequence, cotangent, w_query, b_query, w_key, w_value, b_value, w_out, b_out, gain_attn, shift_attn,
           w_in, b_in, w_back, b_back, gain_ffn, shift_ffn):
    spans, rows, width = sequence.shape
    own = w_in.shape[1]
    at = jnp.stack([lax.axis_index("dp") & (INNER - 1), lax.axis_index("mp")]).astype(jnp.int32)

    def swap(a, k):
        return lax.ppermute(a, "dp", [(i, i ^ k) for i in range(dp)])

    def turn(a, s):
        return lax.ppermute(a, "mp", [(i, (i + s) % planes) for i in range(planes)])

    def spread(a, after=()):
        far = [a] + [swap(a, 2 * k) for k in range(1, INNER // 2)]
        far = lax.optimization_barrier((*far, *after))[: INNER // 2]
        return list(far) + [swap(b, 1) for b in far]

    def from_plane(parts):
        return [parts[0]] + [swap(parts[k], 2 * k) for k in range(1, INNER // 2)]

    def outer(totals):
        totals = list(totals)
        step = INNER
        while step < dp:
            totals = [(t.astype(f32) + swap(t, step).astype(f32)).astype(bf16) for t in totals]
            step *= 2
        return totals

    def to_planes(totals):
        return [totals[0]] + [turn(totals[s], -s) for s in range(1, planes)]

    piece = prep(at, w_in, w_back, b_in)
    far = [turn(piece, s) for s in range(1, planes)]
    vec = stack_vectors((b_query, b_value, b_out, b_back, gain_attn, shift_attn, gain_ffn, shift_ffn), (piece,))
    common = (sequence, w_query, w_key, w_value, w_out, vec)
    head = 1
    first = attend(*common, 0, head)
    far, bias_far = join(far, first[:1])
    qt, k, v, mt, lt, so, q = attend(*common, head, spans - head, first, (far,))
    far = spread(far, (so,))
    layer_out, gs, d, dt, keep, send, side = ffn(at, so, cotangent, mt, vec, w_out, b_in, bias_far, w_in, w_back, far)
    *grad0, keep0, send0 = back(at, sequence, qt, q, k, v, mt, dt, d, lt, 0, planes, (side,))
    got0 = swap(send0, 1)
    ffn_parts = core_sum([(keep, swap(send, 1))], (keep0,), "core_ffn")
    *grad1, keep1, send1 = back(at, sequence, qt, q, k, v, mt, dt, d, lt, 1, planes, (), (ffn_parts[0], got0))
    ffn_parts = from_plane(ffn_parts)
    parts = core_sum([(keep0, got0), (keep1, swap(send1, 1))], ffn_parts[1:], "core_attn")
    ffn_totals = to_planes(outer(plane_sum(ffn_parts, (parts[0],), "plane_ffn")))
    by_input = input_grad(rows, gs, [grad0, grad1], w_query, w_key, w_value, (ffn_totals[0],))
    totals = to_planes(outer(plane_sum(from_plane(parts), (by_input,), "plane_attn")))
    layer_out, by_input = lax.optimization_barrier((layer_out, by_input, totals[0]))[:2]
    layer_out, by_input = (lax.optimization_barrier(jnp.transpose(a, (1, 0, 2))) for a in (layer_out, by_input))
    pieces = spread(last_sum([ffn_totals, totals], (by_input, layer_out), "last"))
    wi, wb, wo, wq, wk, wv, bins, gg2, gs2, bb, gg1, gs1, bo, bq, bv = final(at, pieces, own, planes)
    row = lambda a: a.reshape(-1)
    layer_out, by_input = (jnp.transpose(a, (1, 0, 2)) for a in (layer_out, by_input))
    return (layer_out, by_input, wq, row(bq), wk, wv, row(bv), wo, row(bo), row(gg1), row(gs1), wi, row(bins), wb,
            row(bb), row(gg2), row(gs2))


def solution(mesh):
    spans, vector = P(("dp", "mp"), None, None), P("mp")
    return jax.shard_map(
        functools.partial(shards, mesh.shape["dp"], mesh.shape["mp"]),
        mesh=mesh,
        in_specs=(spans, spans) + (P(),) * 9 + (P(None, "mp"), vector, P("mp", None)) + (P(),) * 3,
        out_specs=(spans, spans, P("mp", None), vector, P("mp", None), P("mp", None), vector, P("mp", None), vector, vector, vector,
                   P(None, "mp"), vector, P("mp", None), vector, vector, vector),
        check_vma=False,
    )
```

```python
import functools

import jax
import jax.numpy as jnp
from jax import lax
from jax.experimental import pallas as pl
from jax.experimental.pallas import tpu as pltpu
from jax.sharding import PartitionSpec as P

HEADS = 8
GROUPS = 2
INNER = 8
NEG = -1e30
C0 = (2.0 / 3.141592653589793) ** 0.5
C1 = C0 * 0.044715
LOG2E = 1.4426950408889634
f32 = jnp.float32
bf16 = jnp.bfloat16


def dot(left, right, a, b):
    return lax.dot_general(left, right, (((a,), (b,)), ((), ())), preferred_element_type=f32)


def nn(left, right):
    return dot(left, right, 1, 0)


def nt(left, right):
    return dot(left, right, 1, 1)


def tn(left, right):
    return dot(left, right, 0, 0)


def fold(v):
    return jnp.sum(v.reshape(v.shape[0] // 8, 8, v.shape[1]), 0)


def row_mean(v):
    return jnp.mean(v, -1, keepdims=True)


def lanes(n):
    return (n + 127) // 128 * 128


def cost(us):
    return pl.CostEstimate(flops=int(us * 1e9), bytes_accessed=int(us * 1e5), transcendentals=0)


def params(mib=60):
    return pltpu.CompilerParams(vmem_limit_bytes=mib * 2**20)


def whole(a):
    return pl.BlockSpec(a.shape, lambda *_: (0,) * len(a.shape), pipeline_mode=pl.Buffered(1))


ANY = pl.BlockSpec(memory_space=pl.ANY)


def shape(dims, dtype):
    return jax.ShapeDtypeStruct(tuple(dims), dtype)


def prep_body(at_ref, wi_ref, wb_ref, bi_ref, piece_ref):
    a, b = wi_ref.shape[0], wb_ref.shape[0]
    piece_ref[:a, :] = wi_ref[...]
    piece_ref[a : a + b, :] = wb_ref[...]
    bias = bi_ref[...].astype(f32).reshape(1, -1)
    piece_ref[a + b :, :] = jnp.concatenate([bias, jnp.zeros((15, bias.shape[1]), f32)], 0).astype(bf16)


def prep(at, wi, wb, bi):
    width, own = wi.shape
    a, b = width // INNER, own // INNER
    return pl.pallas_call(
        prep_body,
        grid_spec=pltpu.PrefetchScalarGridSpec(
            num_scalar_prefetch=1,
            grid=(1,),
            in_specs=[pl.BlockSpec((a, own), lambda i, at: (at[0], 0)), pl.BlockSpec((b, width), lambda i, at: (at[0], 0)), whole(bi)],
            out_specs=pl.BlockSpec((a + b + 16, width), lambda *_: (0, 0)),
        ),
        out_shape=shape((a + b + 16, width), bf16),
        compiler_params=params(),
        cost_estimate=cost(2),
        name="prep",
    )(at, wi, wb, bi)


def vectors_body(*refs):
    for j, v in enumerate(refs[:8]):
        refs[-1][j : j + 1, :] = v[...].astype(f32).reshape(1, -1)


def stack_vectors(vectors, after):
    return pl.pallas_call(
        vectors_body,
        in_specs=[pl.BlockSpec(memory_space=pltpu.VMEM)] * 8 + [ANY] * len(after),
        out_specs=pl.BlockSpec(memory_space=pltpu.VMEM),
        out_shape=shape((8, vectors[0].shape[0]), f32),
        cost_estimate=cost(1),
        name="vectors",
    )(*vectors, *after)


def attend_body(rows, pad, skip, x_ref, wq_ref, wk_ref, wv_ref, wo_ref, vec_ref, *refs):
    qt_ref, k_ref, v_ref, mt_ref, lt_ref, so_ref, q_ref, xp, vt = refs[skip:]
    width = x_ref.shape[-1]
    hs = width // HEADS
    main = rows // 128 * 128
    left = pad - main
    group = 128 // left
    top = rows // 16 * 16

    @pl.when(pl.program_id(0) == 0)
    def _():
        xp[top:, :] = jnp.zeros((pad - top, width), bf16)

    xp[:rows, :] = x_ref[0]
    x = xp[...]
    scale = hs**-0.5
    q = ((nn(x, wq_ref[...]) + vec_ref[0:1, :]) * (scale * LOG2E)).astype(bf16)
    q_ref[0] = q
    qt_ref[0, :, :pad] = q.T
    k_ref[0] = nn(x, wk_ref[...]).astype(bf16)
    v = (nn(x, wv_ref[...]) + vec_ref[1:2, :]).astype(bf16)
    v_ref[0] = v
    vt[...] = v.T
    valid = lax.broadcasted_iota(jnp.int32, (pad - top, 1), 0) < rows - top
    ones = jnp.ones((16, pad), bf16)

    def soft(st):
        s_top = st[:top]
        s_bot = jnp.where(valid, st[top:], NEG)
        m = jnp.maximum(jnp.max(s_top, 0, keepdims=True), jnp.max(s_bot, 0, keepdims=True))
        p = jnp.concatenate([jnp.exp2(s_top - m).astype(bf16), jnp.exp2(s_bot - m).astype(bf16)], 0)
        return m, p

    cs = [slice(hs * h, hs * h + hs) for h in range(HEADS)]
    following = nn(k_ref[0, :, cs[0]], qt_ref[0, cs[0], :main])
    for h in range(HEADS):
        c = cs[h]
        st = following
        if h + 1 < HEADS:
            following = nn(k_ref[0, :, cs[h + 1]], qt_ref[0, cs[h + 1], :main])
        m, p = soft(st)
        ot = nn(jnp.concatenate([vt[c, :], ones], 0), p)
        total = ot[hs : hs + 1]
        mt_ref[0, c, :main] = (ot[:hs] * (1.0 / total)).astype(bf16)
        lt_ref[0, h // (HEADS // GROUPS), h % (HEADS // GROUPS) : h % (HEADS // GROUPS) + 1, :main] = m + jnp.log2(total)
    for g in range(HEADS // group):
        w = hs * group
        c = slice(w * g, w * g + w)
        same = (lax.broadcasted_iota(jnp.int32, (w, 128), 0) // hs
                == lax.broadcasted_iota(jnp.int32, (w, 128), 1) // left)
        ql = jnp.where(same, jnp.concatenate([qt_ref[0, c, main:pad]] * group, 1), 0).astype(bf16)
        m, p = soft(nn(k_ref[0, :, c], ql))
        ot = nn(jnp.concatenate([vt[c, :], ones], 0), p)
        total = ot[w : w + 1]
        o = ot[:w] * (1.0 / total)
        lt = m + jnp.log2(total)
        for j in range(group):
            h = g * group + j
            mt_ref[0, hs * h : hs * h + hs, main:pad] = o[hs * j : hs * j + hs, left * j : left * j + left].astype(bf16)
            lt_ref[0, h // (HEADS // GROUPS), h % (HEADS // GROUPS) : h % (HEADS // GROUPS) + 1, main:pad] = lt[:, left * j : left * j + left]
    so_ref[0] = tn(mt_ref[0, :, :pad], wo_ref[...]) + vec_ref[2:3, :] + xp[...].astype(f32)


def attend(sequence, wq, wk, wv, wo, vec, first, count, before=(), after=()):
    spans, rows, width = sequence.shape
    pad = (rows + 31) // 32 * 32
    wide = lanes(pad)
    per = HEADS // GROUPS
    spec = lambda a, b: pl.BlockSpec((1, a, b), lambda i: (i + first, 0, 0))
    return pl.pallas_call(
        functools.partial(attend_body, rows, pad, len(before) + len(after)),
        grid=(count,),
        in_specs=[spec(rows, width)] + [whole(w) for w in (wq, wk, wv, wo, vec)] + [ANY] * (len(before) + len(after)),
        out_specs=[spec(width, wide), spec(pad, width), spec(pad, width), spec(width, wide),
                   pl.BlockSpec((1, GROUPS, per, wide), lambda i: (i + first, 0, 0, 0)), spec(pad, width), spec(pad, width)],
        out_shape=[shape((spans, width, wide), bf16), shape((spans, pad, width), bf16), shape((spans, pad, width), bf16),
                   shape((spans, width, wide), bf16), shape((spans, GROUPS, per, wide), f32), shape((spans, pad, width), f32),
                   shape((spans, pad, width), bf16)],
        scratch_shapes=[pltpu.VMEM((pad, width), bf16), pltpu.VMEM((width, pad), bf16)],
        input_output_aliases={6 + n: n for n in range(len(before))},
        compiler_params=params(),
        cost_estimate=cost(16),
        name=f"attend{first}",
    )(sequence, wq, wk, wv, wo, vec, *before, *after)


def vector_rows(vec, slot, count):
    mine = lax.broadcasted_iota(jnp.int32, vec.shape, 0) == slot
    row = jnp.sum(jnp.where(mine, vec, 0.0), 0, keepdims=True)
    return jnp.concatenate([row, jnp.zeros((count - 1, vec.shape[1]), f32)], 0)


def ffn_body(rows, slices, planes, at_ref, so_ref, ct_ref, mt_ref, vec_ref, wo_ref, bi_ref, bf_ref, wi_ref, wb_ref, *refs):
    (lo_ref, gs_ref, d_ref, dot_ref, o0_ref, o1_ref, side_ref,
     col, binv, wi, wb, one, two, inv1, act, pre_grad, low, grad, acc, turn, low_grad, sem) = refs[slices:]
    pad, width = so_ref.shape[1:]
    own = wb_ref.shape[0]
    hidden = wb.shape[0]
    cut_in, cut_back = width // INNER, own // INNER
    step = pl.program_id(0)

    def slot_of(half, hi):
        return at_ref[0] ^ (half + 2 * hi)

    def loads():
        copies = [pltpu.make_async_copy(wi_ref, wi.at[:, :own], sem.at[0]),
                  pltpu.make_async_copy(wb_ref, wb.at[:own, :], sem.at[1])]
        for q in range(slices):
            slot = slot_of(q // (INNER // 2), q % (INNER // 2))
            for s in range(1, planes):
                n = 2 + 2 * (q * (planes - 1) + s - 1)
                there = wi.at[pl.ds(pl.multiple_of(slot * cut_in, cut_in), cut_in), own * s : own * s + own]
                copies.append(pltpu.make_async_copy(refs[q].at[s - 1, :cut_in, :], there, sem.at[n]))
                there = wb.at[pl.ds(pl.multiple_of(own * s + slot * cut_back, cut_back), cut_back), :]
                copies.append(pltpu.make_async_copy(refs[q].at[s - 1, cut_in : cut_in + cut_back, :], there, sem.at[n + 1]))
        return copies

    @pl.when(step == 0)
    def _():
        for c in loads():
            c.start()
        col[...] = jnp.zeros_like(col)
        binv[...] = jnp.zeros_like(binv)
        acc[...] = jnp.zeros_like(acc)

    bb, g1, s1, g2, s2 = (vec_ref[n : n + 1, :] for n in range(3, 8))
    base = pl.multiple_of(step * pad, pad)
    unit = own
    chunks = [slice(n, n + unit) for n in range(0, hidden, unit)]
    bias = [bi_ref[...].astype(f32).reshape(1, -1)] + [bf_ref[s : s + 1, :] for s in range(planes - 1)]
    zero = [jnp.zeros((8, width), f32)] * 3

    def chain(first, size, tall):
        here = pl.ds(pl.multiple_of(base + first, 16), size)
        blocks = [slice(first + n, first + n + tall) for n in range(0, size, tall)]
        local = lambda b: slice(b.start - first, b.stop - first)
        there = lambda b: pl.ds(pl.multiple_of(base + b.start, 16), tall)

        def norm():
            for b in blocks:
                r = so_ref[0, b, :]
                c = r - row_mean(r)
                inv = lax.rsqrt(row_mean(c * c) + 1e-5)
                unit1 = c * inv
                one[b, :] = unit1
                inv1[b, :] = jnp.broadcast_to(inv, (tall, 128))
                low[there(b), :] = (unit1 * g1 + s1).astype(bf16)

        def hidden_units():
            nl = low[here, :]
            for cs, add_bias in zip(chunks, bias):
                pre = nn(nl, wi[:, cs])
                for b in blocks:
                    v = (pre[local(b)] + add_bias).astype(bf16)
                    cube = (v * v) * bf16(C1)
                    t = jnp.tanh(v * (cube + bf16(C0)))
                    double = v * (bf16(1.0) + t)
                    act[there(b), cs] = double
                    slope = cube * bf16(3.0) + bf16(C0)
                    pre_grad[there(b), cs] = (bf16(1.0) + t) + double * ((bf16(1.0) - t) * slope)

        def output():
            out = nn(act[here, :], wb[...])
            sums = zero
            for b in blocks:
                r = out[local(b)] + (one[b, :] * g1 + (s1 + bb))
                c = r - row_mean(r)
                inv = lax.rsqrt(row_mean(c * c) + 1e-5)
                unit2 = c * inv
                last = min(b.stop, rows)
                lo_ref[0, b.start : last, :] = (unit2 * g2 + s2)[: last - b.start].astype(bf16)
                up = ct_ref[0, b.start : last, :].astype(f32)
                if last < b.stop:
                    up = jnp.concatenate([up, jnp.zeros((b.stop - last, width), f32)], 0)
                gu = up * g2
                back = inv * (gu - row_mean(gu) - unit2 * row_mean(gu * unit2))
                two[b, :] = back
                grad[there(b), :] = back.astype(bf16)
                sums = [a + fold(v) for a, v in zip(sums, (up * unit2, up, back))]
            for n in range(3):
                col[n] += sums[n]

        def hidden_grads():
            f = grad[here, :]
            for cs in chunks:
                da = nt(f, wb[cs, :])
                total = jnp.zeros((8, unit), f32)
                for b in blocks:
                    g = da[local(b)] * pre_grad[there(b), cs].astype(f32)
                    total = total + fold(g)
                    pre_grad[there(b), cs] = g.astype(bf16)
                binv[:, cs] += total

        def input_grads():
            out = nt(pre_grad[here, :], wi[...])
            sums = zero
            for b in blocks:
                dn = out[local(b)] + two[b, :]
                unit1 = one[b, :]
                gu = dn * g1
                back = inv1[b, 0:1] * (gu - row_mean(gu) - unit1 * row_mean(gu * unit1))
                gs_ref[0, b, :] = back
                low_grad[b, :] = back.astype(bf16)
                sums = [a + fold(v) for a, v in zip(sums, (dn * unit1, dn, back))]
            for n in range(3):
                col[3 + n] += sums[n]

        return norm, hidden_units, output, hidden_grads, input_grads

    parts, tall = 2, 16
    size = pad // parts
    plan = [[(0, 0), (1, 0)], [(0, 1), (1, 1), (0, 2), (1, 2), (0, 3), (1, 3), (0, 4), (1, 4)]]
    sections = [chain(n * size, size, tall) for n in range(parts)]
    for at, group in enumerate(plan):

        @pl.when(step >= 0)
        def _():
            for p, n in group:
                sections[p][n]()

        if at == 0:

            @pl.when(step == 0)
            def _():
                for c in loads():
                    c.wait()
                wb[...] = wb[...] * bf16(0.5)

    ga = low_grad[...]
    d = nt(ga, wo_ref[...]).astype(bf16)
    d_ref[0] = d
    dot_ref[0, :, :pad] = d.T
    acc[...] += nn(mt_ref[0, :, :pad], ga)

    @pl.when(step == pl.num_programs(0) - 1)
    def _():
        n = width // planes
        size = n // INNER
        outs = (o0_ref, o1_ref)
        peers = [(half, hi) for half in range(2) for hi in range(INNER // 2)]
        for m, (at, cut) in enumerate(((0, cut_in), (cut_in, cut_back))):
            for s, cs in enumerate(chunks):
                piece = tn(low[...], pre_grad[:, cs]) if m == 0 else tn(act[:, cs], grad[...])
                turn[m] = piece.astype(bf16) if m == 0 else (0.5 * piece).astype(bf16)
                for half, hi in peers:
                    start = pl.multiple_of(slot_of(half, hi) * cut, cut)
                    outs[half][hi, s, at : at + cut, :] = turn[m, pl.ds(start, cut), :]
        at = cut_in + cut_back
        totals = jnp.sum(col[...], 1)
        bins = jnp.sum(binv[...], 0, keepdims=True)
        for s, cs in enumerate(chunks):
            plane = lax.rem(at_ref[1] + planes - s, planes)
            mine = jnp.zeros((8, n), f32)
            for p in range(planes):
                mine = jnp.where(plane == p, totals[:, n * p : n * p + n], mine)
            mine = jnp.concatenate([mine, jnp.zeros((8, width - n), f32)], 1)
            mine = jnp.where(lax.broadcasted_iota(jnp.int32, mine.shape, 0) == 6, bins[:, cs], mine)
            for half, hi in peers:
                slot = slot_of(half, hi)
                start = pl.multiple_of(plane * n + slot * size, size)
                outs[half][hi, s, at : at + size, :] = acc[pl.ds(start, size), :].astype(bf16)
                row = vector_rows(mine, slot, 8)
                w = width // 2
                side_ref[half, hi, s] = jnp.concatenate([row[0:1, :w], row[0:1, w:], jnp.zeros((6, w), f32)], 0)


def ffn(at, so, cotangent, mt, vec, wo, bi, bias_far, wi, wb, far):
    spans, pad, width = so.shape
    rows = cotangent.shape[1]
    own = wb.shape[0]
    planes = far[0].shape[0] + 1
    hidden = own * planes
    spec = lambda a, b: pl.BlockSpec((1, a, b), lambda i, *_: (i, 0, 0))
    st = lambda a, b, t: shape((spans, a, b), t)
    half = (INNER // 2, planes, (width + own) // INNER + width // (planes * INNER), width)
    side = (2, INNER // 2, planes, 8, width // 2)
    out = pl.BlockSpec(half, lambda i, *_: (0, 0, 0, 0), pipeline_mode=pl.Buffered(1))
    total = spans * pad
    vmem = pltpu.VMEM
    return pl.pallas_call(
        functools.partial(ffn_body, rows, len(far), planes),
        grid_spec=pltpu.PrefetchScalarGridSpec(
            num_scalar_prefetch=1,
            grid=(spans,),
            in_specs=[spec(pad, width), spec(rows, width), spec(width, lanes(pad))] + [whole(w) for w in (vec, wo, bi, bias_far)]
            + [ANY] * (2 + len(far)),
            out_specs=[spec(rows, width), spec(pad, width), spec(pad, width), spec(width, lanes(pad)), out, out,
                       pl.BlockSpec(side, lambda i, *_: (0,) * 5)],
            scratch_shapes=[vmem((8, 8, width), f32), vmem((8, hidden), f32), vmem((width, hidden), bf16), vmem((hidden, width), bf16),
                            vmem((pad, width), f32), vmem((pad, width), f32), vmem((pad, 128), f32),
                            vmem((total, hidden), bf16), vmem((total, hidden), bf16), vmem((total, width), bf16),
                            vmem((total, width), bf16), vmem((width, width), f32), vmem((2, width, width), bf16),
                            vmem((pad, width), bf16),
                            pltpu.SemaphoreType.DMA((2 + 2 * len(far) * (planes - 1),))],
        ),
        out_shape=[st(rows, width, bf16), st(pad, width, f32), st(pad, width, bf16), st(width, lanes(pad), bf16)] + [shape(half, bf16)] * 2
        + [shape(side, f32)],
        compiler_params=params(62),
        cost_estimate=cost(46),
        name="ffn",
    )(at, so, cotangent, mt, vec, wo, bi, bias_far, wi, wb, *far)


def join_body(count, *refs):
    o_ref, b_ref = refs[-2:]
    rows = o_ref.shape[1]
    for i in range(count):
        o_ref[i] = refs[i][:rows, :]
        b_ref[i : i + 1, :] = refs[i][rows:, :].astype(f32)[0:1]


def join(parts, after):
    rows, width = parts[0].shape
    return pl.pallas_call(
        functools.partial(join_body, len(parts)),
        in_specs=[pl.BlockSpec(memory_space=pltpu.VMEM)] * len(parts) + [ANY] * len(after),
        out_specs=[pl.BlockSpec(memory_space=pltpu.VMEM)] * 2,
        out_shape=[shape((len(parts), rows - 16, width), bf16), shape((len(parts), width), f32)],
        compiler_params=params(),
        cost_estimate=cost(1),
        name="join",
    )(*parts, *after)


def add(*refs):
    total = refs[0][...].astype(f32)
    for ref in refs[1:]:
        total = total + ref[...].astype(f32)
    return total.astype(bf16)


def core_sum_body(pairs, skip, *refs):
    outs = refs[2 * pairs + skip :]
    for p, o_ref in enumerate(outs):
        o_ref[...] = jnp.concatenate([add(refs[2 * i].at[p], refs[2 * i + 1].at[p]) for i in range(pairs)], 1)


def core_sum(pairs, after, name):
    peers, planes, _, width = pairs[0][0].shape
    rows = sum(a.shape[2] for a, _ in pairs)
    flat = [a for pair in pairs for a in pair]
    return pl.pallas_call(
        functools.partial(core_sum_body, len(pairs), len(after)),
        grid=(planes,),
        in_specs=[pl.BlockSpec((peers, 1) + a.shape[2:], lambda i: (0, i, 0, 0)) for a in flat] + [ANY] * len(after),
        out_specs=[pl.BlockSpec((1, rows, width), lambda i: (i, 0, 0))] * peers,
        out_shape=[shape((planes, rows, width), bf16)] * peers,
        compiler_params=params(),
        cost_estimate=cost(0.001),
        name=name,
    )(*flat, *after)


def plane_sum_body(count, skip, *refs):
    outs = refs[count + skip :]
    for s, o_ref in enumerate(outs):
        o_ref[...] = add(*(ref.at[s] for ref in refs[:count]))


def plane_sum(parts, after, name):
    planes, rows, width = parts[0].shape
    return pl.pallas_call(
        functools.partial(plane_sum_body, len(parts), len(after)),
        in_specs=[pl.BlockSpec(memory_space=pltpu.VMEM)] * len(parts) + [ANY] * len(after),
        out_specs=[pl.BlockSpec(memory_space=pltpu.VMEM)] * planes,
        out_shape=[shape((rows, width), bf16)] * planes,
        compiler_params=params(),
        cost_estimate=cost(0.001),
        name=name,
    )(*parts, *after)


def last_sum_body(count, groups, skip, *refs):
    o_ref = refs[count * groups + skip]
    at = 0
    for g in range(groups):
        total = add(*refs[count * g : count * g + count])
        o_ref[at : at + total.shape[0], :] = total
        at += total.shape[0]


def last_sum(groups, after, name):
    flat = [a for group in groups for a in group]
    rows = sum(group[0].shape[0] for group in groups)
    return pl.pallas_call(
        functools.partial(last_sum_body, len(groups[0]), len(groups), len(after)),
        in_specs=[pl.BlockSpec(memory_space=pltpu.VMEM)] * len(flat) + [ANY] * len(after),
        out_specs=pl.BlockSpec(memory_space=pltpu.VMEM),
        out_shape=shape((rows, flat[0].shape[1]), bf16),
        compiler_params=params(),
        cost_estimate=cost(0.001),
        name=name,
    )(*flat, *after)


def back_body(rows, planes, group, skip, sides, at_ref, x_ref, qt_ref, q_ref, k_ref, v_ref, mt_ref, dt_ref, d_ref, lt_ref, *refs):
    dq_ref, dk_ref, dv_ref, o0_ref, o1_ref, aq, ak, av, ab, row, xp, vec, turn = refs[sides + skip :]
    w, pad = k_ref.shape[2], k_ref.shape[1]
    width = x_ref.shape[-1]
    hs = width // HEADS
    scale = hs**-0.5
    main = rows // 128 * 128
    left = pad - main
    heads = w // hs
    top = rows // 16 * 16
    step = pl.program_id(0)

    @pl.when(step == 0)
    def _():
        for a in (aq, ak, av, ab, row):
            a[...] = jnp.zeros_like(a)
        xp[top:, :] = jnp.zeros((pad - top, width), bf16)

    xp[:rows, :] = x_ref[0]
    k = k_ref[0]
    kt = k.T
    v = v_ref[0]
    valid = lax.broadcasted_iota(jnp.int32, (pad - top, 1), 0) < rows - top

    def core(ks, qs, vs, ds, ls, ms):
        delta = jnp.sum(ds.astype(f32) * ms.astype(f32), 0, keepdims=True)
        st = nn(ks, qs)
        st = jnp.concatenate([st[:top], jnp.where(valid, st[top:], NEG)], 0)
        p = jnp.exp2(st - ls)
        gsc = (p * (nn(vs, ds) - delta)).astype(bf16)
        return p.astype(bf16), gsc

    def own_block(shape, rows_per, lanes_per):
        return (lax.broadcasted_iota(jnp.int32, shape, 0) // rows_per
                == lax.broadcasted_iota(jnp.int32, shape, 1) // lanes_per)

    flat = own_block((w, 128), hs, left)
    tall = own_block((128, w), left, hs)
    tile = lambda a: jnp.where(flat, jnp.concatenate([a] * heads, 1), 0).astype(bf16)
    pile = lambda a: jnp.where(tall, jnp.concatenate([a] * heads, 0), 0).astype(bf16)
    ql, dl, ml = (tile(ref[0, :, main:pad]) for ref in (qt_ref, dt_ref, mt_ref))
    ll = jnp.concatenate([lt_ref[0, 0, h : h + 1, main:pad] for h in range(heads)], 1)
    p, gsc = core(k, ql, v, dl, ll, ml)
    dv_left = nn(p, pile(d_ref[0, main:pad, :]))
    dk_left = nn(gsc, pile(q_ref[0, main:pad, :]))
    dq_left = nn(kt, gsc)
    even = lax.broadcasted_iota(jnp.int32, (pad, 2 * hs), 1) < hs
    for pair in range(heads // 2):
        both = slice(2 * hs * pair, 2 * hs * pair + 2 * hs)
        q, d = q_ref[0, :main, both], d_ref[0, :main, both]
        dk, dv = [], []
        for h in (2 * pair, 2 * pair + 1):
            c = slice(hs * h, hs * h + hs)
            p, gsc = core(k[:, c], qt_ref[0, c, :main], v[:, c], dt_ref[0, c, :main], lt_ref[0, 0, h : h + 1, :main], mt_ref[0, c, :main])
            dv.append(nn(p, d))
            dk.append(nn(gsc, q))
            dq_ref[0, c, :main] = (nn(kt[c], gsc) * scale).astype(bf16)
            dq_ref[0, c, main:pad] = (dq_left[c, left * h : left * h + left] * scale).astype(bf16)
        dv = jnp.where(even, *dv) + dv_left[:, both]
        row[:, both] += fold(dv)
        dv_ref[0, :, both] = dv.astype(bf16)
        dk_ref[0, :, both] = ((jnp.where(even, *dk) + dk_left[:, both]) * (1.0 / LOG2E)).astype(bf16)
    x = xp[...]
    aq[...] += nn(dq_ref[0, :, :pad], x)
    ak[...] += tn(dk_ref[0], x)
    av[...] += tn(dv_ref[0], x)
    ab[:, 0:1] += jnp.sum(dq_ref[0, :, :pad].astype(f32), 1, keepdims=True)

    @pl.when(step == pl.num_programs(0) - 1)
    def _():
        size = width // (planes * INNER)
        n = width // planes
        vec[...] = jnp.zeros_like(vec)
        vec[0:1, group * w : group * w + w] = ab[...].T[0:1]
        vec[1:2, group * w : group * w + w] = jnp.sum(row[...], 0, keepdims=True)
        for i, a in enumerate((aq, ak, av)):
            turn[i] = a[...].T
        for half, o_ref in enumerate((o0_ref, o1_ref)):
            for hi in range(INNER // 2):
                for s in range(planes):
                    peer = half + 2 * hi
                    plane = lax.rem(at_ref[1] + planes - s, planes)
                    start = pl.multiple_of(plane * n + (at_ref[0] ^ peer) * size, size)
                    for i in range(3):
                        r, c = size * (i // 2), w * (i % 2)
                        o_ref[hi, s, r : r + size, c : c + w] = turn[i, pl.ds(start, size), :].astype(bf16)
                    mine = vec[:, pl.ds(pl.multiple_of(plane * n, n), n)]
                    mine = jnp.concatenate([vector_rows(mine, at_ref[0] ^ peer, size), jnp.zeros((size, w - n), f32)], 1)
                    if sides:
                        mine = jnp.concatenate([mine[0:1], refs[0][half, hi, s, 0:2, :], mine[3:]], 0)
                    o_ref[hi, s, size:, w:] = mine.astype(bf16)


def back(at, sequence, qt, q, k, v, mt, dt, d, lt, group, planes, sides=(), after=()):
    spans, rows, width = sequence.shape
    pad = k.shape[1]
    wide = qt.shape[2]
    w = width // GROUPS
    tr = pl.BlockSpec((1, w, wide), lambda i, *_: (i, group, 0))
    nat = pl.BlockSpec((1, pad, w), lambda i, *_: (i, 0, group))
    grad = pl.BlockSpec((1, w, wide), lambda i, *_: (i, 0, 0))
    nat_grad = pl.BlockSpec((1, pad, w), lambda i, *_: (i, 0, 0))
    half = (INNER // 2, planes, 2 * width // (planes * INNER), 2 * w)
    out = pl.BlockSpec(half, lambda i, *_: (0, 0, 0, 0))
    return pl.pallas_call(
        functools.partial(back_body, rows, planes, group, len(after), len(sides)),
        grid_spec=pltpu.PrefetchScalarGridSpec(
            num_scalar_prefetch=1,
            grid=(spans,),
            in_specs=[pl.BlockSpec((1, rows, width), lambda i, *_: (i, 0, 0)), tr, nat, nat, nat, tr, tr, nat,
                      pl.BlockSpec((1, 1, HEADS // GROUPS, wide), lambda i, *_: (i, group, 0, 0))] + [whole(a) for a in sides]
            + [ANY] * len(after),
            out_specs=[grad, nat_grad, nat_grad] + [out] * 2,
            scratch_shapes=[pltpu.VMEM((w, width), f32)] * 3
            + [pltpu.VMEM((w, 8), f32), pltpu.VMEM((8, w), f32), pltpu.VMEM((pad, width), bf16), pltpu.VMEM((8, width), f32),
               pltpu.VMEM((3, width, w), f32)],
        ),
        out_shape=[shape((spans, w, wide), bf16)] + [shape((spans, pad, w), bf16)] * 2 + [shape(half, bf16)] * 2,
        compiler_params=params(),
        cost_estimate=cost(21),
        name=f"back{group}",
    )(at, sequence, qt, q, k, v, mt, dt, d, lt, *sides, *after)


def input_body(rows, groups, skip, *refs):
    refs = refs[skip:]
    gs_ref = refs[0]
    parts = refs[1 : 1 + 3 * groups]
    ws = refs[1 + 3 * groups : 4 + 3 * groups]
    out_ref = refs[4 + 3 * groups]
    wt = refs[5 + 3 * groups :]

    @pl.when(pl.program_id(0) == 0)
    def _():
        wt[0][...] = ws[0][...].T

    total = gs_ref[0]
    for g in range(groups):
        dq, dk, dv = (ref[0] for ref in parts[3 * g : 3 * g + 3])
        cols = slice(dq.shape[0] * g, dq.shape[0] * g + dq.shape[0])
        total = total + tn(dq[:, : total.shape[0]], wt[0][cols, :])
        total = total + nt(dk, ws[1][:, cols])
        total = total + nt(dv, ws[2][:, cols])
    out_ref[0] = total[:rows]


def input_grad(rows, gs, parts, wq, wk, wv, after=()):
    spans, pad, width = gs.shape
    flat = [a for part in parts for a in part]
    spec = lambda a: pl.BlockSpec((1,) + a.shape[1:], lambda i: (i, 0, 0))
    return pl.pallas_call(
        functools.partial(input_body, rows, len(parts), len(after)),
        grid=(spans,),
        in_specs=[ANY] * len(after) + [spec(gs)] + [spec(a) for a in flat] + [whole(w) for w in (wq, wk, wv)],
        out_specs=pl.BlockSpec((1, rows, width), lambda i: (i, 0, 0)),
        out_shape=shape((spans, rows, width), f32),
        scratch_shapes=[pltpu.VMEM((width, width), bf16)],
        compiler_params=params(),
        cost_estimate=cost(10),
        name="input_grad",
    )(*after, gs, *flat, wq, wk, wv)


def final_body(cut_in, cut_back, at_ref, *refs):
    pieces = refs[:INNER]
    wi_ref, wb_ref, wo_ref, wq_ref, wk_ref, wv_ref, bin_ref, *vec_refs = refs[INNER:]
    n, width = wo_ref.shape
    size = n // INNER
    w = width // GROUPS
    for q in range(INNER):
        slot = at_ref[0] ^ (q // (INNER // 2) + 2 * (q % (INNER // 2)))
        small = pl.ds(pl.multiple_of(slot * size, size), size)
        p = pieces[q]
        wi_ref[pl.ds(pl.multiple_of(slot * cut_in, cut_in), cut_in), :] = p[:cut_in, :].astype(f32)
        at = cut_in
        wb_ref[pl.ds(pl.multiple_of(slot * cut_back, cut_back), cut_back), :] = p[at : at + cut_back, :].astype(f32)
        at += cut_back
        wo_ref[small, :] = p[at : at + size, :].astype(f32)
        at += size
        tail = p[at + size : at + 2 * size, w : 2 * w].astype(f32)
        tail = jnp.concatenate([tail[1:2], tail[2:3]], 1)
        pair = jnp.zeros((1, n), f32)
        for g in range(GROUPS):
            for i, o_ref in enumerate((wq_ref, wk_ref, wv_ref)):
                r, c = at + size * (i // 2), w * (i % 2)
                o_ref[small, w * g : w * g + w] = p[r : r + size, c : c + w].astype(f32)
            pair = pair + p[at + size : at + 2 * size, w : w + n].astype(f32)[0:1]
            at += 2 * size
        for i, v_ref in enumerate(vec_refs):

            @pl.when(slot == i % 6)
            def _():
                v_ref[...] = tail[:, :n] if i < 6 else pair

        @pl.when(slot == 6)
        def _():
            bin_ref[...] = tail


def final(at, pieces, own, planes):
    width = pieces[0].shape[1]
    n = width // planes
    out = [(width, own), (own, width)] + [(n, width)] * 4 + [(1, own)] + [(1, n)] * 8
    return pl.pallas_call(
        functools.partial(final_body, width // INNER, own // INNER),
        grid_spec=pltpu.PrefetchScalarGridSpec(
            num_scalar_prefetch=1,
            grid=(1,),
            in_specs=[whole(a) for a in pieces],
            out_specs=[pl.BlockSpec(d, lambda *_: (0, 0)) for d in out],
        ),
        out_shape=[shape(d, f32) for d in out],
        compiler_params=params(),
        cost_estimate=cost(3),
        name="final",
    )(at, *pieces)


def shards(dp, planes, sequence, cotangent, w_query, b_query, w_key, w_value, b_value, w_out, b_out, gain_attn, shift_attn,
           w_in, b_in, w_back, b_back, gain_ffn, shift_ffn):
    spans, rows, width = sequence.shape
    own = w_in.shape[1]
    at = jnp.stack([lax.axis_index("dp") & (INNER - 1), lax.axis_index("mp")]).astype(jnp.int32)

    def swap(a, k):
        return lax.ppermute(a, "dp", [(i, i ^ k) for i in range(dp)])

    def turn(a, s):
        return lax.ppermute(a, "mp", [(i, (i + s) % planes) for i in range(planes)])

    def spread(a, after=()):
        far = [a] + [swap(a, 2 * k) for k in range(1, INNER // 2)]
        far = lax.optimization_barrier((*far, *after))[: INNER // 2]
        return list(far) + [swap(b, 1) for b in far]

    def from_plane(parts):
        return [parts[0]] + [swap(parts[k], 2 * k) for k in range(1, INNER // 2)]

    def outer(totals):
        totals = list(totals)
        step = INNER
        while step < dp:
            totals = [(t.astype(f32) + swap(t, step).astype(f32)).astype(bf16) for t in totals]
            step *= 2
        return totals

    def to_planes(totals):
        return [totals[0]] + [turn(totals[s], -s) for s in range(1, planes)]

    piece = prep(at, w_in, w_back, b_in)
    far = [turn(piece, s) for s in range(1, planes)]
    vec = stack_vectors((b_query, b_value, b_out, b_back, gain_attn, shift_attn, gain_ffn, shift_ffn), (piece,))
    common = (sequence, w_query, w_key, w_value, w_out, vec)
    head = 1
    first = attend(*common, 0, head)
    far, bias_far = join(far, first[:1])
    qt, k, v, mt, lt, so, q = attend(*common, head, spans - head, first, (far,))
    far = spread(far, (so,))
    layer_out, gs, d, dt, keep, send, side = ffn(at, so, cotangent, mt, vec, w_out, b_in, bias_far, w_in, w_back, far)
    *grad0, keep0, send0 = back(at, sequence, qt, q, k, v, mt, dt, d, lt, 0, planes, (side,))
    got0 = swap(send0, 1)
    ffn_parts = core_sum([(keep, swap(send, 1))], (keep0,), "core_ffn")
    *grad1, keep1, send1 = back(at, sequence, qt, q, k, v, mt, dt, d, lt, 1, planes, (), (ffn_parts[0], got0))
    ffn_parts = from_plane(ffn_parts)
    layer_out = lax.optimization_barrier((layer_out, keep1))[0]
    layer_out = lax.optimization_barrier(jnp.transpose(layer_out, (1, 0, 2)))
    parts = core_sum([(keep0, got0), (keep1, swap(send1, 1))], (*ffn_parts[1:], layer_out), "core_attn")
    ffn_totals = to_planes(outer(plane_sum(ffn_parts, (parts[0],), "plane_ffn")))
    by_input = input_grad(rows, gs, [grad0, grad1], w_query, w_key, w_value, (ffn_totals[0],))
    totals = to_planes(outer(plane_sum(from_plane(parts), (by_input,), "plane_attn")))
    by_input = lax.optimization_barrier((by_input, totals[0]))[0]
    by_input = lax.optimization_barrier(jnp.transpose(by_input, (1, 0, 2)))
    pieces = spread(last_sum([ffn_totals, totals], (by_input,), "last"))
    wi, wb, wo, wq, wk, wv, bins, gg2, gs2, bb, gg1, gs1, bo, bq, bv = final(at, pieces, own, planes)
    row = lambda a: a.reshape(-1)
    layer_out, by_input = (jnp.transpose(a, (1, 0, 2)) for a in (layer_out, by_input))
    return (layer_out, by_input, wq, row(bq), wk, wv, row(bv), wo, row(bo), row(gg1), row(gs1), wi, row(bins), wb,
            row(bb), row(gg2), row(gs2))


def solution(mesh):
    spans, vector = P(("dp", "mp"), None, None), P("mp")
    return jax.shard_map(
        functools.partial(shards, mesh.shape["dp"], mesh.shape["mp"]),
        mesh=mesh,
        in_specs=(spans, spans) + (P(),) * 9 + (P(None, "mp"), vector, P("mp", None)) + (P(),) * 3,
        out_specs=(spans, spans, P("mp", None), vector, P("mp", None), P("mp", None), vector, P("mp", None), vector, vector, vector,
                   P(None, "mp"), vector, P("mp", None), vector, vector, vector),
        check_vma=False,
    )
```
